32 devices in a mesh: blk: 4 (over y, x), dp: 8 (over z, core).
Axes of the slice: x: 2, y: 2, z: 4, core: 2. Of those that a mesh axis runs over, the one named last changes fastest.
Arguments:
- tokens: bfloat16 [64, 512, 768], P('dp', 'blk'), may hold values from -6 to 6
- cotangent: bfloat16 [64, 512, 768], P('dp', 'blk'), may hold values from -6 to 6
- lengths: int32 [64], P('dp'), may hold values from 1 to 512, as said below
- owners: int32 [8], replicated, may hold values from 0 to 7, as said below
- master: float32 [9216, 768], P('dp')
- moment_one: float32 [9216, 768], P('dp')
- moment_two: float32 [9216, 768], P('dp'), as said below
- vectors: float32 [9216], replicated
- vector_one: float32 [9216], replicated
- vector_two: float32 [9216], replicated, as said below
Outputs:
- output: bfloat16 [64, 512, 768], P('dp', 'blk')
- grad_tokens: bfloat16 [64, 512, 768], P('dp', 'blk')
- grad_norm: float32 [], replicated
- new_master: float32 [9216, 768], P('dp')
- new_moment_one: float32 [9216, 768], P('dp')
- new_moment_two: float32 [9216, 768], P('dp')
- new_vectors: float32 [9216], replicated
- new_vector_one: float32 [9216], replicated
- new_vector_two: float32 [9216], replicated
The draws below stay inside these ranges and needn't reach their ends.
Inputs may be any that keep to these rules, and one draw needn't show every extreme that they name: `lengths`: in each aligned block of 8 passages (those of one index of dp) at least one passage has length 512. A permutation: index d of dp owns row block owners[d] of the weight table. `moment_two`: Positive. `vector_two`: Positive.
All inputs are finite; a program needn't handle non-finite values.
Results may differ from the reference program's by a relative error of at most 0.014.
Values may be sent and summed in bfloat16 or wider, within the bound.
A program may use at most 256 MiB of HBM per device.

```python
import jax
import jax.numpy as jnp
from jax import lax

D = 768
HEADS = 12
HEAD_DIM = 64
FF = 3072
SEQ = 512
PASS_DEV = 8
STEP = 10
PASSAGES = 64
PARAM_ROWS = 9216
VEC_LEN = 9216
N_DP = 8


def owner_order(key):
    return jax.random.permutation(jax.random.fold_in(key, 101), N_DP).astype(jnp.int32)


def row_kinds(key):
    owners = owner_order(key)
    own_rows = PARAM_ROWS // N_DP
    row_index = jnp.arange(PARAM_ROWS)
    return owners[row_index // own_rows] * own_rows + row_index % own_rows


def kind_of(table_row, levels):
    edge_list = [D, 2 * D, 3 * D, 4 * D, 4 * D + FF]
    result = jnp.full(table_row.shape, levels[5], jnp.float32)
    for edge_row, level_val in reversed(list(zip(edge_list, levels[:5]))):
        result = jnp.where(table_row < edge_row, level_val, result)
    return result


def segment_values(levels):
    edge_list = [D, 2 * D, 3 * D, 3 * D + FF, 4 * D + FF, 5 * D + FF, 6 * D + FF, 7 * D + FF]
    row_index = jnp.arange(VEC_LEN)
    result = jnp.full((VEC_LEN,), levels[8], jnp.float32)
    for edge_row, level_val in reversed(list(zip(edge_list, levels[:8]))):
        result = jnp.where(row_index < edge_row, level_val, result)
    return result


def grad_scale():
    weighted = 0.09 * D * D * 2 + 0.36 * D * D * 2 + 1.0 * D * FF * 2 + 4.0 * (8 * D + FF)
    return weighted ** (-0.5)


def grad_levels():
    base_scale = grad_scale()
    return (0.3 * base_scale, 0.3 * base_scale, 0.6 * base_scale, 0.6 * base_scale, base_scale, base_scale)


def unit_draw(key, shape, bound):
    return jnp.clip(jax.random.normal(key, shape, jnp.float32), -bound, bound)


def factor_draw(key, shape):
    return jnp.exp(jax.random.uniform(key, shape, jnp.float32, 0.0, 1.3862944))


def draw_lengths(key, part):
    key = jax.random.fold_in(key, 31)
    k_bucket, k_len, k_full = jax.random.split(key, 3)
    bucket_pick = jax.random.randint(k_bucket, (PASSAGES,), 0, 10)
    low_edge = jnp.where(bucket_pick < 5, 0, jnp.where(bucket_pick < 8, SEQ // 4, SEQ // 2))
    bucket_span = jnp.where(bucket_pick < 8, SEQ // 4, SEQ // 2)
    offset = jax.random.randint(k_len, (PASSAGES,), 0, SEQ // 2)
    length = low_edge + 1 + offset % bucket_span
    full_slot = jax.random.randint(k_full, (N_DP,), 0, PASS_DEV)
    is_full = jnp.arange(PASSAGES) % PASS_DEV == jnp.repeat(full_slot, PASS_DEV)
    return jnp.where(is_full, SEQ, length).astype(jnp.int32)


def draw_owners(key, part):
    return owner_order(key)


def draw_master(key, part):
    table_row = row_kinds(key)
    key = jax.random.fold_in(key, 11)
    scales = kind_of(table_row, (1.3 * D ** (-0.5), 1.3 * D ** (-0.5), D ** (-0.5), 4.0 * D ** (-0.5), D ** (-0.5), FF ** (-0.5)))
    return (unit_draw(key, (PARAM_ROWS, D), 5.0) * scales[:, None]).astype(jnp.float32)


def draw_moment_one(key, part):
    table_row = row_kinds(key)
    key = jax.random.fold_in(key, 12)
    scales = kind_of(table_row, grad_levels())
    return (unit_draw(key, (PARAM_ROWS, D), 5.0) * scales[:, None]).astype(jnp.float32)


def draw_moment_two(key, part):
    table_row = row_kinds(key)
    key = jax.random.fold_in(key, 13)
    scales = kind_of(table_row, grad_levels())
    return (factor_draw(key, (PARAM_ROWS, D)) * (scales * scales)[:, None]).astype(jnp.float32)


def draw_vectors(key, part):
    key = jax.random.fold_in(key, 41)
    base_draw = unit_draw(key, (VEC_LEN,), 3.0)
    spread = segment_values((0.5, 0.2, 0.3, 0.5, 0.3, 0.2, 0.3, 0.2, 0.3))
    centre = segment_values((0.0, 0.0, 0.0, 0.0, 0.0, 1.0, 0.0, 1.0, 0.0))
    return (base_draw * spread + centre).astype(jnp.float32)


def draw_vector_one(key, part):
    key = jax.random.fold_in(key, 42)
    return (unit_draw(key, (VEC_LEN,), 5.0) * (2.0 * grad_scale())).astype(jnp.float32)


def draw_vector_two(key, part):
    key = jax.random.fold_in(key, 43)
    vec_scale = 2.0 * grad_scale()
    return (factor_draw(key, (VEC_LEN,)) * vec_scale * vec_scale).astype(jnp.float32)


def shard_levels(stream_key, dims, cuts, low, top_value):
    level = 1.0
    for dim, shards_of in cuts:
        draws = jax.random.uniform(jax.random.fold_in(jax.random.fold_in(stream_key, 6), dim), (shards_of,), jnp.float32, low / len(cuts), top_value / len(cuts))
        level = level * jnp.repeat(jnp.exp(draws), dims[dim] // shards_of).reshape((-1,) + (1,) * (len(dims) - 1 - dim))
    return level


def scatter_about(own_key, extent, scale, most, pieces=(), held_as=jnp.bfloat16):
    entries = scale * jax.random.normal(own_key, extent, jnp.float32)
    if pieces:
        entries = entries * shard_levels(own_key, extent, pieces, -0.22, 0.18)
    return jnp.clip(entries, -most, most).astype(held_as)


def setup_inputs(seed: int = 0) -> dict:
    seeds = jax.random.split(jax.random.key(seed), 11)
    return {
        "tokens": scatter_about(seeds[0], (PASSAGES, SEQ, D), 1.0, 6.0, ((0, 8), (1, 4))),
        "cotangent": scatter_about(seeds[1], (PASSAGES, SEQ, D), 1.0, 6.0, ((0, 8), (1, 4))),
        "lengths": draw_lengths(jax.random.fold_in(seeds[10], 71), 0),
        "owners": draw_owners(jax.random.fold_in(seeds[10], 71), 0),
        "master": draw_master(jax.random.fold_in(seeds[10], 71), 0),
        "moment_one": draw_moment_one(jax.random.fold_in(seeds[10], 71), 0),
        "moment_two": draw_moment_two(jax.random.fold_in(seeds[10], 71), 0),
        "vectors": draw_vectors(jax.random.fold_in(seeds[10], 71), 0),
        "vector_one": draw_vector_one(jax.random.fold_in(seeds[10], 71), 0),
        "vector_two": draw_vector_two(jax.random.fold_in(seeds[10], 71), 0),
    }


HIGH = lax.Precision.HIGHEST
beta_one = 0.5
beta_two = 0.5
learn_rate = 0.05
vector_rate = 0.3
weight_decay = 0.01
adam_eps = 1e-08
clip_norm = 1.0

@jax.custom_vjp
def low(v):
    return lax.optimization_barrier(v.astype(jnp.bfloat16)).astype(jnp.float32)

@jax.custom_vjp
def low_back(v):
    return v

def low_keep(v):
    return (low(v), None)

def low_pass(kept, grad):
    return (grad,)

def back_keep(v):
    return (v, None)

def back_low(kept, grad):
    return (low(grad),)
low.defvjp(low_keep, low_pass)
low_back.defvjp(back_keep, back_low)

def split_table(weight_table):
    return (weight_table[0:D], weight_table[D:2 * D], weight_table[2 * D:3 * D], weight_table[3 * D:4 * D], weight_table[4 * D:4 * D + FF], weight_table[4 * D + FF:4 * D + 2 * FF])

def split_vector(vec_table):
    edge_list = [0, D, 2 * D, 3 * D, 3 * D + FF, 4 * D + FF, 5 * D + FF, 6 * D + FF, 7 * D + FF, 8 * D + FF]
    return tuple((vec_table[edge_list[slot]:edge_list[slot + 1]] for slot in range(9)))

def layer_norm(mixed, gain_vec, shift_vec):
    row_mean = lax.optimization_barrier(jnp.mean(mixed, axis=-1, keepdims=True))
    centred = mixed - row_mean
    row_var = lax.optimization_barrier(jnp.mean(centred * centred, axis=-1, keepdims=True))
    return centred * lax.rsqrt(row_var + 1e-12) * gain_vec + shift_vec

def forward(token_rows, weight_table, vec_table, lengths):
    group_size = token_rows.shape[0]
    w_query, w_key, w_value, w_out, w_inner, w_outer = split_table(weight_table)
    b_query, b_value, b_out, b_inner, b_outer, gain_one, shift_one, gain_two, shift_two = split_vector(vec_table)
    queries = low(low_back(jnp.einsum('psd,de->pse', token_rows, w_query, precision=HIGH) + b_query))
    key_rows = low(low_back(jnp.einsum('psd,de->pse', token_rows, w_key, precision=HIGH)))
    values = low(low_back(jnp.einsum('psd,de->pse', token_rows, w_value, precision=HIGH) + b_value))
    q_heads = queries.reshape(group_size, SEQ, HEADS, HEAD_DIM)
    k_heads = key_rows.reshape(group_size, SEQ, HEADS, HEAD_DIM)
    v_heads = values.reshape(group_size, SEQ, HEADS, HEAD_DIM)
    key_valid = jnp.arange(SEQ)[None, :] < lengths[:, None]
    scores = low_back(jnp.einsum('pqhe,pkhe->phqk', q_heads, k_heads, precision=HIGH) * 0.125)
    scores = jnp.where(key_valid[:, None, None, :], scores, -1000000000.0)
    attn_probs = low(jax.nn.softmax(scores, axis=-1))
    context = jnp.einsum('phqk,pkhe->pqhe', attn_probs, v_heads, precision=HIGH).reshape(group_size, SEQ, D)
    context = low(low_back(context))
    attn_out = low_back(jnp.einsum('psd,de->pse', context, w_out, precision=HIGH) + b_out)
    hidden = layer_norm(token_rows + attn_out, gain_one, shift_one)
    inner_pre = low_back(jnp.einsum('psd,fd->psf', low(hidden), w_inner, precision=HIGH) + b_inner)
    active = low(jax.nn.gelu(inner_pre, approximate=False))
    branch = low_back(jnp.einsum('psf,fd->psd', active, w_outer, precision=HIGH) + b_outer)
    return layer_norm(hidden + branch, gain_two, shift_two)

def adamw(weight, first, second, grad, decay, rate):
    new_first = beta_one * first + (1.0 - beta_one) * grad
    new_second = beta_two * second + (1.0 - beta_two) * grad * grad
    direction = new_first / (1.0 - beta_one ** STEP) / (jnp.sqrt(new_second / (1.0 - beta_two ** STEP)) + adam_eps)
    return (weight - rate * (direction + decay * weight), new_first, new_second)

def reference(tokens, cotangent, lengths, owners, master, moment_one, moment_two, vectors, vector_one, vector_two):
    own_rows = master.shape[0] // N_DP
    inverse = jnp.argsort(owners).astype(jnp.int32)
    table_f32 = low(master).reshape(N_DP, own_rows, D)[inverse].reshape(-1, D)
    token_groups = tokens.astype(jnp.float32).reshape(N_DP, PASS_DEV, SEQ, D)
    cot_groups = cotangent.astype(jnp.float32).reshape(N_DP, PASS_DEV, SEQ, D)
    len_groups = lengths.reshape(N_DP, PASS_DEV)

    def group_step(carry, item):
        token_group, cot_group, len_group = item

        def apply_layer(token_rows, weight_table, vec_table):
            return forward(token_rows, weight_table, vec_table, len_group)
        result, pull_back = jax.vjp(apply_layer, token_group, table_f32, vectors)
        row_mask = (jnp.arange(SEQ)[None, :] < len_group[:, None]).astype(jnp.float32)
        d_tokens, d_table, d_vector = pull_back(cot_group * row_mask[:, :, None])
        return ((carry[0] + d_table, carry[1] + d_vector), (result.astype(jnp.bfloat16), d_tokens.astype(jnp.bfloat16)))
    start = (jnp.zeros((4 * D + 2 * FF, D), jnp.float32), jnp.zeros((8 * D + FF,), jnp.float32))
    (grad_table, grad_vector), (outputs, grads) = lax.scan(group_step, start, (token_groups, cot_groups, len_groups))
    grad_owned = grad_table.reshape(N_DP, own_rows, D)[owners].reshape(-1, D)
    grad_norm = jnp.sqrt(jnp.sum(grad_owned * grad_owned) + jnp.sum(grad_vector * grad_vector))
    factor = jnp.minimum(1.0, clip_norm / (grad_norm + 1e-06))
    new_master, new_one, new_two = adamw(master, moment_one, moment_two, grad_owned * factor, weight_decay, learn_rate)
    new_vectors, new_vone, new_vtwo = adamw(vectors, vector_one, vector_two, grad_vector * factor, 0.0, vector_rate)
    return (outputs.reshape(-1, SEQ, D), grads.reshape(-1, SEQ, D), grad_norm, new_master, new_one, new_two, new_vectors, new_vone, new_vtwo)
```

```python
import functools
import math

import jax
import jax.numpy as jnp
from jax import lax
from jax.experimental import pallas as pl
from jax.experimental.pallas import tpu as pltpu
from jax.sharding import PartitionSpec as P

D = 768
HEADS = 12
HEAD_DIM = 64
FF = 3072
STEP = 10
VEC_LEN = 8 * D + FF


beta_one = 0.5
beta_two = 0.5
learn_rate = 0.05
vector_rate = 0.3
weight_decay = 0.01
adam_eps = 1e-08
clip_norm = 1.0


def norm_back(d_normed, normed, inv_std):
    first_mean = jnp.mean(d_normed, axis=-1, keepdims=True)
    second_mean = jnp.mean(d_normed * normed, axis=-1, keepdims=True)
    return inv_std * (d_normed - first_mean - normed * second_mean)


def contract_rows(left, right):
    return lax.dot_general(
        left, right, (((0,), (0,)), ((), ())), preferred_element_type=jnp.float32
    )


def contract_cols(left, right):
    return lax.dot_general(
        left, right, (((1,), (1,)), ((), ())), preferred_element_type=jnp.float32
    )


def adamw(weight, first, second, grad, decay, rate):
    new_first = beta_one * first + (1.0 - beta_one) * grad
    new_second = beta_two * second + (1.0 - beta_two) * grad * grad
    direction = (
        new_first
        / (1.0 - beta_one**STEP)
        / (jnp.sqrt(new_second / (1.0 - beta_two**STEP)) + adam_eps)
    )
    return (weight - rate * (direction + decay * weight), new_first, new_second)


MESH = pl.DeviceIdType.MESH
GRAIN = 48
OUTER_COUNTS = (8,)
BACK_COUNTS = (2, 8)
QKV_COUNTS = (6,)


def add_low(left, right):
    return (left.astype(jnp.float32) + right.astype(jnp.float32)).astype(jnp.bfloat16)


def enter_kernel(
    nz,
    full,
    owners_ref,
    tokens_ref,
    cot_ref,
    master_ref,
    lengths_ref,
    lanes_ref,
    tokens_out,
    cot_out,
    table_out,
    q_out,
    k_out,
    v_out,
    lse_out,
    ctx_out,
    normed_out,
    inv_out,
    vec_ref,
    wide,
    own_wide,
    tokens_land,
    cot_land,
    whole_out,
    quarter_out,
    ordered,
    load_sem,
    swap_sem,
    keep_sem,
    z_sem,
    one_sem,
    two_sem,
    sib_sem,
    sib_own_sem,
    out_sem,
    q_all,
    k_all,
    v_all,
    v_turned,
    lse_all,
    ctx_all,
    normed_all,
    inv_all,
    ctx_turned,
    scores,
    weights,
    work_sem,
):
    dp, blk, z, c, y, x, sibling, x_peer, y_peer = place_of()
    diagonal = (3 - blk, dp)
    passages, span = tokens_out.shape[0], tokens_ref.shape[1]
    quarter = quarter_out.shape[4]
    low_whole, low_quarter = whole_out.at[dp], quarter_out.at[dp]

    own_rows = pl.ds(pl.multiple_of(full + blk * 2 * quarter, 16), 2 * quarter)
    loads = [
        pltpu.make_async_copy(master_ref.at[own_rows], own_wide, load_sem.at[0]),
        pltpu.make_async_copy(master_ref, wide, load_sem.at[1]),
    ]
    for load in loads:
        load.start()
    own_copies = []
    for slot, (rows_in, rows_out) in enumerate(((tokens_ref, tokens_land), (cot_ref, cot_land))):
        own_copies.append(
            pltpu.make_async_copy(
                rows_in.at[pl.ds(blk * passages, passages)],
                rows_out.at[:, pl.ds(blk * span, span)],
                keep_sem.at[slot],
            )
        )
        own_copies[-1].start()

    for row in range(VEC_LEN // D):
        for col in range(D // 128):
            at = row * (D // 128) + col
            vec_ref[row : row + 1, col * 128 : (col + 1) * 128] = lanes_ref[at : at + 1]

    barrier = pltpu.get_barrier_semaphore()
    for partner in (sibling, x_peer, y_peer, diagonal):
        pl.semaphore_signal(barrier, inc=1, device_id=partner, device_id_type=MESH)
    below, above = z > 0, z < nz - 1

    @pl.when(below)
    def _():
        pl.semaphore_signal(barrier, inc=1, device_id=(blk, dp - 2), device_id_type=MESH)

    @pl.when(above)
    def _():
        pl.semaphore_signal(barrier, inc=1, device_id=(blk, dp + 2), device_id_type=MESH)

    pl.semaphore_wait(barrier, 4 + jnp.where(below, 1, 0) + jnp.where(above, 1, 0))

    def remote(src, dst, sems, slot, device):
        return pltpu.make_async_remote_copy(
            src_ref=src,
            dst_ref=dst,
            send_sem=sems.at[(0, *slot)],
            recv_sem=sems.at[(1, *slot)],
            device_id=device,
            device_id_type=MESH,
        )

    def swap(which, rows_in, rows_out, peer, slot):
        return remote(
            rows_in.at[pl.ds(peer[0] * passages, passages)],
            rows_out.at[:, pl.ds(blk * span, span)],
            swap_sem,
            (which, slot),
            peer,
        )

    swaps = [
        swap(which, rows_in, rows_out, peer, slot)
        for which, (rows_in, rows_out) in enumerate(((tokens_ref, tokens_land), (cot_ref, cot_land)))
        for slot, peer in enumerate((x_peer, y_peer, diagonal))
    ]
    loads[0].wait()
    for half in range(2):
        quarter_out[dp, y, x, half] = own_wide[half * quarter : (half + 1) * quarter].astype(
            jnp.bfloat16
        )

    def pass_on(src_quarter, src_whole, at, upward, which):
        device = (blk, dp + 2 if upward else dp - 2)
        way = 0 if upward else 1
        if which == 0:
            return remote(src_quarter, quarter_out.at[at, y, x], z_sem, (way, 0, at // 2), device)
        return remote(src_whole, whole_out.at[at], z_sem, (way, 1, at // 2), device)

    @pl.when(above)
    def _():
        pass_on(low_quarter.at[y, x], None, dp, True, 0).start()

    @pl.when(below)
    def _():
        pass_on(low_quarter.at[y, x], None, dp, False, 0).start()

    for copy in swaps[:3]:
        copy.start()
    loads[1].wait()
    whole_out[dp] = wide[0:full].astype(jnp.bfloat16)
    for part in range(8):

        @pl.when(blk != part // 2)
        def _(part=part):
            start = full + part * quarter
            quarter_out[dp, part // 4, part // 2 % 2, part % 2] = wide[
                start : start + quarter
            ].astype(jnp.bfloat16)

    def own_whole(turn):
        @pl.when(jnp.logical_and(above, z + 1 == turn))
        def _():
            pass_on(None, low_whole, dp, True, 1).start()

        @pl.when(jnp.logical_and(below, nz - z == turn))
        def _():
            pass_on(None, low_whole, dp, False, 1).start()

    sib_own = [
        remote(low_quarter, quarter_out.at[dp], sib_own_sem, (0,), sibling),
        remote(low_whole, whole_out.at[dp], sib_own_sem, (1,), sibling),
    ]
    for copy in sib_own:
        copy.start()
    def sources(act):
        def at_distance(distance):
            @pl.when(z >= distance)
            def _():
                act(dp - 2 * distance, True, z < nz - 1)

            @pl.when(z + distance < nz)
            def _():
                act(dp + 2 * distance, False, z > 0)

        return at_distance

    def forward(ref_view, at, slot):
        return remote(ref_view, ref_view, sib_sem, (slot, at // 2), sibling)

    def one_x(at):
        view = quarter_out.at[at, y, x, 0]
        return remote(view, view, one_sem, (0, at // 2), x_peer)

    def one_y(at):
        view = quarter_out.at[at, y, x, 1]
        return remote(view, view, one_sem, (1, at // 2), y_peer)

    def two_y(at):
        view = quarter_out.at[at, y, :, 0]
        return remote(view, view, two_sem, (0, at // 2), y_peer)

    def two_x(at):
        view = quarter_out.at[at, :, x, 1]
        return remote(view, view, two_sem, (1, at // 2), x_peer)

    def sib_views(at):
        return [
            quarter_out.at[at, y, x],
            quarter_out.at[at, y, 1 - x, 0],
            quarter_out.at[at, 1 - y, x, 1],
            quarter_out.at[at, 1 - y, :, 0],
            quarter_out.at[at, :, 1 - x, 1],
            whole_out.at[at],
        ]

    def quarter_came(at, upward, onward):
        view = quarter_out.at[at, y, x]
        pass_on(view, None, at, upward, 0).wait_recv()

        @pl.when(onward)
        def _():
            pass_on(view, None, at, upward, 0).start()

        one_x(at).start()
        one_y(at).start()
        forward(sib_views(at)[0], at, 0).start()

    def whole_came(at, upward, onward):
        view = whole_out.at[at]
        pass_on(None, view, at, upward, 1).wait_recv()

        @pl.when(onward)
        def _():
            pass_on(None, view, at, upward, 1).start()

        forward(sib_views(at)[5], at, 5).start()

    def one_came(at, upward, onward):
        one_x(at).wait_recv()
        two_y(at).start()
        forward(sib_views(at)[1], at, 1).start()
        one_y(at).wait_recv()
        two_x(at).start()
        forward(sib_views(at)[2], at, 2).start()

    def two_came(at, upward, onward):
        two_y(at).wait_recv()
        forward(sib_views(at)[3], at, 3).start()
        two_x(at).wait_recv()
        forward(sib_views(at)[4], at, 4).start()

    def finished(at, upward, onward):
        view = quarter_out.at[at, y, x]

        @pl.when(onward)
        def _():
            pass_on(view, None, at, upward, 0).wait_send()
            pass_on(None, whole_out.at[at], at, upward, 1).wait_send()

        one_x(at).wait_send()
        one_y(at).wait_send()
        two_x(at).wait_send()
        two_y(at).wait_send()
        for slot, ref_view in enumerate(sib_views(at)):
            copy = forward(ref_view, at, slot)
            copy.wait_send()
            copy.wait_recv()

    for distance in range(1, nz):
        sources(quarter_came)(distance)
        if distance == nz - 1:
            sources(one_came)(1)
        own_whole(distance)
    plan = [(whole_came, 1)] + [(one_came, d) for d in range(2, nz)]
    for distance in range(2, nz):
        plan += [(whole_came, distance), (two_came, distance - 1)]
    plan += [(two_came, nz - 1)]
    for act, distance in plan:
        sources(act)(distance)
    for distance in range(1, nz):
        sources(finished)(distance)

    @pl.when(above)
    def _():
        pass_on(low_quarter.at[y, x], None, dp, True, 0).wait_send()
        pass_on(None, low_whole, dp, True, 1).wait_send()

    @pl.when(below)
    def _():
        pass_on(low_quarter.at[y, x], None, dp, False, 0).wait_send()
        pass_on(None, low_whole, dp, False, 1).wait_send()

    for copy in swaps[3:]:
        copy.start()
    for copy in own_copies[:1] + swaps[:3] + sib_own:
        copy.wait()
    stores = [pltpu.make_async_copy(tokens_land, tokens_out, out_sem.at[2 * nz])]
    stores[0].start()

    def put(block):
        place = 0
        for index in range(2 * nz):
            place = jnp.where(owners_ref[index] == block, index, place)
        rows = wide.shape[0]
        base = block * rows
        ordered[base : base + full] = whole_out[place]
        for part in range(8):
            start = base + full + part * quarter
            ordered[start : start + quarter] = quarter_out[
                place, part // 4, part // 2 % 2, part % 2
            ]
        table = pl.ds(base, rows)
        return pltpu.make_async_copy(ordered.at[table], table_out.at[table], out_sem.at[block])

    early = -(-4 * D // wide.shape[0])
    for block in range(early):
        stores.append(put(block))
        stores[-1].start()

    results = []

    def give(src, dst):
        copy = pltpu.make_async_copy(src, dst, work_sem.at[len(results)])
        results.append(copy)
        return copy

    for p in range(passages):
        project(
            tokens_land[p], ordered, vec_ref, q_all.at[p], k_all.at[p], v_all.at[p], v_turned.at[p]
        )
    for src, dst in ((q_all, q_out), (k_all, k_out), (v_all, v_out)):
        give(src, dst).start()
    pairs = HEADS // 2
    lengths = [lengths_ref[blk * passages + p] for p in range(passages)]

    def finish(p):
        first_norm(
            tokens_land[p], ctx_all[p], ordered, vec_ref, normed_all.at[p], inv_all.at[p]
        )
        for src, dst in (
            (ctx_all, ctx_out),
            (normed_all, normed_out),
            (inv_all, inv_out),
            (lse_all, lse_out),
        ):
            give(src.at[p], dst.at[p]).start()

    for p in range(passages):

        @pl.loop(0, pairs)
        def _(pair, p=p):
            for slot in range(pairs):
                block = early + p * pairs + slot
                if block < 2 * nz:

                    @pl.when(pair == slot)
                    def _(block=block):
                        put(block).start()

            attend_pair(
                pair,
                lengths[p],
                q_all.at[p],
                k_all.at[p],
                v_turned.at[p],
                lse_all.at[p],
                ctx_all.at[p],
                ctx_turned,
                scores,
                weights,
            )

        if p == passages - 1:
            for copy in own_copies[1:] + swaps[3:]:
                copy.wait()
            give(cot_land, cot_out).start()
        finish(p)
    for block in range(early, 2 * nz):
        table = pl.ds(block * wide.shape[0], wide.shape[0])
        stores.append(
            pltpu.make_async_copy(ordered.at[table], table_out.at[table], out_sem.at[block])
        )
    for copy in stores + results:
        copy.wait()


def enter(nz, full, owners, tokens, cotangent, master, lengths, vectors):
    f32, low = jnp.float32, jnp.bfloat16
    rows = master.shape[0]
    quarter = (rows - full) // 8
    shares, span, _ = tokens.shape
    passages, span = shares // 4, 4 * span
    swapped = (passages, span, D)
    any_spec = pl.BlockSpec(memory_space=pl.ANY)
    smem = pl.BlockSpec(memory_space=pltpu.SMEM)
    dma = pltpu.SemaphoreType.DMA
    shape = lambda kind: jax.ShapeDtypeStruct(swapped, kind)
    lse = (passages, HEADS, 1, span)
    return pl.pallas_call(
        functools.partial(enter_kernel, nz, full),
        out_shape=(
            shape(low),
            shape(low),
            jax.ShapeDtypeStruct((2 * nz * rows, D), low),
            shape(low),
            shape(low),
            shape(low),
            jax.ShapeDtypeStruct(lse, f32),
            shape(low),
            shape(f32),
            jax.ShapeDtypeStruct((passages, span, 128), f32),
            jax.ShapeDtypeStruct((VEC_LEN // D, D), f32),
        ),
        in_specs=[smem] + [any_spec] * 3 + [smem, pl.BlockSpec(memory_space=pltpu.VMEM)],
        out_specs=[any_spec] * 10 + [pl.BlockSpec(memory_space=pltpu.VMEM)],
        scratch_shapes=[
            pltpu.VMEM((rows, D), f32),
            pltpu.VMEM((2 * quarter, D), f32),
            pltpu.VMEM(swapped, low),
            pltpu.VMEM(swapped, low),
            pltpu.VMEM((2 * nz, full, D), low),
            pltpu.VMEM((2 * nz, 2, 2, 2, quarter, D), low),
            pltpu.VMEM((2 * nz * rows, D), low),
            dma((2,)),
            dma((2, 2, 3)),
            dma((2,)),
            dma((2, 2, 2, nz)),
            dma((2, 2, nz)),
            dma((2, 2, nz)),
            dma((2, 6, nz)),
            dma((2, 2)),
            dma((2 * nz + 1,)),
            pltpu.VMEM(swapped, low),
            pltpu.VMEM(swapped, low),
            pltpu.VMEM(swapped, low),
            pltpu.VMEM((passages, D, span), low),
            pltpu.VMEM(lse, f32),
            pltpu.VMEM(swapped, low),
            pltpu.VMEM(swapped, f32),
            pltpu.VMEM((passages, span, 128), f32),
            pltpu.VMEM((128, span), f32),
            pltpu.VMEM((2, span, span // 2), f32),
            pltpu.VMEM((2, span, span // 2), low),
            dma((4 + 4 * passages,)),
        ],
        compiler_params=pltpu.CompilerParams(
            collective_id=2, has_side_effects=True, vmem_limit_bytes=60 * 1024 * 1024
        ),
        cost_estimate=pl.CostEstimate(
            flops=passages * span * (8 * D * D + 4 * D * span),
            bytes_accessed=6 * 10**7,
            transcendentals=passages * HEADS * span * span,
        ),
        name="enter",
    )(owners, tokens, cotangent, master, lengths, vectors.reshape(-1, 128))


def tail_kernel(
    nz,
    owners_ref,
    qkv_ref,
    back_ref,
    vec_ref,
    d_tokens_ref,
    own_ref,
    vec_sum_ref,
    norm_ref,
    d_tokens_out,
    acc,
    core_land,
    land_one,
    land_two,
    load_sem,
    core_sem,
    one_sem,
    two_sem,
    part,
    mine,
    up_land,
    down_land,
    up_send,
    down_send,
    own_part,
    assembled,
    vec_send,
    vec_land,
    sq_send,
    sq_land,
    part_sem,
    up_sem,
    down_sem,
    gather_sem,
    vec_sem,
    sq_sem,
    out_sem,
    *swap_refs,
):
    dp, blk, z, c, y, x, sibling, x_peer, y_peer = place_of()

    def z_peer(hop):
        return (blk, 2 * lax.rem(z + hop, nz) + c)

    def send(src, dst, sems, slot, device):
        copy = remote_copy(src, dst, sems, slot, device)
        copy.start()
        return copy

    swaps = [
        PositionSwap(d_tokens_ref, d_tokens_out, *swap_refs),
    ]
    partners = [sibling, x_peer, y_peer, swaps[0].diagonal] + [z_peer(h) for h in range(1, nz)]
    barrier = greet(partners)
    late = qkv_ref.shape[0]
    load = pltpu.make_async_copy(back_ref, part.at[pl.ds(late, back_ref.shape[0])], part_sem)
    load.start()
    sems = (load_sem, core_sem, one_sem, two_sem)
    summed = PlaneSum((qkv_ref,), QKV_COUNTS, acc, core_land, land_one, land_two, part, sems)
    slots = range(len(summed.chunks))
    for row in range(VEC_LEN // D):
        for col in range(D // 128):
            at = row * (D // 128) + col
            vec_send[0, at : at + 1] = vec_ref[row : row + 1, col * 128 : (col + 1) * 128]
    pl.semaphore_wait(barrier, len(partners))
    summed.begin(slots)

    def vec_copy(turn):
        peer = (sibling, x_peer, y_peer)[turn]
        return remote_copy(vec_send.at[turn], vec_land.at[turn], vec_sem, turn, peer)

    def vec_next(turn):
        vec_copy(turn).wait()
        vec_send[turn + 1] = vec_send[turn] + vec_land[turn]
        if turn < 2:
            vec_copy(turn + 1).start()

    vec_copy(0).start()
    summed.paired(slots)
    vec_next(0)
    vec_next(1)
    vec_next(2)
    vec_z = [
        send(vec_send.at[3], vec_land.at[3 + z], vec_sem, 2 + hop, z_peer(hop))
        for hop in range(1, nz)
    ]
    summed.crossed(slots)
    load.wait()
    summed.settled(slots)
    for swap in swaps:
        swap.begin()

    grains = part.shape[0] // (2 * nz)
    for block in range(2 * nz):
        place = owners_ref[block] * grains
        for g in range(grains):
            mine[block, g] = part[place + g]

    def gather(turn, piece):
        views = (
            (own_part.at[1 - c, piece], assembled.at[piece, c, y, x], sibling),
            (assembled.at[piece, 0, y, x], assembled.at[piece, 0, y, x], x_peer),
            (assembled.at[piece, 1, y, x], assembled.at[piece, 1, y, x], y_peer),
            (assembled.at[piece, 0, y], assembled.at[piece, 0, y], y_peer),
            (assembled.at[piece, 1, :, x], assembled.at[piece, 1, :, x], x_peer),
        )
        src, dst, peer = views[turn]
        return remote_copy(src, dst, gather_sem, turn * grains + piece, peer)

    def chain(zv):
        unit, wait = 3.0, 2.5
        steps, copies = [], []

        def message(upward, d, piece):
            land, sends, sems = (
                (up_land, up_send, up_sem) if upward else (down_land, down_send, down_sem)
            )
            target = (blk, dp + 2 if upward else dp - 2)
            return remote_copy(
                sends.at[d, piece], land.at[d, piece], sems, d * grains + piece, target
            )

        def passing(upward, d, piece):
            def run():
                land, sends = (up_land, up_send) if upward else (down_land, down_send)
                fed = zv > 0 if upward else zv < nz - 1
                copy = message(upward, d, piece)
                if fed:
                    copy.wait_recv()
                for j in range(2):
                    value = mine[2 * d + j, piece]
                    if fed:
                        value = add_low(value, land[d, piece, j])
                    sends[d, piece, j] = value
                copy.start()
                copies.append(copy)

            return run

        def arrived(piece):
            if zv > 0:
                message(True, zv, piece).wait_recv()
            if zv < nz - 1:
                message(False, zv, piece).wait_recv()
            squares = jnp.zeros((8, D), jnp.float32)
            for j in range(2):
                value = mine[2 * zv + j, piece].astype(jnp.float32)
                if zv > 0:
                    value = value + up_land[zv, piece, j].astype(jnp.float32)
                if zv < nz - 1:
                    value = value + down_land[zv, piece, j].astype(jnp.float32)
                rounded = value.astype(jnp.bfloat16)
                own_part[j, piece] = rounded
                again = rounded.astype(jnp.float32)
                squares = squares + jnp.sum((again * again).reshape(-1, 8, D), axis=0)
            total = squares[:, 0:128]
            for col in range(1, D // 128):
                total = total + squares[:, col * 128 : (col + 1) * 128]
            sq_send[0] = total if piece == 0 else sq_send[0] + total
            assembled[piece, c, y, x] = own_part[c, piece]
            gather(0, piece).start()

        def over_pair(piece):
            gather(0, piece).wait()
            gather(1, piece).start()
            gather(2, piece).start()

        def over_plane(piece):
            gather(1, piece).wait()
            gather(3, piece).start()
            gather(2, piece).wait()
            gather(4, piece).start()

        for piece in range(grains):
            first = piece * (nz - 1)
            for d in range(zv + 1, nz):
                at = (zv + first + nz - 1 - d) * unit + zv * wait
                steps.append((at, passing(True, d, piece)))
            for d in range(zv):
                at = (nz - 1 - zv + first + d) * unit + (nz - 1 - zv) * wait
                steps.append((at, passing(False, d, piece)))
            end = (first + nz - 1) * unit + (nz - 1) * wait
            steps.append((end, functools.partial(arrived, piece)))
            if piece < grains - 1:
                steps.append((end + 5.0, functools.partial(over_pair, piece)))
                steps.append((end + 9.5, functools.partial(over_plane, piece)))
        for _, step in sorted(steps, key=lambda entry: entry[0]):
            step()
        for copy in copies:
            copy.wait_send()
        sq = remote_copy(sq_send.at[0], sq_land.at[0], sq_sem, 0, sibling)
        sq.start()
        over_pair(grains - 1)
        sq.wait()

    for zv in range(nz):
        run_when(z == zv, functools.partial(chain, zv))

    for swap in swaps:
        swap.passed()
    sq_send[1] = sq_send[0] + sq_land[0]
    sq = send(sq_send.at[1], sq_land.at[1], sq_sem, 1, x_peer)
    sq.wait()
    sq_send[2] = sq_send[1] + sq_land[1]
    sq = send(sq_send.at[2], sq_land.at[2], sq_sem, 2, y_peer)
    last = grains - 1
    gather(1, last).wait()
    gather(3, last).start()
    gather(2, last).wait()
    gather(4, last).start()
    sq.wait()
    sq_send[3] = sq_send[2] + sq_land[2]
    sq_z = [
        send(sq_send.at[3], sq_land.at[3 + z], sq_sem, 2 + hop, z_peer(hop)) for hop in range(1, nz)
    ]
    for copy in vec_z + sq_z:
        copy.wait()
    vec_land[3 + z] = vec_send[3]
    sq_land[3 + z] = sq_send[3]
    vec_total, sq_total = vec_land[3], sq_land[3]
    for other in range(1, nz):
        vec_total = vec_total + vec_land[3 + other]
        sq_total = sq_total + sq_land[3 + other]
    vec_sum_ref[...] = vec_total
    grad_norm = jnp.sqrt(
        jnp.sum(sq_total, keepdims=True) + jnp.sum(vec_total * vec_total, keepdims=True)
    )
    norm_ref[...] = grad_norm
    done = []
    for piece in range(grains):
        gather(3, piece).wait()
        gather(4, piece).wait()
        done.append(pltpu.make_async_copy(assembled.at[piece], own_ref.at[piece], out_sem.at[piece]))
        done[-1].start()
    for swap in swaps:
        swap.end()
    for copy in done:
        copy.wait()


def tail(nz, owners, g_qkv, back, grad_vector, d_tokens):
    low, f32 = jnp.bfloat16, jnp.float32
    passages, span, _ = d_tokens.shape
    swapped = jax.ShapeDtypeStruct((4 * passages, span // 4, D), low)
    granules = g_qkv.shape[0] + back.shape[0]
    grains = granules // (2 * nz)
    any_spec = pl.BlockSpec(memory_space=pl.ANY)
    vmem = pl.BlockSpec(memory_space=pltpu.VMEM)
    dma = pltpu.SemaphoreType.DMA
    block = lambda *lead: pltpu.VMEM((*lead, GRAIN, D), low)
    lanes = (VEC_LEN // 128, 128)
    return pl.pallas_call(
        functools.partial(tail_kernel, nz),
        out_shape=(
            jax.ShapeDtypeStruct((grains, 2, 2, 2, GRAIN, D), low),
            jax.ShapeDtypeStruct(lanes, f32),
            jax.ShapeDtypeStruct((1, 1), f32),
            swapped,
        ),
        in_specs=[pl.BlockSpec(memory_space=pltpu.SMEM)]
        + [any_spec] * 2
        + [vmem, any_spec],
        out_specs=(any_spec, vmem, vmem, any_spec),
        scratch_shapes=PlaneSum.scratch(QKV_COUNTS, with_part=False)
        + [
            block(granules),
            block(2 * nz, grains),
            block(nz, grains, 2),
            block(nz, grains, 2),
            block(nz, grains, 2),
            block(nz, grains, 2),
            block(2, grains),
            block(grains, 2, 2, 2),
            pltpu.VMEM((4, *lanes), f32),
            pltpu.VMEM((3 + nz, *lanes), f32),
            pltpu.VMEM((4, 8, 128), f32),
            pltpu.VMEM((3 + nz, 8, 128), f32),
            dma(()),
            dma((2, nz * grains)),
            dma((2, nz * grains)),
            dma((2, 5 * grains)),
            dma((2, 2 + nz)),
            dma((2, 2 + nz)),
            dma((grains,)),
        ]
        + PositionSwap.scratch(passages, span),
        compiler_params=pltpu.CompilerParams(
            collective_id=1, has_side_effects=True, vmem_limit_bytes=60 * 1024 * 1024
        ),
        cost_estimate=pl.CostEstimate(flops=10**7, bytes_accessed=3 * 10**7, transcendentals=0),
        name="grad_tail",
    )(owners, g_qkv, back, grad_vector, d_tokens)


def keep_lanes(rows, half):
    lane = lax.broadcasted_iota(jnp.int32, rows.shape, 1)
    keep = lane < HEAD_DIM if half == 0 else lane >= HEAD_DIM
    return jnp.where(keep, rows, jnp.zeros_like(rows))


def norm_rows(mixed):
    row_mean = jnp.mean(mixed, axis=-1, keepdims=True)
    centred = mixed - row_mean
    inv_std = lax.rsqrt(jnp.mean(centred * centred, axis=-1, keepdims=True) + 1e-12)
    return centred * inv_std, inv_std


def project(x, w_ref, vec_ref, q_out, k_out, v_out, v_turned):
    f32, low = jnp.float32, jnp.bfloat16

    def product(lo):
        return jnp.dot(x, w_ref[lo : lo + D], preferred_element_type=f32)

    q_out[...] = ((product(0) + vec_ref[0:1]).astype(low).astype(f32) * 0.125).astype(low)
    k_out[...] = product(D).astype(low)
    values = product(2 * D) + vec_ref[1:2]
    v_out[...] = values.astype(low)
    v_turned[...] = values.T.astype(low)


def attend_pair(pair, length, q_ref, k_ref, v_turned, lse_ref, ctx_ref, ctx_turned, scores, weights):
    f32, low = jnp.float32, jnp.bfloat16
    span = q_ref.shape[0]
    width, strip = span // 2, 64
    lanes = pl.ds(pl.multiple_of(pair * 128, 128), 128)
    keys = k_ref[:, lanes]
    head_keys = [keep_lanes(keys, half) for half in range(2)]
    units = [(half, part) for half in range(2) for part in range(2)]

    def score(unit):
        half, part = units[unit]
        scores[unit % 2] = contract_cols(head_keys[half], q_ref[part * width : (part + 1) * width, lanes])

    def masked(unit, at):
        row = at + lax.broadcasted_iota(jnp.int32, (strip, width), 0)
        return jnp.where(row < length, scores[unit % 2, at : at + strip], -1000000000.0)

    def fold(value, op):
        return op(value.reshape(strip // 8, 8, width), axis=0)

    score(0)
    for unit, (half, part) in enumerate(units):
        if unit + 1 < len(units):
            score(unit + 1)
        cols = pl.ds(part * width, width)
        tops = fold(masked(unit, 0), jnp.max)
        for at in range(strip, span, strip):
            tops = jnp.maximum(tops, fold(masked(unit, at), jnp.max))
        peak = jnp.max(tops, axis=0, keepdims=True)
        sums = jnp.zeros((8, width), f32)
        for at in range(0, span, strip):
            weight = jnp.exp(masked(unit, at) - peak)
            sums = sums + fold(weight, jnp.sum)
            weights[unit % 2, at : at + strip] = weight.astype(low)
        total = jnp.sum(sums, axis=0, keepdims=True)
        lse_ref[2 * pair + half, :, cols] = peak + jnp.log(total)
        turned = v_turned[pl.ds(pl.multiple_of(pair * 128 + half * 64, 64), 64), :]
        out = jnp.dot(turned, weights[unit % 2], preferred_element_type=f32)
        ctx_turned[half * 64 : half * 64 + 64, cols] = out / total
    ctx_ref[:, lanes] = ctx_turned[...].T.astype(low)


def first_norm(x, ctx, w_ref, vec_ref, normed_ref, inv_ref):
    attn_out = jnp.dot(ctx, w_ref[3 * D : 4 * D], preferred_element_type=jnp.float32)
    normed, inv_std = norm_rows(x.astype(jnp.float32) + (attn_out + vec_ref[2:3]))
    normed_ref[...] = normed
    inv_ref[...] = jnp.broadcast_to(inv_std, inv_ref.shape)


def attend_kernel(
    lengths_ref,
    x_ref,
    w_ref,
    vec_ref,
    q_ref,
    k_ref,
    v_ref,
    lse_ref,
    ctx_ref,
    normed_ref,
    inv_ref,
    v_turned,
    ctx_turned,
    scores,
    weights,
):
    length = lengths_ref[lax.axis_index("blk") * pl.num_programs(0) + pl.program_id(0)]
    x = x_ref[0]
    project(x, w_ref, vec_ref, q_ref.at[0], k_ref.at[0], v_ref.at[0], v_turned)

    @pl.loop(0, HEADS // 2)
    def _(pair):
        attend_pair(
            pair,
            length,
            q_ref.at[0],
            k_ref.at[0],
            v_turned,
            lse_ref.at[0],
            ctx_ref.at[0],
            ctx_turned,
            scores,
            weights,
        )

    first_norm(x, ctx_ref[0], w_ref, vec_ref, normed_ref.at[0], inv_ref.at[0])


def attend(lengths, tokens, table, vec_rows):
    f32, low = jnp.float32, jnp.bfloat16
    passages, span, _ = tokens.shape
    rows = pl.BlockSpec((1, span, D), lambda p: (p, 0, 0))
    shape = lambda kind: jax.ShapeDtypeStruct((passages, span, D), kind)
    return pl.pallas_call(
        attend_kernel,
        grid=(passages,),
        out_shape=(
            shape(low),
            shape(low),
            shape(low),
            jax.ShapeDtypeStruct((passages, HEADS, 1, span), f32),
            shape(low),
            shape(f32),
            jax.ShapeDtypeStruct((passages, span, 128), f32),
        ),
        in_specs=[
            pl.BlockSpec(memory_space=pltpu.SMEM),
            rows,
            pl.BlockSpec((4 * D, D), lambda p: (0, 0)),
            pl.BlockSpec((VEC_LEN // D, D), lambda p: (0, 0)),
        ],
        out_specs=(
            rows,
            rows,
            rows,
            pl.BlockSpec((1, HEADS, 1, span), lambda p: (p, 0, 0, 0)),
            rows,
            rows,
            pl.BlockSpec((1, span, 128), lambda p: (p, 0, 0)),
        ),
        scratch_shapes=[
            pltpu.VMEM((D, span), low),
            pltpu.VMEM((128, span), f32),
            pltpu.VMEM((2, span, span // 2), f32),
            pltpu.VMEM((2, span, span // 2), low),
        ],
        compiler_params=pltpu.CompilerParams(vmem_limit_bytes=56 * 1024 * 1024),
        cost_estimate=pl.CostEstimate(
            flops=passages * span * (8 * D * D + 4 * D * span),
            bytes_accessed=passages * span * D * 20,
            transcendentals=passages * HEADS * span * span,
        ),
        name="attend",
    )(lengths, tokens, table, vec_rows)


def plane_chunks(counts):
    chunks, base = [], 0
    for source, count in enumerate(counts):
        half = count // 2
        step = half if half % 2 else 2
        for first in range(0, half, step):
            chunks.append((source, first, step, base + first, True))
            chunks.append((source, half + first, step, base + half + first, False))
        base += count
    return chunks


def plane_order(granules):
    half = granules // 2

    def order(turn):
        pair = turn // 2
        return lax.rem(pair, 2) * half + (pair // 2) * 2 + lax.rem(turn, 2)

    return order


def place_of():
    dp, blk = lax.axis_index("dp"), lax.axis_index("blk")
    z, c, y, x = dp // 2, dp % 2, blk // 2, blk % 2
    sibling = (blk, 2 * z + 1 - c)
    x_peer = (2 * y + 1 - x, dp)
    y_peer = (2 * (1 - y) + x, dp)
    return dp, blk, z, c, y, x, sibling, x_peer, y_peer


def remote_copy(src, dst, sems, slot, device):
    return pltpu.make_async_remote_copy(
        src_ref=src,
        dst_ref=dst,
        send_sem=sems.at[0, slot],
        recv_sem=sems.at[1, slot],
        device_id=device,
        device_id_type=MESH,
    )


class PlaneSum:
    def __init__(self, sources, counts, acc, core_land, one_land, two_land, part, sems, base=0):
        self.sources, self.acc, self.core_land = sources, acc, core_land
        self.one_land, self.two_land, self.part, self.base = one_land, two_land, part, base
        self.load_sem, self.core_sem, self.one_sem, self.two_sem = sems
        self.chunks = plane_chunks(counts)
        self.place = place_of()

    def load(self, slot):
        source, first, count, at, _ = self.chunks[slot]
        return pltpu.make_async_copy(
            self.sources[source].at[pl.ds(first, count), self.place[3]],
            self.acc.at[pl.ds(at, count)],
            self.load_sem.at[slot],
        )

    def core(self, slot):
        source, first, count, at, _ = self.chunks[slot]
        return remote_copy(
            self.sources[source].at[pl.ds(first, count), 1 - self.place[3]],
            self.core_land.at[pl.ds(at, count)],
            self.core_sem,
            slot,
            self.place[6],
        )

    def one(self, slot):
        _, _, count, at, x_first = self.chunks[slot]
        _, _, _, _, y, x, _, x_peer, y_peer = self.place
        rows = pl.ds(at, count)
        view = self.acc.at[rows, :, 1 - x] if x_first else self.acc.at[rows, 1 - y]
        return remote_copy(
            view, self.one_land.at[rows], self.one_sem, slot, x_peer if x_first else y_peer
        )

    def two(self, slot):
        _, _, count, at, x_first = self.chunks[slot]
        _, _, _, _, y, x, _, x_peer, y_peer = self.place
        rows = pl.ds(at, count)
        view = self.acc.at[rows, 1 - y, x] if x_first else self.acc.at[rows, y, 1 - x]
        return remote_copy(
            view, self.two_land.at[rows], self.two_sem, slot, y_peer if x_first else x_peer
        )

    def begin(self, slots):
        for slot in slots:
            self.load(slot).start()
            self.core(slot).start()

    def paired(self, slots):
        for slot in slots:
            self.load(slot).wait()
            self.core(slot).wait()
            _, _, count, at, _ = self.chunks[slot]

            @pl.loop(at, at + count)
            def _(g):
                self.acc[g] = add_low(self.acc[g], self.core_land[g])

            self.one(slot).start()

    def crossed(self, slots):
        _, _, _, _, y, x, _, _, _ = self.place
        for slot in slots:
            self.one(slot).wait()
            _, _, count, at, x_first = self.chunks[slot]

            @pl.loop(at, at + count)
            def _(g):
                for side in range(2):
                    if x_first:
                        self.acc[g, side, x] = add_low(self.acc[g, side, x], self.one_land[g, side])
                    else:
                        self.acc[g, y, side] = add_low(self.acc[g, y, side], self.one_land[g, side])

            self.two(slot).start()

    def half_settled(self, slots, red_ref, red_sem):
        _, _, _, _, y, x, _, _, _ = self.place
        for slot in slots:
            self.one(slot).wait()
            _, _, count, at, x_first = self.chunks[slot]

            @pl.loop(at, at + count)
            def _(g):
                for side in range(2):
                    if x_first:
                        self.acc[g, side, x] = add_low(self.acc[g, side, x], self.one_land[g, side])
                    else:
                        self.acc[g, y, side] = add_low(self.acc[g, y, side], self.one_land[g, side])

            self.kept(slot, red_ref, red_sem).start()

    def kept(self, slot, red_ref, red_sem):
        _, _, count, at, x_first = self.chunks[slot]
        _, _, _, _, y, x, _, _, _ = self.place
        rows = pl.ds(at, count)
        view = self.acc.at[rows, :, x] if x_first else self.acc.at[rows, y]
        return pltpu.make_async_copy(view, red_ref.at[rows], red_sem.at[slot])

    def settled(self, slots):
        _, _, _, _, y, x, _, _, _ = self.place
        for slot in slots:
            self.two(slot).wait()
            _, _, count, at, _ = self.chunks[slot]

            @pl.loop(at, at + count)
            def _(g):
                self.part[self.base + g] = add_low(self.acc[g, y, x], self.two_land[g])

    @staticmethod
    def scratch(counts, with_part=True):
        low, dma = jnp.bfloat16, pltpu.SemaphoreType.DMA
        total, slots = sum(counts), len(plane_chunks(counts))
        shapes = [
            pltpu.VMEM((total, 2, 2, GRAIN, D), low),
            pltpu.VMEM((total, 2, 2, GRAIN, D), low),
            pltpu.VMEM((total, 2, GRAIN, D), low),
            pltpu.VMEM((total, GRAIN, D), low),
            dma((slots,)),
            dma((2, slots)),
            dma((2, slots)),
            dma((2, slots)),
        ]
        return shapes + ([pltpu.VMEM((total, GRAIN, D), low)] if with_part else [])


class SecondStep:
    def __init__(self, red_ref, counts, keep, land, part, load_sem, two_sem, base):
        _, _, _, _, y, x, _, x_peer, y_peer = place_of()
        self.keep, self.land, self.part, self.base = keep, land, part, base
        self.chunks = plane_chunks(counts)
        self.loads, self.sends = [], []
        for slot, (_, _, count, at, x_first) in enumerate(self.chunks):
            rows = pl.ds(at, count)
            near, far, peer = (y, 1 - y, y_peer) if x_first else (x, 1 - x, x_peer)
            self.loads.append(
                pltpu.make_async_copy(red_ref.at[rows, near], keep.at[rows], load_sem.at[slot])
            )
            self.sends.append(
                remote_copy(red_ref.at[rows, far], land.at[rows], two_sem, slot, peer)
            )

    def begin(self):
        for copy in self.loads + self.sends:
            copy.start()

    def end(self):
        for slot, (_, _, count, at, _) in enumerate(self.chunks):
            self.loads[slot].wait()
            self.sends[slot].wait()

            @pl.loop(at, at + count)
            def _(g):
                self.part[self.base + g] = add_low(self.keep[g], self.land[g])

    @staticmethod
    def scratch(counts):
        low, dma = jnp.bfloat16, pltpu.SemaphoreType.DMA
        total, slots = sum(counts), len(plane_chunks(counts))
        block = pltpu.VMEM((total, GRAIN, D), low)
        return [block, block, dma((slots,)), dma((2, slots))]


def run_when(condition, task):
    @pl.when(condition)
    def _():
        task()


def greet(partners):
    barrier = pltpu.get_barrier_semaphore()
    for partner in partners:
        pl.semaphore_signal(barrier, inc=1, device_id=partner, device_id_type=MESH)
    return barrier


class PositionSwap:
    def __init__(self, rows_in, rows_out, keep, keep_sem, swap_sem):
        dp, blk, _, _, _, _, _, x_peer, y_peer = place_of()
        passages, span = rows_in.shape[0], rows_out.shape[1]
        self.diagonal = (3 - blk, dp)
        at = pl.ds(blk * passages, passages)
        self.first = pltpu.make_async_copy(
            rows_in.at[:, pl.ds(blk * span, span)], keep, keep_sem.at[0]
        )
        self.second = pltpu.make_async_copy(keep, rows_out.at[at], keep_sem.at[1])
        self.pushes = [
            remote_copy(
                rows_in.at[:, pl.ds(peer[0] * span, span)], rows_out.at[at], swap_sem, slot, peer
            )
            for slot, peer in enumerate((x_peer, y_peer, self.diagonal))
        ]

    def begin(self):
        for copy in [self.first] + self.pushes:
            copy.start()

    def passed(self):
        self.first.wait()
        self.second.start()

    def end(self):
        for copy in [self.second] + self.pushes:
            copy.wait()

    @staticmethod
    def scratch(passages, span):
        dma = pltpu.SemaphoreType.DMA
        return [pltpu.VMEM((passages, span // 4, D), jnp.bfloat16), dma((2,)), dma((2, 3))]


def attend_back_kernel(
    lengths_ref,
    x_ref,
    w_ref,
    q_ref,
    k_ref,
    v_ref,
    lse_ref,
    d_ctx_ref,
    d_mixed_ref,
    vec_in_ref,
    *refs,
):
    f32, low = jnp.float32, jnp.bfloat16
    beside = len(refs) > 9
    tasks = {}
    if beside:
        *sources, outer_red, refs = *refs[:3], refs[3:]
        red_ref, refs = refs[3], refs[:3] + refs[4:]
        extra, refs = refs[9:], refs[:9]
        acc, core_land, one_land, two_land, *sems, keep, land, keep_sem, keep_two, share, red_sem = extra
    grad_ref, table_ref, vec_ref, k_turned, dq_turned, dq_all, dk_all, dv_all, x_all = refs
    passage = pl.program_id(0)
    if beside:
        summed = PlaneSum(sources, BACK_COUNTS, acc, core_land, one_land, two_land, share, sems)
        second = SecondStep(
            outer_red, OUTER_COUNTS, keep, land, share, keep_sem, keep_two, sum(BACK_COUNTS)
        )
        slots = range(len(summed.chunks))

        @pl.when(passage == 0)
        def _():
            greet(summed.place[6:])

        def begin():
            pl.semaphore_wait(pltpu.get_barrier_semaphore(), 3)
            summed.begin(slots)
            second.begin()

        tasks = {
            0: begin,
            3: lambda: summed.paired(slots),
            5: second.end,
            9: lambda: summed.crossed(slots),
        }

        def end():
            summed.settled(slots)
            stored = pltpu.make_async_copy(share, red_ref, red_sem)
            stored.start()
            stored.wait()

    span = x_ref.shape[1]
    half_span = span // 2
    length = lengths_ref[lax.axis_index("blk") * pl.num_programs(0) + passage]
    rows = pl.ds(pl.multiple_of(passage * span, span), span)
    x_all[rows, :] = x_ref[0]
    k_turned[...] = k_ref[0].astype(f32).T.astype(low)
    valid = lax.broadcasted_iota(jnp.int32, (span, half_span), 0) < length

    @pl.loop(0, HEADS // 2)
    def _(pair):
        slot = passage * (HEADS // 2) + pair
        for at in sorted(tasks):
            run_when(slot == at, tasks[at])
        lanes = pl.ds(pl.multiple_of(pair * 128, 128), 128)
        keys, values = k_ref[0, :, lanes], v_ref[0, :, lanes]
        dk, dv = jnp.zeros((span, 128), f32), jnp.zeros((span, 128), f32)
        for half in range(2):
            head_keys, head_values = keep_lanes(keys, half), keep_lanes(values, half)
            turned = k_turned[pl.ds(pl.multiple_of(pair * 128 + half * 64, 64), 64), :]
            for part in range(2):
                cols = pl.ds(part * half_span, half_span)
                queries = q_ref[0, cols, lanes]
                d_out = d_ctx_ref[0, cols, lanes]
                scores = contract_cols(head_keys, queries)
                scores = jnp.where(valid, scores, -1000000000.0)
                probs = jnp.exp(scores - lse_ref[0, 2 * pair + half, :, cols])
                dv = dv + jnp.dot(
                    probs.astype(low), keep_lanes(d_out, half), preferred_element_type=f32
                )
                d_probs = contract_cols(head_values, d_out)
                weighted = probs * d_probs
                inner = jnp.sum(weighted, axis=0, keepdims=True)
                d_scores = (weighted - probs * inner).astype(low)
                dk = dk + jnp.dot(d_scores, keep_lanes(queries, half), preferred_element_type=f32)
                dq_turned[half * 64 : half * 64 + 64, cols] = (
                    jnp.dot(turned, d_scores, preferred_element_type=f32) * 0.125
                )
        dq_all[rows, lanes] = dq_turned[...].T.astype(low)
        dk_all[rows, lanes] = dk.astype(low)
        dv_all[rows, lanes] = dv.astype(low)

    grad = d_mixed_ref[0]
    for lo, part in ((0, dq_all), (D, dk_all), (2 * D, dv_all)):
        grad = grad + contract_cols(part[rows, :], w_ref[lo : lo + D])
    grad_ref[0] = grad.astype(low)

    @pl.when(passage == pl.num_programs(0) - 1)
    def _():
        for lo, part in ((0, dq_all), (D, dk_all), (2 * D, dv_all)):
            table_ref[lo : lo + D] = contract_rows(x_all[...], part[...]).astype(low)
        if beside:
            end()
        vec_ref[...] = vec_in_ref[...]
        vec_ref[0:1] = jnp.sum(dq_all[...].astype(f32), axis=0, keepdims=True)
        vec_ref[1:2] = jnp.sum(dv_all[...].astype(f32), axis=0, keepdims=True)


def attend_back(
    lengths, tokens, table, queries, keys, values, lse, d_ctx, d_mixed, vec_grad, sources=()
):
    f32, low = jnp.float32, jnp.bfloat16
    passages, span, _ = tokens.shape
    rows = pl.BlockSpec((1, span, D), lambda p: (p, 0, 0))
    whole = pltpu.VMEM((passages * span, D), low)
    any_spec = pl.BlockSpec(memory_space=pl.ANY)
    red_shape, beside, extra, more = (), [], {}, ()
    if sources:
        total = sum(BACK_COUNTS) + sum(OUTER_COUNTS)
        red_shape = (jax.ShapeDtypeStruct((total, GRAIN, D), low),)
        beside = PlaneSum.scratch(BACK_COUNTS, with_part=False) + SecondStep.scratch(OUTER_COUNTS)
        beside += [pltpu.VMEM((total, GRAIN, D), low), pltpu.SemaphoreType.DMA]
        extra = dict(collective_id=3, has_side_effects=True)
        more = sources
    return pl.pallas_call(
        attend_back_kernel,
        grid=(passages,),
        out_shape=(
            jax.ShapeDtypeStruct((passages, span, D), low),
            jax.ShapeDtypeStruct((3 * D, D), low),
            jax.ShapeDtypeStruct((VEC_LEN // D, D), f32),
        )
        + red_shape,
        in_specs=[
            pl.BlockSpec(memory_space=pltpu.SMEM),
            rows,
            pl.BlockSpec((3 * D, D), lambda p: (0, 0)),
            rows,
            rows,
            rows,
            pl.BlockSpec((1, HEADS, 1, span), lambda p: (p, 0, 0, 0)),
            rows,
            rows,
            pl.BlockSpec((VEC_LEN // D, D), lambda p: (0, 0)),
        ]
        + [any_spec] * len(more),
        out_specs=(
            rows,
            pl.BlockSpec((3 * D, D), lambda p: (0, 0)),
            pl.BlockSpec((VEC_LEN // D, D), lambda p: (0, 0)),
        )
        + (any_spec,) * len(red_shape),
        scratch_shapes=[pltpu.VMEM((D, span), low), pltpu.VMEM((128, span), f32)]
        + [whole] * 4
        + beside,
        compiler_params=pltpu.CompilerParams(vmem_limit_bytes=60 * 1024 * 1024, **extra),
        cost_estimate=pl.CostEstimate(
            flops=passages * span * (12 * D * D + 10 * D * span),
            bytes_accessed=passages * span * D * 24,
            transcendentals=passages * HEADS * span * span,
        ),
        name="attend_back",
    )(lengths, tokens, table, queries, keys, values, lse, d_ctx, d_mixed, vec_grad, *more)


ERFC_SLOPE = 0.42
ERFC_TERMS = (
    0.23681282137224371,
    0.23975548803522717,
    0.19369618325685073,
    0.27205881038432234,
    -0.136659548208163,
    0.44720921707821076,
    -0.32398587364624676,
    0.07111276080879629,
)


def gelu_pair(x):
    slope = 1.0 + (ERFC_SLOPE * math.sqrt(0.5)) * jnp.abs(x)
    t = pltpu.reciprocal(slope, approx=True)
    t = t * (2.0 - slope * t)
    bell = jnp.exp2(x * x * (-0.5 / math.log(2.0)))
    series = 0.5 * ERFC_TERMS[-1]
    for term in ERFC_TERMS[-2::-1]:
        series = series * t + 0.5 * term
    low_side = series * t * bell
    cdf = jnp.where(x < 0.0, low_side, 1.0 - low_side)
    return x * cdf, cdf + x * bell * (1.0 / math.sqrt(2.0 * math.pi))


def ffn_kernel(
    lengths_ref,
    vec_ref,
    normed_ref,
    inv_ref,
    cot_ref,
    ctx_ref,
    table_ref,
    output_ref,
    d_mixed_ref,
    d_ctx_ref,
    vec_grad_ref,
    d_out_ref,
    d_inner_ref,
    d_outer_ref,
    *refs,
):
    beside = len(refs) > 20
    if beside:
        red_ref, refs = refs[0], refs[1:]
    (
        w_out,
        w_inner,
        w_outer,
        normed,
        inv_std,
        cot,
        left_pre,
        right_pre,
        slope,
        active,
        hidden,
        output,
        d_branch,
        d_mixed,
        staged,
        staged_outer,
        load_sem,
        store_sem,
        done_sem,
        wide_sem,
        *extra,
    ) = refs
    f32, low = jnp.float32, jnp.bfloat16
    count = normed.shape[0]
    chunk = left_pre.shape[1]
    chunks = FF // chunk
    tile, strip = 256, 32
    tiles = count // tile
    sources = (
        (normed_ref, normed),
        (table_ref.at[pl.ds(4 * D + FF, FF)], w_outer),
        (cot_ref, cot),
        (inv_ref, inv_std),
        (table_ref.at[pl.ds(3 * D, D)], w_out),
        (ctx_ref, hidden),
    )
    loads = [
        pltpu.make_async_copy(src, dst, load_sem.at[slot])
        for slot, (src, dst) in enumerate(sources)
    ]
    loads[0].start()

    def columns(part):
        return pl.ds(pl.multiple_of(part * chunk, chunk), chunk)

    def load_wide(part):
        rows = pl.ds(4 * D + part * chunk, chunk)
        return pltpu.make_async_copy(
            table_ref.at[rows], w_inner.at[columns(part)], wide_sem.at[part]
        )

    for part in range(chunks):
        load_wide(part).start()
    for load in loads[1:5]:
        load.start()

    if beside:
        acc, core_land, one_land, two_land, *sems, red_sem, swap_sem = extra
        summed = PlaneSum((d_outer_ref,), OUTER_COUNTS, acc, core_land, one_land, None, None, sems)
        dp, blk = summed.place[:2]
        diagonal = (3 - blk, dp)
        greet((*summed.place[6:], diagonal))

    def vec(row):
        return vec_ref[row : row + 1]

    vec_grad_ref[...] = jnp.zeros_like(vec_grad_ref)
    loads[0].wait()

    @pl.loop(0, count // strip)
    def _(at):
        rows = pl.ds(pl.multiple_of(at * strip, strip), strip)
        hidden[rows, :] = (normed[rows, :] * vec(8) + vec(9)).astype(low)

    def widen(part, pre):
        load_wide(part).wait()
        pre[...] = contract_cols(hidden[...], w_inner[columns(part), :])

    per_row = D // chunk

    def bend(part, pre):
        bias = vec_ref[pl.ds(3 + part // per_row, 1), :]
        side = lax.rem(part, per_row)
        piece = bias[:, 0:chunk]
        for other in range(1, per_row):
            piece = jnp.where(side == other, bias[:, other * chunk : (other + 1) * chunk], piece)
        for at in range(0, count, strip):
            value, pull = gelu_pair(pre[at : at + strip] + piece)
            active[at : at + strip, columns(part)] = value.astype(low)
            slope[at : at + strip, columns(part)] = pull

    widen(0, left_pre)

    @pl.loop(0, chunks // 2 - 1)
    def _(turn):
        widen(2 * turn + 1, right_pre)
        bend(2 * turn, left_pre)
        widen(2 * turn + 2, left_pre)
        bend(2 * turn + 1, right_pre)

    widen(chunks - 1, right_pre)
    bend(chunks - 2, left_pre)
    bend(chunks - 1, right_pre)

    for load in loads[1:4]:
        load.wait()
    passages = lengths_ref.shape[0] // lax.axis_size("blk")
    per_passage = count // passages

    def put_tile(at, value):
        rows = slice(at % 2 * tile, (at % 2 + 1) * tile)
        left_pre[rows] = value[:, 0:chunk]
        right_pre[rows] = value[:, chunk:]

    def get_strip(at, inner_at):
        first = at % 2 * tile + inner_at
        rows = slice(first, first + strip)
        return jnp.concatenate([left_pre[rows], right_pre[rows]], axis=1)

    def narrow(at):
        return jnp.dot(active[at * tile : (at + 1) * tile], w_outer[...], preferred_element_type=f32)

    def sums(totals, values):
        return [
            total + jnp.sum(value, axis=0, keepdims=True) for total, value in zip(totals, values)
        ]

    nothing = [jnp.zeros((1, D), f32)] * 3
    totals = nothing
    for at in range(tiles):
        put_tile(at, narrow(at))
        passage = at * tile // per_passage
        length = lengths_ref[lax.axis_index("blk") * passages + passage]
        for inner_at in range(0, tile, strip):
            first = at * tile + inner_at
            rows = slice(first, first + strip)
            mixed = normed[rows] * vec(8) + vec(9) + (
                get_strip(at, inner_at) + vec(7)
            )
            normed_two, inv_two = norm_rows(mixed)
            local = first - passage * per_passage
            output[passage, local : local + strip] = (normed_two * vec(10) + vec(11)).astype(low)
            position = local + lax.broadcasted_iota(
                jnp.int32, (strip, 1), 0
            )
            grad_out = jnp.where(position < length, cot[rows].astype(f32), 0.0)
            d_mixed_two = norm_back(grad_out * vec(10), normed_two, inv_two)
            d_mixed[rows] = d_mixed_two
            low_branch = d_mixed_two.astype(low)
            d_branch[rows] = low_branch
            totals = sums(totals, (grad_out * normed_two, grad_out, low_branch.astype(f32)))
    for row, total in zip((10, 11, 7), totals):
        vec_grad_ref[row : row + 1] = total
    if beside:
        blk = lax.axis_index("blk")
        pl.semaphore_wait(pltpu.get_barrier_semaphore(), 4)
        span = output_ref.shape[1]
        there = output_ref.at[pl.ds(blk * passages, passages)]
        given = [
            remote_copy(output.at[:, pl.ds(peer[0] * span, span)], there, swap_sem, slot, peer)
            for slot, peer in enumerate((*summed.place[7:], diagonal))
        ]
        own_piece = output.at[:, pl.ds(blk * span, span)]
        given.append(pltpu.make_async_copy(own_piece, there, done_sem.at[0]))
    else:
        given = [pltpu.make_async_copy(output, output_ref, done_sem.at[0])]
    for copy in given:
        copy.start()

    order = plane_order(chunks)

    def store(turn, side):
        part, slot = order(turn), lax.rem(turn, 2)
        if side == 0:
            return pltpu.make_async_copy(
                staged_outer.at[slot], d_outer_ref.at[part], store_sem.at[slot, 0]
            )
        rows = pl.ds(part * chunk, chunk)
        return pltpu.make_async_copy(staged.at[slot], d_inner_ref.at[rows], store_sem.at[slot, 1])

    tasks = {}
    if beside:

        tasks = {
            2: lambda: summed.begin([0]),
            4: lambda: (summed.paired([0]), summed.begin([1])),
            6: lambda: (summed.paired([1]), summed.begin([2])),
        }

    @pl.loop(0, chunks)
    def _(turn):
        part, slot = order(turn), lax.rem(turn, 2)
        cols = columns(part)
        left_pre[...] = contract_cols(d_branch[...], w_outer[cols, :])
        outer_rows = contract_rows(active[:, cols], d_branch[...]).astype(low)
        staged_outer[slot] = outer_rows.reshape(staged_outer.shape[1:])
        total = jnp.zeros((1, chunk), f32)
        for at in range(0, count, strip):
            d_pre = (left_pre[at : at + strip] * slope[at : at + strip, cols]).astype(low)
            active[at : at + strip, cols] = d_pre
            total = total + jnp.sum(d_pre.astype(f32), axis=0, keepdims=True)
        bias_row = pl.ds(3 + part // per_row, 1)
        side_at = lax.rem(part, per_row)
        for other in range(per_row):
            lanes = slice(other * chunk, (other + 1) * chunk)
            vec_grad_ref[bias_row, lanes] += jnp.where(side_at == other, total, 0.0)
        staged[slot] = contract_rows(active[:, cols], hidden[...]).astype(low)
        for side in range(2):
            store(turn, side).start()

        @pl.when(turn >= 1)
        def _():
            for side in range(2):
                store(turn - 1, side).wait()

        for at in sorted(tasks):
            run_when(turn == at, tasks[at])

    for side in range(2):
        store(chunks - 1, side).wait()
    if beside:
        summed.begin([3])
        summed.paired([2])
    loads[5].start()
    loads[4].wait()
    ctx, d_attn, d_ctx = hidden, d_branch, cot
    totals = nothing
    for at in range(tiles):
        span = slice(at * tile, (at + 1) * tile)
        put_tile(at, jnp.dot(active[span], w_inner[...], preferred_element_type=f32))
        for inner_at in range(0, tile, strip):
            first = at * tile + inner_at
            rows = slice(first, first + strip)
            d_hidden = d_mixed[rows] + get_strip(at, inner_at)
            normed_one = normed[rows]
            d_mixed_one = norm_back(d_hidden * vec(8), normed_one, inv_std[rows, 0:1])
            d_mixed[rows] = d_mixed_one
            low_attn = d_mixed_one.astype(low)
            d_attn[rows] = low_attn
            totals = sums(totals, (d_hidden * normed_one, d_hidden, low_attn.astype(f32)))
        d_ctx[span] = contract_cols(d_attn[span], w_out[...]).astype(low)
        if beside and at == 0:
            summed.paired([3])
        if beside and at == 2:
            summed.half_settled([0, 1], red_ref, red_sem)
    for row, total in zip((8, 9, 2), totals):
        vec_grad_ref[row : row + 1] = total
    results = [
        pltpu.make_async_copy(d_ctx, d_ctx_ref, done_sem.at[1]),
        pltpu.make_async_copy(d_mixed, d_mixed_ref, done_sem.at[2]),
    ]
    for copy in results:
        copy.start()
    half = staged.shape[1]
    loads[5].wait()
    for side in range(2):
        rows = slice(side * half, (side + 1) * half)
        staged[side] = contract_rows(ctx[:, rows], d_attn[...]).astype(low)
        copy = pltpu.make_async_copy(staged.at[side], d_out_ref.at[rows], done_sem.at[3 + side])
        copy.start()
        results.append(copy)
    if beside:
        summed.half_settled([2, 3], red_ref, red_sem)
        results += [summed.kept(slot, red_ref, red_sem) for slot in range(4)]
    for copy in given + results:
        copy.wait()


def ffn(lengths, normed, inv_std, cotangent, context, vec_rows, table, passages, beside):
    f32, low = jnp.float32, jnp.bfloat16
    count = normed.shape[0]
    shares = (4 * passages, count // passages // 4) if beside else (passages, count // passages)
    chunk = 8 * GRAIN
    any_spec = pl.BlockSpec(memory_space=pl.ANY)
    vmem = pl.BlockSpec(memory_space=pltpu.VMEM)
    dma = pltpu.SemaphoreType.DMA
    whole = lambda width, kind=low: pltpu.VMEM((count, width), kind)
    granules = FF // chunk
    more_shape, more, extra = (), [], {}
    if beside:
        more_shape = (jax.ShapeDtypeStruct((granules, 2, GRAIN, D), low),)
        more = PlaneSum.scratch(OUTER_COUNTS, with_part=False)
        more[3] = pltpu.VMEM((1, GRAIN, D), low)
        more += [dma((4,)), dma((2, 3))]
        extra = dict(collective_id=4, has_side_effects=True)
    return pl.pallas_call(
        ffn_kernel,
        out_shape=(
            jax.ShapeDtypeStruct((*shares, D), low),
            jax.ShapeDtypeStruct((count, D), f32),
            jax.ShapeDtypeStruct((count, D), low),
            jax.ShapeDtypeStruct((VEC_LEN // D, D), f32),
            jax.ShapeDtypeStruct((D, D), low),
            jax.ShapeDtypeStruct((FF, D), low),
            jax.ShapeDtypeStruct((granules, 2, 2, 2, GRAIN, D), low),
        )
        + more_shape,
        in_specs=[pl.BlockSpec(memory_space=pltpu.SMEM), vmem] + [any_spec] * 5,
        out_specs=(any_spec, any_spec, any_spec, vmem)
        + (any_spec,) * (3 + len(more_shape)),
        scratch_shapes=[
            pltpu.VMEM((D, D), low),
            pltpu.VMEM((FF, D), low),
            pltpu.VMEM((FF, D), low),
            whole(D, f32),
            whole(128, f32),
            whole(D),
            whole(chunk, f32),
            whole(chunk, f32),
            whole(FF, f32),
            whole(FF),
            whole(D),
            pltpu.VMEM((passages, count // passages, D), low),
            whole(D),
            whole(D, f32),
            pltpu.VMEM((2, chunk, D), low),
            pltpu.VMEM((2, 2, 2, 2, GRAIN, D), low),
            dma((6,)),
            dma((2, 2)),
            dma((5,)),
            dma((granules,)),
        ]
        + more,
        compiler_params=pltpu.CompilerParams(vmem_limit_bytes=63 * 1024 * 1024, **extra),
        cost_estimate=pl.CostEstimate(
            flops=count * (12 * D * FF + 4 * D * D),
            bytes_accessed=2 * (14 * D * D + 14 * D * count),
            transcendentals=count * FF,
        ),
        name="ffn",
    )(lengths, vec_rows, normed, inv_std, cotangent, context, table)


def paired(own_rows, dp_count, blk_count):
    return blk_count == 4 and dp_count % 2 == 0 and own_rows % 384 == 0


def swap_in(rows):
    return lax.all_to_all(rows, "blk", split_axis=0, concat_axis=1, tiled=True)


def swap_out(rows):
    return lax.all_to_all(rows, "blk", split_axis=1, concat_axis=0, tiled=True)


def pick_blocks(blocks, order):
    return jnp.concatenate(
        [lax.dynamic_index_in_dim(blocks, order[i], 0) for i in range(blocks.shape[0])], axis=0
    )


def body(
    tokens,
    cotangent,
    lengths,
    owners,
    master,
    moment_one,
    moment_two,
    vectors,
    vector_one,
    vector_two,
):
    dp_count = lax.axis_size("dp")
    blk_count = lax.axis_size("blk")
    blk = lax.axis_index("blk")
    own_rows = master.shape[0]
    grain = math.gcd(own_rows, D)
    part = grain // blk_count
    own_grains = own_rows // grain
    fast = paired(own_rows, dp_count, blk_count)
    if fast:
        full = own_rows * 2 // 9
        tokens, cotangent, table, *attended, vec_rows = enter(
            dp_count // 2, full, owners, tokens, cotangent, master, lengths, vectors
        )
    else:
        own_part = lax.dynamic_index_in_dim(
            master.reshape(own_grains, blk_count, part, D), blk, 1, keepdims=False
        ).astype(jnp.bfloat16)
        part_blocks = lax.all_gather(own_part, "dp", axis=0)
        part_table = pick_blocks(part_blocks, jnp.argsort(owners)).reshape(dp_count * own_grains, part, D)
        tokens = swap_in(tokens)
        cotangent = swap_in(cotangent)

        rows = lax.all_gather(part_table, "blk", axis=1)
        table = rows.reshape(-1, D)
        vec_rows = vectors.reshape(-1, D)
        attended = attend(lengths, tokens, table, vec_rows)
    queries, keys, values, log_total, context, normed_one, inv_one = attended
    passages, span_len, _ = tokens.shape
    tok_rows = passages * span_len
    flat = lambda rows: rows.reshape(tok_rows, -1)
    output, d_mixed_one, d_context, grad_vector, d_w_out, d_w_inner, d_w_outer, *outer_red = ffn(
        lengths,
        flat(normed_one),
        flat(inv_one),
        flat(cotangent),
        flat(context),
        vec_rows,
        table,
        passages,
        fast,
    )
    split = lambda g: g.reshape(-1, 2, 2, 2, GRAIN, D)
    d_tokens, d_w_qkv, grad_vector, *back = attend_back(
        lengths,
        tokens,
        table,
        queries,
        keys,
        values,
        log_total,
        d_context.reshape(passages, span_len, D),
        d_mixed_one.reshape(passages, span_len, D),
        grad_vector,
        [split(d_w_out), split(d_w_inner), *outer_red] if fast else (),
    )

    def own_parts(rows):
        split = rows.astype(jnp.bfloat16).reshape(-1, blk_count, part, D)
        return lax.psum_scatter(split, "blk", scatter_dimension=1)

    if fast:
        own_block, vector_sum, norms, grad_tokens = tail(
            dp_count // 2, owners, split(d_w_qkv), back[0], grad_vector, d_tokens
        )
        grad_norm = norms[0, 0]
        vector_sum = vector_sum.reshape(-1)
        own_block = own_block.reshape(own_rows, D)
    else:
        output, grad_tokens = swap_out(output), swap_out(d_tokens)
        part_grads = jnp.concatenate(
            [own_parts(d_w_qkv), own_parts(d_w_out), own_parts(d_w_inner), own_parts(d_w_outer.reshape(FF, D))],
            axis=0,
        )
        ordered = pick_blocks(part_grads.reshape(dp_count, own_grains, part, D), owners)
        own_grad = lax.psum_scatter(ordered, "dp", scatter_dimension=0)
        own_f32 = own_grad.astype(jnp.float32)
        own_block = lax.all_gather(own_grad, "blk", axis=1).reshape(own_rows, D)
        vector_sum = lax.psum(grad_vector, ("dp", "blk"))
        squares = lax.psum(jnp.sum(own_f32 * own_f32), ("dp", "blk"))
        vector_sum = vector_sum.reshape(-1)
        grad_norm = jnp.sqrt(squares + jnp.sum(vector_sum * vector_sum))
    factor = jnp.minimum(1.0, clip_norm / (grad_norm + 1e-06))
    own_grad = own_block.astype(jnp.float32) * factor
    new_vectors, new_vone, new_vtwo = adamw(
        vectors, vector_one, vector_two, vector_sum * factor, 0.0, vector_rate
    )
    new_master, new_one, new_two = adamw(
        master, moment_one, moment_two, own_grad, weight_decay, learn_rate
    )
    return (
        output,
        grad_tokens,
        grad_norm,
        new_master,
        new_one,
        new_two,
        new_vectors,
        new_vone,
        new_vtwo,
    )


def solution(mesh):
    in_specs = (
        P("dp", "blk", None),
        P("dp", "blk", None),
        P("dp"),
        P(),
        P("dp", None),
        P("dp", None),
        P("dp", None),
        P(),
        P(),
        P(),
    )
    out_specs = (
        P("dp", "blk", None),
        P("dp", "blk", None),
        P(),
        P("dp", None),
        P("dp", None),
        P("dp", None),
        P(),
        P(),
        P(),
    )
    return jax.shard_map(body, mesh=mesh, in_specs=in_specs, out_specs=out_specs, check_vma=False)
```

```python
import functools
import math

import jax
import jax.numpy as jnp
from jax import lax
from jax.experimental import pallas as pl
from jax.experimental.pallas import tpu as pltpu
from jax.sharding import PartitionSpec as P

D = 768
HEADS = 12
HEAD_DIM = 64
FF = 3072
STEP = 10
VEC_LEN = 8 * D + FF


beta_one = 0.5
beta_two = 0.5
learn_rate = 0.05
vector_rate = 0.3
weight_decay = 0.01
adam_eps = 1e-08
clip_norm = 1.0


def norm_back(d_normed, normed, inv_std):
    first_mean = jnp.mean(d_normed, axis=-1, keepdims=True)
    second_mean = jnp.mean(d_normed * normed, axis=-1, keepdims=True)
    return inv_std * (d_normed - first_mean - normed * second_mean)


def contract_rows(left, right):
    return lax.dot_general(
        left, right, (((0,), (0,)), ((), ())), preferred_element_type=jnp.float32
    )


def contract_cols(left, right):
    return lax.dot_general(
        left, right, (((1,), (1,)), ((), ())), preferred_element_type=jnp.float32
    )


def adamw(weight, first, second, grad, decay, rate):
    new_first = beta_one * first + (1.0 - beta_one) * grad
    new_second = beta_two * second + (1.0 - beta_two) * grad * grad
    direction = (
        new_first
        / (1.0 - beta_one**STEP)
        / (jnp.sqrt(new_second / (1.0 - beta_two**STEP)) + adam_eps)
    )
    return (weight - rate * (direction + decay * weight), new_first, new_second)


MESH = pl.DeviceIdType.MESH
GRAIN = 48
OUTER_COUNTS = (8,)
BACK_COUNTS = (2, 8)
QKV_COUNTS = (6,)


def add_low(left, right):
    return (left.astype(jnp.float32) + right.astype(jnp.float32)).astype(jnp.bfloat16)


def enter_kernel(
    nz,
    full,
    owners_ref,
    tokens_ref,
    cot_ref,
    master_ref,
    lengths_ref,
    lanes_ref,
    tokens_out,
    cot_out,
    table_out,
    q_out,
    k_out,
    v_out,
    lse_out,
    ctx_out,
    normed_out,
    inv_out,
    vec_ref,
    wide,
    own_wide,
    tokens_land,
    cot_land,
    whole_out,
    quarter_out,
    ordered,
    load_sem,
    swap_sem,
    keep_sem,
    z_sem,
    one_sem,
    two_sem,
    sib_sem,
    sib_own_sem,
    out_sem,
    q_all,
    k_all,
    v_all,
    v_turned,
    lse_all,
    ctx_all,
    normed_all,
    inv_all,
    ctx_turned,
    scores,
    weights,
    work_sem,
):
    dp, blk, z, c, y, x, sibling, x_peer, y_peer = place_of()
    diagonal = (3 - blk, dp)
    passages, span = tokens_out.shape[0], tokens_ref.shape[1]
    quarter = quarter_out.shape[4]
    low_whole, low_quarter = whole_out.at[dp], quarter_out.at[dp]

    own_rows = pl.ds(pl.multiple_of(full + blk * 2 * quarter, 16), 2 * quarter)
    loads = [
        pltpu.make_async_copy(master_ref.at[own_rows], own_wide, load_sem.at[0]),
        pltpu.make_async_copy(master_ref, wide, load_sem.at[1]),
    ]
    for load in loads:
        load.start()
    own_copies = []
    for slot, (rows_in, rows_out) in enumerate(((tokens_ref, tokens_land), (cot_ref, cot_land))):
        own_copies.append(
            pltpu.make_async_copy(
                rows_in.at[pl.ds(blk * passages, passages)],
                rows_out.at[:, pl.ds(blk * span, span)],
                keep_sem.at[slot],
            )
        )
        own_copies[-1].start()

    for row in range(VEC_LEN // D):
        for col in range(D // 128):
            at = row * (D // 128) + col
            vec_ref[row : row + 1, col * 128 : (col + 1) * 128] = lanes_ref[at : at + 1]

    barrier = pltpu.get_barrier_semaphore()
    for partner in (sibling, x_peer, y_peer, diagonal):
        pl.semaphore_signal(barrier, inc=1, device_id=partner, device_id_type=MESH)
    below, above = z > 0, z < nz - 1

    @pl.when(below)
    def _():
        pl.semaphore_signal(barrier, inc=1, device_id=(blk, dp - 2), device_id_type=MESH)

    @pl.when(above)
    def _():
        pl.semaphore_signal(barrier, inc=1, device_id=(blk, dp + 2), device_id_type=MESH)

    pl.semaphore_wait(barrier, 4 + jnp.where(below, 1, 0) + jnp.where(above, 1, 0))

    def remote(src, dst, sems, slot, device):
        return pltpu.make_async_remote_copy(
            src_ref=src,
            dst_ref=dst,
            send_sem=sems.at[(0, *slot)],
            recv_sem=sems.at[(1, *slot)],
            device_id=device,
            device_id_type=MESH,
        )

    def swap(which, rows_in, rows_out, peer, slot):
        return remote(
            rows_in.at[pl.ds(peer[0] * passages, passages)],
            rows_out.at[:, pl.ds(blk * span, span)],
            swap_sem,
            (which, slot),
            peer,
        )

    swaps = [
        swap(which, rows_in, rows_out, peer, slot)
        for which, (rows_in, rows_out) in enumerate(((tokens_ref, tokens_land), (cot_ref, cot_land)))
        for slot, peer in enumerate((x_peer, y_peer, diagonal))
    ]
    loads[0].wait()
    for half in range(2):
        quarter_out[dp, y, x, half] = own_wide[half * quarter : (half + 1) * quarter].astype(
            jnp.bfloat16
        )

    def pass_on(src_quarter, src_whole, at, upward, which):
        device = (blk, dp + 2 if upward else dp - 2)
        way = 0 if upward else 1
        if which == 0:
            return remote(src_quarter, quarter_out.at[at, y, x], z_sem, (way, 0, at // 2), device)
        return remote(src_whole, whole_out.at[at], z_sem, (way, 1, at // 2), device)

    @pl.when(above)
    def _():
        pass_on(low_quarter.at[y, x], None, dp, True, 0).start()

    @pl.when(below)
    def _():
        pass_on(low_quarter.at[y, x], None, dp, False, 0).start()

    for copy in swaps[:3]:
        copy.start()
    loads[1].wait()
    whole_out[dp] = wide[0:full].astype(jnp.bfloat16)
    for part in range(8):

        @pl.when(blk != part // 2)
        def _(part=part):
            start = full + part * quarter
            quarter_out[dp, part // 4, part // 2 % 2, part % 2] = wide[
                start : start + quarter
            ].astype(jnp.bfloat16)

    def own_whole(turn):
        @pl.when(jnp.logical_and(above, z + 1 == turn))
        def _():
            pass_on(None, low_whole, dp, True, 1).start()

        @pl.when(jnp.logical_and(below, nz - z == turn))
        def _():
            pass_on(None, low_whole, dp, False, 1).start()

    sib_own = [
        remote(low_quarter, quarter_out.at[dp], sib_own_sem, (0,), sibling),
        remote(low_whole, whole_out.at[dp], sib_own_sem, (1,), sibling),
    ]
    for copy in sib_own:
        copy.start()
    def sources(act):
        def at_distance(distance):
            @pl.when(z >= distance)
            def _():
                act(dp - 2 * distance, True, z < nz - 1)

            @pl.when(z + distance < nz)
            def _():
                act(dp + 2 * distance, False, z > 0)

        return at_distance

    def forward(ref_view, at, slot):
        return remote(ref_view, ref_view, sib_sem, (slot, at // 2), sibling)

    def one_x(at):
        view = quarter_out.at[at, y, x, 0]
        return remote(view, view, one_sem, (0, at // 2), x_peer)

    def one_y(at):
        view = quarter_out.at[at, y, x, 1]
        return remote(view, view, one_sem, (1, at // 2), y_peer)

    def two_y(at):
        view = quarter_out.at[at, y, :, 0]
        return remote(view, view, two_sem, (0, at // 2), y_peer)

    def two_x(at):
        view = quarter_out.at[at, :, x, 1]
        return remote(view, view, two_sem, (1, at // 2), x_peer)

    def sib_views(at):
        return [
            quarter_out.at[at, y, x],
            quarter_out.at[at, y, 1 - x, 0],
            quarter_out.at[at, 1 - y, x, 1],
            quarter_out.at[at, 1 - y, :, 0],
            quarter_out.at[at, :, 1 - x, 1],
            whole_out.at[at],
        ]

    def quarter_came(at, upward, onward):
        view = quarter_out.at[at, y, x]
        pass_on(view, None, at, upward, 0).wait_recv()

        @pl.when(onward)
        def _():
            pass_on(view, None, at, upward, 0).start()

        one_x(at).start()
        one_y(at).start()
        forward(sib_views(at)[0], at, 0).start()

    def whole_came(at, upward, onward):
        view = whole_out.at[at]
        pass_on(None, view, at, upward, 1).wait_recv()

        @pl.when(onward)
        def _():
            pass_on(None, view, at, upward, 1).start()

        forward(sib_views(at)[5], at, 5).start()

    def one_came(at, upward, onward):
        one_x(at).wait_recv()
        two_y(at).start()
        forward(sib_views(at)[1], at, 1).start()
        one_y(at).wait_recv()
        two_x(at).start()
        forward(sib_views(at)[2], at, 2).start()

    def two_came(at, upward, onward):
        two_y(at).wait_recv()
        forward(sib_views(at)[3], at, 3).start()
        two_x(at).wait_recv()
        forward(sib_views(at)[4], at, 4).start()

    def finished(at, upward, onward):
        view = quarter_out.at[at, y, x]

        @pl.when(onward)
        def _():
            pass_on(view, None, at, upward, 0).wait_send()
            pass_on(None, whole_out.at[at], at, upward, 1).wait_send()

        one_x(at).wait_send()
        one_y(at).wait_send()
        two_x(at).wait_send()
        two_y(at).wait_send()
        for slot, ref_view in enumerate(sib_views(at)):
            copy = forward(ref_view, at, slot)
            copy.wait_send()
            copy.wait_recv()

    for distance in range(1, nz):
        sources(quarter_came)(distance)
        if distance == nz - 1:
            sources(one_came)(1)
        own_whole(distance)
    plan = [(whole_came, 1)] + [(one_came, d) for d in range(2, nz)]
    for distance in range(2, nz):
        plan += [(whole_came, distance), (two_came, distance - 1)]
    plan += [(two_came, nz - 1)]
    for act, distance in plan:
        sources(act)(distance)
    for distance in range(1, nz):
        sources(finished)(distance)

    @pl.when(above)
    def _():
        pass_on(low_quarter.at[y, x], None, dp, True, 0).wait_send()
        pass_on(None, low_whole, dp, True, 1).wait_send()

    @pl.when(below)
    def _():
        pass_on(low_quarter.at[y, x], None, dp, False, 0).wait_send()
        pass_on(None, low_whole, dp, False, 1).wait_send()

    for copy in swaps[3:]:
        copy.start()
    for copy in own_copies[:1] + swaps[:3] + sib_own:
        copy.wait()
    stores = [pltpu.make_async_copy(tokens_land, tokens_out, out_sem.at[2 * nz])]
    stores[0].start()

    def put(block):
        place = 0
        for index in range(2 * nz):
            place = jnp.where(owners_ref[index] == block, index, place)
        rows = wide.shape[0]
        base = block * rows
        ordered[base : base + full] = whole_out[place]
        for part in range(8):
            start = base + full + part * quarter
            ordered[start : start + quarter] = quarter_out[
                place, part // 4, part // 2 % 2, part % 2
            ]
        table = pl.ds(base, rows)
        return pltpu.make_async_copy(ordered.at[table], table_out.at[table], out_sem.at[block])

    early = -(-4 * D // wide.shape[0])
    for block in range(early):
        stores.append(put(block))
        stores[-1].start()

    results = []

    def give(src, dst):
        copy = pltpu.make_async_copy(src, dst, work_sem.at[len(results)])
        results.append(copy)
        return copy

    for p in range(passages):
        project(
            tokens_land[p], ordered, vec_ref, q_all.at[p], k_all.at[p], v_all.at[p], v_turned.at[p]
        )
    for src, dst in ((q_all, q_out), (k_all, k_out), (v_all, v_out)):
        give(src, dst).start()
    pairs = HEADS // 2
    lengths = [lengths_ref[blk * passages + p] for p in range(passages)]

    def finish(p):
        first_norm(
            tokens_land[p], ctx_all[p], ordered, vec_ref, normed_all.at[p], inv_all.at[p]
        )
        for src, dst in (
            (ctx_all, ctx_out),
            (normed_all, normed_out),
            (inv_all, inv_out),
            (lse_all, lse_out),
        ):
            give(src.at[p], dst.at[p]).start()

    for p in range(passages):

        @pl.loop(0, pairs)
        def _(pair, p=p):
            for slot in range(pairs):
                block = early + p * pairs + slot
                if block < 2 * nz:

                    @pl.when(pair == slot)
                    def _(block=block):
                        put(block).start()

            attend_pair(
                pair,
                lengths[p],
                q_all.at[p],
                k_all.at[p],
                v_turned.at[p],
                lse_all.at[p],
                ctx_all.at[p],
                ctx_turned,
                scores,
                weights,
            )

        if p == passages - 1:
            for copy in own_copies[1:] + swaps[3:]:
                copy.wait()
            give(cot_land, cot_out).start()
        finish(p)
    for block in range(early, 2 * nz):
        table = pl.ds(block * wide.shape[0], wide.shape[0])
        stores.append(
            pltpu.make_async_copy(ordered.at[table], table_out.at[table], out_sem.at[block])
        )
    for copy in stores + results:
        copy.wait()


def enter(nz, full, owners, tokens, cotangent, master, lengths, vectors):
    f32, low = jnp.float32, jnp.bfloat16
    rows = master.shape[0]
    quarter = (rows - full) // 8
    shares, span, _ = tokens.shape
    passages, span = shares // 4, 4 * span
    swapped = (passages, span, D)
    any_spec = pl.BlockSpec(memory_space=pl.ANY)
    smem = pl.BlockSpec(memory_space=pltpu.SMEM)
    dma = pltpu.SemaphoreType.DMA
    shape = lambda kind: jax.ShapeDtypeStruct(swapped, kind)
    lse = (passages, HEADS, 1, span)
    return pl.pallas_call(
        functools.partial(enter_kernel, nz, full),
        out_shape=(
            shape(low),
            shape(low),
            jax.ShapeDtypeStruct((2 * nz * rows, D), low),
            shape(low),
            shape(low),
            shape(low),
            jax.ShapeDtypeStruct(lse, f32),
            shape(low),
            shape(f32),
            jax.ShapeDtypeStruct((passages, span, 128), f32),
            jax.ShapeDtypeStruct((VEC_LEN // D, D), f32),
        ),
        in_specs=[smem] + [any_spec] * 3 + [smem, pl.BlockSpec(memory_space=pltpu.VMEM)],
        out_specs=[any_spec] * 10 + [pl.BlockSpec(memory_space=pltpu.VMEM)],
        scratch_shapes=[
            pltpu.VMEM((rows, D), f32),
            pltpu.VMEM((2 * quarter, D), f32),
            pltpu.VMEM(swapped, low),
            pltpu.VMEM(swapped, low),
            pltpu.VMEM((2 * nz, full, D), low),
            pltpu.VMEM((2 * nz, 2, 2, 2, quarter, D), low),
            pltpu.VMEM((2 * nz * rows, D), low),
            dma((2,)),
            dma((2, 2, 3)),
            dma((2,)),
            dma((2, 2, 2, nz)),
            dma((2, 2, nz)),
            dma((2, 2, nz)),
            dma((2, 6, nz)),
            dma((2, 2)),
            dma((2 * nz + 1,)),
            pltpu.VMEM(swapped, low),
            pltpu.VMEM(swapped, low),
            pltpu.VMEM(swapped, low),
            pltpu.VMEM((passages, D, span), low),
            pltpu.VMEM(lse, f32),
            pltpu.VMEM(swapped, low),
            pltpu.VMEM(swapped, f32),
            pltpu.VMEM((passages, span, 128), f32),
            pltpu.VMEM((128, span), f32),
            pltpu.VMEM((2, span, span // 2), f32),
            pltpu.VMEM((2, span, span // 2), low),
            dma((4 + 4 * passages,)),
        ],
        compiler_params=pltpu.CompilerParams(
            collective_id=2, has_side_effects=True, vmem_limit_bytes=60 * 1024 * 1024
        ),
        cost_estimate=pl.CostEstimate(
            flops=passages * span * (8 * D * D + 4 * D * span),
            bytes_accessed=6 * 10**7,
            transcendentals=passages * HEADS * span * span,
        ),
        name="enter",
    )(owners, tokens, cotangent, master, lengths, vectors.reshape(-1, 128))


def tail_kernel(
    nz,
    owners_ref,
    qkv_ref,
    back_ref,
    vec_ref,
    d_tokens_ref,
    own_ref,
    vec_sum_ref,
    norm_ref,
    d_tokens_out,
    acc,
    land_one,
    land_two,
    one_sem,
    two_sem,
    late_sem,
    part,
    mine,
    up_land,
    down_land,
    up_send,
    down_send,
    own_part,
    assembled,
    vec_send,
    vec_land,
    sq_send,
    sq_land,
    part_sem,
    up_sem,
    down_sem,
    gather_sem,
    vec_sem,
    sq_sem,
    out_sem,
    *swap_refs,
):
    dp, blk, z, c, y, x, sibling, x_peer, y_peer = place_of()

    def z_peer(hop):
        return (blk, 2 * lax.rem(z + hop, nz) + c)

    def send(src, dst, sems, slot, device):
        copy = remote_copy(src, dst, sems, slot, device)
        copy.start()
        return copy

    swaps = [
        PositionSwap(d_tokens_ref, d_tokens_out, *swap_refs),
    ]
    partners = [sibling, x_peer, y_peer, swaps[0].diagonal] + [z_peer(h) for h in range(1, nz)]
    barrier = greet(partners)
    late = qkv_ref.shape[0]
    load = pltpu.make_async_copy(back_ref, part.at[pl.ds(late, back_ref.shape[0])], part_sem)
    load.start()
    late_load = pltpu.make_async_copy(qkv_ref, acc, late_sem)
    late_load.start()
    sems = (None, None, one_sem, two_sem)
    summed = PlaneSum((), QKV_COUNTS, acc, None, land_one, land_two, part, sems)
    slots = range(len(summed.chunks))
    for row in range(VEC_LEN // D):
        for col in range(D // 128):
            at = row * (D // 128) + col
            vec_send[0, at : at + 1] = vec_ref[row : row + 1, col * 128 : (col + 1) * 128]
    late_load.wait()
    pl.semaphore_wait(barrier, len(partners))
    for slot in slots:
        summed.one(slot).start()

    def vec_copy(turn):
        peer = (sibling, x_peer, y_peer)[turn]
        return remote_copy(vec_send.at[turn], vec_land.at[turn], vec_sem, turn, peer)

    def vec_next(turn):
        vec_copy(turn).wait()
        vec_send[turn + 1] = vec_send[turn] + vec_land[turn]
        if turn < 2:
            vec_copy(turn + 1).start()

    vec_copy(0).start()
    vec_next(0)
    vec_next(1)
    vec_next(2)
    vec_z = [
        send(vec_send.at[3], vec_land.at[3 + z], vec_sem, 2 + hop, z_peer(hop))
        for hop in range(1, nz)
    ]
    summed.crossed(slots)
    load.wait()
    summed.settled(slots)
    for swap in swaps:
        swap.begin()

    grains = part.shape[0] // (2 * nz)
    for block in range(2 * nz):
        place = owners_ref[block] * grains
        for g in range(grains):
            mine[block, g] = part[place + g]

    def gather(turn, piece):
        views = (
            (own_part.at[1 - c, piece], assembled.at[piece, c, y, x], sibling),
            (assembled.at[piece, 0, y, x], assembled.at[piece, 0, y, x], x_peer),
            (assembled.at[piece, 1, y, x], assembled.at[piece, 1, y, x], y_peer),
            (assembled.at[piece, 0, y], assembled.at[piece, 0, y], y_peer),
            (assembled.at[piece, 1, :, x], assembled.at[piece, 1, :, x], x_peer),
        )
        src, dst, peer = views[turn]
        return remote_copy(src, dst, gather_sem, turn * grains + piece, peer)

    def chain(zv):
        unit, wait = 3.0, 2.5
        steps, copies = [], []

        def message(upward, d, piece):
            land, sends, sems = (
                (up_land, up_send, up_sem) if upward else (down_land, down_send, down_sem)
            )
            target = (blk, dp + 2 if upward else dp - 2)
            return remote_copy(
                sends.at[d, piece], land.at[d, piece], sems, d * grains + piece, target
            )

        def passing(upward, d, piece):
            def run():
                land, sends = (up_land, up_send) if upward else (down_land, down_send)
                fed = zv > 0 if upward else zv < nz - 1
                copy = message(upward, d, piece)
                if fed:
                    copy.wait_recv()
                for j in range(2):
                    value = mine[2 * d + j, piece]
                    if fed:
                        value = add_low(value, land[d, piece, j])
                    sends[d, piece, j] = value
                copy.start()
                copies.append(copy)

            return run

        def arrived(piece):
            if zv > 0:
                message(True, zv, piece).wait_recv()
            if zv < nz - 1:
                message(False, zv, piece).wait_recv()
            squares = jnp.zeros((8, D), jnp.float32)
            for j in range(2):
                value = mine[2 * zv + j, piece].astype(jnp.float32)
                if zv > 0:
                    value = value + up_land[zv, piece, j].astype(jnp.float32)
                if zv < nz - 1:
                    value = value + down_land[zv, piece, j].astype(jnp.float32)
                rounded = value.astype(jnp.bfloat16)
                own_part[j, piece] = rounded
                again = rounded.astype(jnp.float32)
                squares = squares + jnp.sum((again * again).reshape(-1, 8, D), axis=0)
            total = squares[:, 0:128]
            for col in range(1, D // 128):
                total = total + squares[:, col * 128 : (col + 1) * 128]
            sq_send[0] = total if piece == 0 else sq_send[0] + total
            assembled[piece, c, y, x] = own_part[c, piece]
            gather(0, piece).start()

        def over_pair(piece):
            gather(0, piece).wait()
            gather(1, piece).start()
            gather(2, piece).start()

        def over_plane(piece):
            gather(1, piece).wait()
            gather(3, piece).start()
            gather(2, piece).wait()
            gather(4, piece).start()

        for piece in range(grains):
            first = piece * (nz - 1)
            for d in range(zv + 1, nz):
                at = (zv + first + nz - 1 - d) * unit + zv * wait
                steps.append((at, passing(True, d, piece)))
            for d in range(zv):
                at = (nz - 1 - zv + first + d) * unit + (nz - 1 - zv) * wait
                steps.append((at, passing(False, d, piece)))
            end = (first + nz - 1) * unit + (nz - 1) * wait
            steps.append((end, functools.partial(arrived, piece)))
            if piece < grains - 1:
                steps.append((end + 5.0, functools.partial(over_pair, piece)))
                steps.append((end + 9.5, functools.partial(over_plane, piece)))
        for _, step in sorted(steps, key=lambda entry: entry[0]):
            step()
        for copy in copies:
            copy.wait_send()
        sq = remote_copy(sq_send.at[0], sq_land.at[0], sq_sem, 0, sibling)
        sq.start()
        over_pair(grains - 1)
        sq.wait()

    for zv in range(nz):
        run_when(z == zv, functools.partial(chain, zv))

    for swap in swaps:
        swap.passed()
    sq_send[1] = sq_send[0] + sq_land[0]
    sq = send(sq_send.at[1], sq_land.at[1], sq_sem, 1, x_peer)
    sq.wait()
    sq_send[2] = sq_send[1] + sq_land[1]
    sq = send(sq_send.at[2], sq_land.at[2], sq_sem, 2, y_peer)
    last = grains - 1
    gather(1, last).wait()
    gather(3, last).start()
    gather(2, last).wait()
    gather(4, last).start()
    sq.wait()
    sq_send[3] = sq_send[2] + sq_land[2]
    sq_z = [
        send(sq_send.at[3], sq_land.at[3 + z], sq_sem, 2 + hop, z_peer(hop)) for hop in range(1, nz)
    ]
    for copy in vec_z + sq_z:
        copy.wait()
    vec_land[3 + z] = vec_send[3]
    sq_land[3 + z] = sq_send[3]
    vec_total, sq_total = vec_land[3], sq_land[3]
    for other in range(1, nz):
        vec_total = vec_total + vec_land[3 + other]
        sq_total = sq_total + sq_land[3 + other]
    vec_sum_ref[...] = vec_total
    grad_norm = jnp.sqrt(
        jnp.sum(sq_total, keepdims=True) + jnp.sum(vec_total * vec_total, keepdims=True)
    )
    norm_ref[...] = grad_norm
    done = []
    for piece in range(grains):
        gather(3, piece).wait()
        gather(4, piece).wait()
        for place in range(8):
            at = (piece * 8 + place) * GRAIN
            done.append(
                pltpu.make_async_copy(
                    assembled.at[piece, place // 4, place // 2 % 2, place % 2],
                    own_ref.at[pl.ds(at, GRAIN)],
                    out_sem.at[piece, place],
                )
            )
            done[-1].start()
    for swap in swaps:
        swap.end()
    for copy in done:
        copy.wait()


def tail(nz, owners, g_qkv, back, grad_vector, d_tokens):
    low, f32 = jnp.bfloat16, jnp.float32
    passages, span, _ = d_tokens.shape
    swapped = jax.ShapeDtypeStruct((4 * passages, span // 4, D), low)
    late = g_qkv.shape[0]
    granules = late + back.shape[0]
    grains = granules // (2 * nz)
    any_spec = pl.BlockSpec(memory_space=pl.ANY)
    vmem = pl.BlockSpec(memory_space=pltpu.VMEM)
    dma = pltpu.SemaphoreType.DMA
    block = lambda *lead: pltpu.VMEM((*lead, GRAIN, D), low)
    lanes = (VEC_LEN // 128, 128)
    return pl.pallas_call(
        functools.partial(tail_kernel, nz),
        out_shape=(
            jax.ShapeDtypeStruct((grains * 8 * GRAIN, D), low),
            jax.ShapeDtypeStruct(lanes, f32),
            jax.ShapeDtypeStruct((1, 1), f32),
            swapped,
        ),
        in_specs=[pl.BlockSpec(memory_space=pltpu.SMEM)]
        + [any_spec] * 2
        + [vmem, any_spec],
        out_specs=(any_spec, vmem, vmem, any_spec),
        scratch_shapes=[
            block(late, 2, 2),
            block(late, 2),
            block(late),
            dma((2, len(plane_chunks(QKV_COUNTS)))),
            dma((2, len(plane_chunks(QKV_COUNTS)))),
            dma(()),
            block(granules),
            block(2 * nz, grains),
            block(nz, grains, 2),
            block(nz, grains, 2),
            block(nz, grains, 2),
            block(nz, grains, 2),
            block(2, grains),
            block(grains, 2, 2, 2),
            pltpu.VMEM((4, *lanes), f32),
            pltpu.VMEM((3 + nz, *lanes), f32),
            pltpu.VMEM((4, 8, 128), f32),
            pltpu.VMEM((3 + nz, 8, 128), f32),
            dma(()),
            dma((2, nz * grains)),
            dma((2, nz * grains)),
            dma((2, 5 * grains)),
            dma((2, 2 + nz)),
            dma((2, 2 + nz)),
            dma((grains, 8)),
        ]
        + PositionSwap.scratch(passages, span),
        compiler_params=pltpu.CompilerParams(
            collective_id=1, has_side_effects=True, vmem_limit_bytes=60 * 1024 * 1024
        ),
        cost_estimate=pl.CostEstimate(flops=10**7, bytes_accessed=3 * 10**7, transcendentals=0),
        name="grad_tail",
    )(owners, g_qkv, back, grad_vector, d_tokens)


def keep_lanes(rows, half):
    lane = lax.broadcasted_iota(jnp.int32, rows.shape, 1)
    keep = lane < HEAD_DIM if half == 0 else lane >= HEAD_DIM
    return jnp.where(keep, rows, jnp.zeros_like(rows))


def norm_rows(mixed):
    row_mean = jnp.mean(mixed, axis=-1, keepdims=True)
    centred = mixed - row_mean
    inv_std = lax.rsqrt(jnp.mean(centred * centred, axis=-1, keepdims=True) + 1e-12)
    return centred * inv_std, inv_std


def project(x, w_ref, vec_ref, q_out, k_out, v_out, v_turned):
    f32, low = jnp.float32, jnp.bfloat16

    def product(lo):
        return jnp.dot(x, w_ref[lo : lo + D], preferred_element_type=f32)

    q_out[...] = ((product(0) + vec_ref[0:1]).astype(low).astype(f32) * 0.125).astype(low)
    k_out[...] = product(D).astype(low)
    values = product(2 * D) + vec_ref[1:2]
    v_out[...] = values.astype(low)
    v_turned[...] = values.T.astype(low)


def attend_pair(pair, length, q_ref, k_ref, v_turned, lse_ref, ctx_ref, ctx_turned, scores, weights):
    f32, low = jnp.float32, jnp.bfloat16
    span = q_ref.shape[0]
    width, strip = span // 2, 64
    lanes = pl.ds(pl.multiple_of(pair * 128, 128), 128)
    keys = k_ref[:, lanes]
    head_keys = [keep_lanes(keys, half) for half in range(2)]
    units = [(half, part) for half in range(2) for part in range(2)]

    def score(unit):
        half, part = units[unit]
        scores[unit % 2] = contract_cols(head_keys[half], q_ref[part * width : (part + 1) * width, lanes])

    def masked(unit, at):
        row = at + lax.broadcasted_iota(jnp.int32, (strip, width), 0)
        return jnp.where(row < length, scores[unit % 2, at : at + strip], -1000000000.0)

    def fold(value, op):
        return op(value.reshape(strip // 8, 8, width), axis=0)

    score(0)
    for unit, (half, part) in enumerate(units):
        if unit + 1 < len(units):
            score(unit + 1)
        cols = pl.ds(part * width, width)
        tops = fold(masked(unit, 0), jnp.max)
        for at in range(strip, span, strip):
            tops = jnp.maximum(tops, fold(masked(unit, at), jnp.max))
        peak = jnp.max(tops, axis=0, keepdims=True)
        sums = jnp.zeros((8, width), f32)
        for at in range(0, span, strip):
            weight = jnp.exp(masked(unit, at) - peak)
            sums = sums + fold(weight, jnp.sum)
            weights[unit % 2, at : at + strip] = weight.astype(low)
        total = jnp.sum(sums, axis=0, keepdims=True)
        lse_ref[2 * pair + half, :, cols] = peak + jnp.log(total)
        turned = v_turned[pl.ds(pl.multiple_of(pair * 128 + half * 64, 64), 64), :]
        out = jnp.dot(turned, weights[unit % 2], preferred_element_type=f32)
        ctx_turned[half * 64 : half * 64 + 64, cols] = out / total
    ctx_ref[:, lanes] = ctx_turned[...].T.astype(low)


def first_norm(x, ctx, w_ref, vec_ref, normed_ref, inv_ref):
    attn_out = jnp.dot(ctx, w_ref[3 * D : 4 * D], preferred_element_type=jnp.float32)
    normed, inv_std = norm_rows(x.astype(jnp.float32) + (attn_out + vec_ref[2:3]))
    normed_ref[...] = normed
    inv_ref[...] = jnp.broadcast_to(inv_std, inv_ref.shape)


def attend_kernel(
    lengths_ref,
    x_ref,
    w_ref,
    vec_ref,
    q_ref,
    k_ref,
    v_ref,
    lse_ref,
    ctx_ref,
    normed_ref,
    inv_ref,
    v_turned,
    ctx_turned,
    scores,
    weights,
):
    length = lengths_ref[lax.axis_index("blk") * pl.num_programs(0) + pl.program_id(0)]
    x = x_ref[0]
    project(x, w_ref, vec_ref, q_ref.at[0], k_ref.at[0], v_ref.at[0], v_turned)

    @pl.loop(0, HEADS // 2)
    def _(pair):
        attend_pair(
            pair,
            length,
            q_ref.at[0],
            k_ref.at[0],
            v_turned,
            lse_ref.at[0],
            ctx_ref.at[0],
            ctx_turned,
            scores,
            weights,
        )

    first_norm(x, ctx_ref[0], w_ref, vec_ref, normed_ref.at[0], inv_ref.at[0])


def attend(lengths, tokens, table, vec_rows):
    f32, low = jnp.float32, jnp.bfloat16
    passages, span, _ = tokens.shape
    rows = pl.BlockSpec((1, span, D), lambda p: (p, 0, 0))
    shape = lambda kind: jax.ShapeDtypeStruct((passages, span, D), kind)
    return pl.pallas_call(
        attend_kernel,
        grid=(passages,),
        out_shape=(
            shape(low),
            shape(low),
            shape(low),
            jax.ShapeDtypeStruct((passages, HEADS, 1, span), f32),
            shape(low),
            shape(f32),
            jax.ShapeDtypeStruct((passages, span, 128), f32),
        ),
        in_specs=[
            pl.BlockSpec(memory_space=pltpu.SMEM),
            rows,
            pl.BlockSpec((4 * D, D), lambda p: (0, 0)),
            pl.BlockSpec((VEC_LEN // D, D), lambda p: (0, 0)),
        ],
        out_specs=(
            rows,
            rows,
            rows,
            pl.BlockSpec((1, HEADS, 1, span), lambda p: (p, 0, 0, 0)),
            rows,
            rows,
            pl.BlockSpec((1, span, 128), lambda p: (p, 0, 0)),
        ),
        scratch_shapes=[
            pltpu.VMEM((D, span), low),
            pltpu.VMEM((128, span), f32),
            pltpu.VMEM((2, span, span // 2), f32),
            pltpu.VMEM((2, span, span // 2), low),
        ],
        compiler_params=pltpu.CompilerParams(vmem_limit_bytes=56 * 1024 * 1024),
        cost_estimate=pl.CostEstimate(
            flops=passages * span * (8 * D * D + 4 * D * span),
            bytes_accessed=passages * span * D * 20,
            transcendentals=passages * HEADS * span * span,
        ),
        name="attend",
    )(lengths, tokens, table, vec_rows)


def plane_chunks(counts):
    chunks, base = [], 0
    for source, count in enumerate(counts):
        half = count // 2
        step = half if half % 2 else 2
        for first in range(0, half, step):
            chunks.append((source, first, step, base + first, True))
            chunks.append((source, half + first, step, base + half + first, False))
        base += count
    return chunks


def plane_order(granules):
    half = granules // 2

    def order(turn):
        pair = turn // 2
        return lax.rem(pair, 2) * half + (pair // 2) * 2 + lax.rem(turn, 2)

    return order


def place_of():
    dp, blk = lax.axis_index("dp"), lax.axis_index("blk")
    z, c, y, x = dp // 2, dp % 2, blk // 2, blk % 2
    sibling = (blk, 2 * z + 1 - c)
    x_peer = (2 * y + 1 - x, dp)
    y_peer = (2 * (1 - y) + x, dp)
    return dp, blk, z, c, y, x, sibling, x_peer, y_peer


def remote_copy(src, dst, sems, slot, device):
    return pltpu.make_async_remote_copy(
        src_ref=src,
        dst_ref=dst,
        send_sem=sems.at[0, slot],
        recv_sem=sems.at[1, slot],
        device_id=device,
        device_id_type=MESH,
    )


class PlaneSum:
    def __init__(self, sources, counts, acc, core_land, one_land, two_land, part, sems, base=0):
        self.sources, self.acc, self.core_land = sources, acc, core_land
        self.one_land, self.two_land, self.part, self.base = one_land, two_land, part, base
        self.load_sem, self.core_sem, self.one_sem, self.two_sem = sems
        self.chunks = plane_chunks(counts)
        self.place = place_of()

    def load(self, slot):
        source, first, count, at, _ = self.chunks[slot]
        return pltpu.make_async_copy(
            self.sources[source].at[pl.ds(first, count), self.place[3]],
            self.acc.at[pl.ds(at, count)],
            self.load_sem.at[slot],
        )

    def core(self, slot):
        source, first, count, at, _ = self.chunks[slot]
        return remote_copy(
            self.sources[source].at[pl.ds(first, count), 1 - self.place[3]],
            self.core_land.at[pl.ds(at, count)],
            self.core_sem,
            slot,
            self.place[6],
        )

    def one(self, slot):
        _, _, count, at, x_first = self.chunks[slot]
        _, _, _, _, y, x, _, x_peer, y_peer = self.place
        rows = pl.ds(at, count)
        view = self.acc.at[rows, :, 1 - x] if x_first else self.acc.at[rows, 1 - y]
        return remote_copy(
            view, self.one_land.at[rows], self.one_sem, slot, x_peer if x_first else y_peer
        )

    def two(self, slot):
        _, _, count, at, x_first = self.chunks[slot]
        _, _, _, _, y, x, _, x_peer, y_peer = self.place
        rows = pl.ds(at, count)
        view = self.acc.at[rows, 1 - y, x] if x_first else self.acc.at[rows, y, 1 - x]
        return remote_copy(
            view, self.two_land.at[rows], self.two_sem, slot, y_peer if x_first else x_peer
        )

    def begin(self, slots):
        for slot in slots:
            self.load(slot).start()
            self.core(slot).start()

    def paired(self, slots, go_on=True):
        for slot in slots:
            self.load(slot).wait()
            self.core(slot).wait()
            _, _, count, at, _ = self.chunks[slot]

            @pl.loop(at, at + count)
            def _(g):
                self.acc[g] = add_low(self.acc[g], self.core_land[g])

            if go_on:
                self.one(slot).start()

    def crossed(self, slots):
        _, _, _, _, y, x, _, _, _ = self.place
        for slot in slots:
            self.one(slot).wait()
            _, _, count, at, x_first = self.chunks[slot]

            @pl.loop(at, at + count)
            def _(g):
                for side in range(2):
                    if x_first:
                        self.acc[g, side, x] = add_low(self.acc[g, side, x], self.one_land[g, side])
                    else:
                        self.acc[g, y, side] = add_low(self.acc[g, y, side], self.one_land[g, side])

            self.two(slot).start()

    def half_settled(self, slots, red_ref, red_sem):
        _, _, _, _, y, x, _, _, _ = self.place
        for slot in slots:
            self.one(slot).wait()
            _, _, count, at, x_first = self.chunks[slot]

            @pl.loop(at, at + count)
            def _(g):
                for side in range(2):
                    if x_first:
                        self.acc[g, side, x] = add_low(self.acc[g, side, x], self.one_land[g, side])
                    else:
                        self.acc[g, y, side] = add_low(self.acc[g, y, side], self.one_land[g, side])

            self.kept(slot, red_ref, red_sem).start()

    def kept(self, slot, red_ref, red_sem):
        _, _, count, at, x_first = self.chunks[slot]
        _, _, _, _, y, x, _, _, _ = self.place
        rows = pl.ds(at, count)
        view = self.acc.at[rows, :, x] if x_first else self.acc.at[rows, y]
        return pltpu.make_async_copy(view, red_ref.at[rows], red_sem.at[slot])

    def settled(self, slots):
        _, _, _, _, y, x, _, _, _ = self.place
        for slot in slots:
            self.two(slot).wait()
            _, _, count, at, _ = self.chunks[slot]

            @pl.loop(at, at + count)
            def _(g):
                self.part[self.base + g] = add_low(self.acc[g, y, x], self.two_land[g])

    @staticmethod
    def scratch(counts, with_part=True):
        low, dma = jnp.bfloat16, pltpu.SemaphoreType.DMA
        total, slots = sum(counts), len(plane_chunks(counts))
        shapes = [
            pltpu.VMEM((total, 2, 2, GRAIN, D), low),
            pltpu.VMEM((total, 2, 2, GRAIN, D), low),
            pltpu.VMEM((total, 2, GRAIN, D), low),
            pltpu.VMEM((total, GRAIN, D), low),
            dma((slots,)),
            dma((2, slots)),
            dma((2, slots)),
            dma((2, slots)),
        ]
        return shapes + ([pltpu.VMEM((total, GRAIN, D), low)] if with_part else [])


class SecondStep:
    def __init__(self, red_ref, counts, keep, land, part, load_sem, two_sem, base):
        _, _, _, _, y, x, _, x_peer, y_peer = place_of()
        self.keep, self.land, self.part, self.base = keep, land, part, base
        self.chunks = plane_chunks(counts)
        self.loads, self.sends = [], []
        for slot, (_, _, count, at, x_first) in enumerate(self.chunks):
            rows = pl.ds(at, count)
            near, far, peer = (y, 1 - y, y_peer) if x_first else (x, 1 - x, x_peer)
            self.loads.append(
                pltpu.make_async_copy(red_ref.at[rows, near], keep.at[rows], load_sem.at[slot])
            )
            self.sends.append(
                remote_copy(red_ref.at[rows, far], land.at[rows], two_sem, slot, peer)
            )

    def begin(self):
        for copy in self.loads + self.sends:
            copy.start()

    def end(self):
        for slot, (_, _, count, at, _) in enumerate(self.chunks):
            self.loads[slot].wait()
            self.sends[slot].wait()

            @pl.loop(at, at + count)
            def _(g):
                self.part[self.base + g] = add_low(self.keep[g], self.land[g])

    @staticmethod
    def scratch(counts):
        low, dma = jnp.bfloat16, pltpu.SemaphoreType.DMA
        total, slots = sum(counts), len(plane_chunks(counts))
        block = pltpu.VMEM((total, GRAIN, D), low)
        return [block, block, dma((slots,)), dma((2, slots))]


def run_when(condition, task):
    @pl.when(condition)
    def _():
        task()


def greet(partners):
    barrier = pltpu.get_barrier_semaphore()
    for partner in partners:
        pl.semaphore_signal(barrier, inc=1, device_id=partner, device_id_type=MESH)
    return barrier


class PositionSwap:
    def __init__(self, rows_in, rows_out, keep, keep_sem, swap_sem):
        dp, blk, _, _, _, _, _, x_peer, y_peer = place_of()
        passages, span = rows_in.shape[0], rows_out.shape[1]
        self.diagonal = (3 - blk, dp)
        at = pl.ds(blk * passages, passages)
        self.first = pltpu.make_async_copy(
            rows_in.at[:, pl.ds(blk * span, span)], keep, keep_sem.at[0]
        )
        self.second = pltpu.make_async_copy(keep, rows_out.at[at], keep_sem.at[1])
        self.pushes = [
            remote_copy(
                rows_in.at[:, pl.ds(peer[0] * span, span)], rows_out.at[at], swap_sem, slot, peer
            )
            for slot, peer in enumerate((x_peer, y_peer, self.diagonal))
        ]

    def begin(self):
        for copy in [self.first] + self.pushes:
            copy.start()

    def passed(self):
        self.first.wait()
        self.second.start()

    def end(self):
        for copy in [self.second] + self.pushes:
            copy.wait()

    @staticmethod
    def scratch(passages, span):
        dma = pltpu.SemaphoreType.DMA
        return [pltpu.VMEM((passages, span // 4, D), jnp.bfloat16), dma((2,)), dma((2, 3))]


def attend_back_kernel(
    lengths_ref,
    x_ref,
    w_ref,
    q_ref,
    k_ref,
    v_ref,
    lse_ref,
    d_ctx_ref,
    d_mixed_ref,
    vec_in_ref,
    *refs,
):
    f32, low = jnp.float32, jnp.bfloat16
    beside = len(refs) > 13
    tasks = {}
    if beside:
        *sources, outer_red, refs = *refs[:3], refs[3:]
        red_ref, refs = refs[3], refs[:3] + refs[4:]
        extra, refs = refs[13:], refs[:13]
        acc, core_land, one_land, two_land, *sems, keep, land, keep_sem, keep_two, share, red_sem = extra[:14]
        late, late_acc, late_land, late_load, late_core, late_sem = extra[14:]
    grad_ref, table_ref, vec_ref, k_turned, dq_turned, dq_all, dk_all, dv_all, x_all = refs[:9]
    scores, d_probs, probs_low, d_scores = refs[9:]
    passage = pl.program_id(0)
    if beside:
        summed = PlaneSum(sources, BACK_COUNTS, acc, core_land, one_land, two_land, share, sems)
        second = SecondStep(
            outer_red, OUTER_COUNTS, keep, land, share, keep_sem, keep_two, sum(BACK_COUNTS)
        )
        slots = range(len(summed.chunks))
        late_sems = (late_load, late_core, None, None)
        late_sum = PlaneSum((late,), QKV_COUNTS, late_acc, late_land, None, None, None, late_sems)
        late_slots = range(len(late_sum.chunks))

        @pl.when(passage == 0)
        def _():
            greet(summed.place[6:])

        def begin():
            pl.semaphore_wait(pltpu.get_barrier_semaphore(), 3)
            summed.begin(slots)
            second.begin()

        tasks = {
            0: begin,
            3: lambda: summed.paired(slots),
            5: second.end,
            9: lambda: summed.crossed(slots),
        }

        def end():
            summed.settled(slots)
            stored = [pltpu.make_async_copy(share, red_ref, red_sem)]
            stored[0].start()
            late_sum.paired(late_slots, go_on=False)
            stored.append(pltpu.make_async_copy(late_acc, table_ref, late_sem))
            stored[1].start()
            for copy in stored:
                copy.wait()

    span = x_ref.shape[1]
    half_span, strip = span // 2, 64
    length = lengths_ref[lax.axis_index("blk") * pl.num_programs(0) + passage]
    rows = pl.ds(pl.multiple_of(passage * span, span), span)
    x_all[rows, :] = x_ref[0]
    k_turned[...] = k_ref[0].astype(f32).T.astype(low)
    @pl.loop(0, HEADS // 2)
    def _(pair):
        slot = passage * (HEADS // 2) + pair
        for at in sorted(tasks):
            run_when(slot == at, tasks[at])
        lanes = pl.ds(pl.multiple_of(pair * 128, 128), 128)
        keys, values = k_ref[0, :, lanes], v_ref[0, :, lanes]
        dk, dv = jnp.zeros((span, 128), f32), jnp.zeros((span, 128), f32)
        units = [(half, part) for half in range(2) for part in range(2)]

        def products(unit):
            half, part = units[unit]
            cols = pl.ds(part * half_span, half_span)
            scores[unit % 2] = contract_cols(keep_lanes(keys, half), q_ref[0, cols, lanes])
            d_probs[unit % 2] = contract_cols(keep_lanes(values, half), d_ctx_ref[0, cols, lanes])

        def fold(value):
            return jnp.sum(value.reshape(strip // 8, 8, half_span), axis=0)

        products(0)
        for unit, (half, part) in enumerate(units):
            if unit + 1 < len(units):
                products(unit + 1)
            cols = pl.ds(part * half_span, half_span)
            side = unit % 2
            log_total = lse_ref[0, 2 * pair + half, :, cols]
            sums = jnp.zeros((8, half_span), f32)
            for at in range(0, span, strip):
                here = slice(at, at + strip)
                row = at + lax.broadcasted_iota(jnp.int32, (strip, half_span), 0)
                masked = jnp.where(row < length, scores[side, here], -1000000000.0)
                probs = jnp.exp(masked - log_total)
                weighted = probs * d_probs[side, here]
                probs_low[side, here] = probs.astype(low)
                scores[side, here] = probs
                d_probs[side, here] = weighted
                sums = sums + fold(weighted)
            inner = jnp.sum(sums, axis=0, keepdims=True)
            for at in range(0, span, strip):
                here = slice(at, at + strip)
                d_scores[side, here] = (d_probs[side, here] - scores[side, here] * inner).astype(low)
            d_out = keep_lanes(d_ctx_ref[0, cols, lanes], half)
            dv = dv + jnp.dot(probs_low[side], d_out, preferred_element_type=f32)
            queries = keep_lanes(q_ref[0, cols, lanes], half)
            dk = dk + jnp.dot(d_scores[side], queries, preferred_element_type=f32)
            turned = k_turned[pl.ds(pl.multiple_of(pair * 128 + half * 64, 64), 64), :]
            dq_turned[half * 64 : half * 64 + 64, cols] = (
                jnp.dot(turned, d_scores[side], preferred_element_type=f32) * 0.125
            )
        dq_all[rows, lanes] = dq_turned[...].T.astype(low)
        dk_all[rows, lanes] = dk.astype(low)
        dv_all[rows, lanes] = dv.astype(low)

    @pl.when(passage == pl.num_programs(0) - 1)
    def _():
        for at, part in enumerate((dq_all, dk_all, dv_all)):
            d_weight = contract_rows(x_all[...], part[...]).astype(low)
            if beside:
                late[2 * at : 2 * at + 2] = d_weight.reshape(2, 2, 2, 2, GRAIN, D)
                if at >= 1:
                    late_sum.begin([at - 1])
            else:
                table_ref[at * D : (at + 1) * D] = d_weight

    grad = d_mixed_ref[0]
    for lo, part in ((0, dq_all), (D, dk_all), (2 * D, dv_all)):
        grad = grad + contract_cols(part[rows, :], w_ref[lo : lo + D])
    grad_ref[0] = grad.astype(low)

    @pl.when(passage == pl.num_programs(0) - 1)
    def _():
        vec_ref[...] = vec_in_ref[...]
        vec_ref[0:1] = jnp.sum(dq_all[...].astype(f32), axis=0, keepdims=True)
        vec_ref[1:2] = jnp.sum(dv_all[...].astype(f32), axis=0, keepdims=True)
        if beside:
            end()


def attend_back(
    lengths, tokens, table, queries, keys, values, lse, d_ctx, d_mixed, vec_grad, sources=()
):
    f32, low = jnp.float32, jnp.bfloat16
    passages, span, _ = tokens.shape
    rows = pl.BlockSpec((1, span, D), lambda p: (p, 0, 0))
    whole = pltpu.VMEM((passages * span, D), low)
    any_spec = pl.BlockSpec(memory_space=pl.ANY)
    red_shape, beside, extra, more = (), [], {}, ()
    table_shape = jax.ShapeDtypeStruct((3 * D, D), low)
    table_spec = pl.BlockSpec((3 * D, D), lambda p: (0, 0))
    if sources:
        total = sum(BACK_COUNTS) + sum(OUTER_COUNTS)
        red_shape = (jax.ShapeDtypeStruct((total, GRAIN, D), low),)
        beside = PlaneSum.scratch(BACK_COUNTS, with_part=False) + SecondStep.scratch(OUTER_COUNTS)
        dma = pltpu.SemaphoreType.DMA
        beside += [pltpu.VMEM((total, GRAIN, D), low), dma]
        late, chunks = sum(QKV_COUNTS), len(plane_chunks(QKV_COUNTS))
        table_shape = jax.ShapeDtypeStruct((late, 2, 2, GRAIN, D), low)
        table_spec = any_spec
        beside += [
            pltpu.VMEM((late, 2, 2, 2, GRAIN, D), low),
            pltpu.VMEM((late, 2, 2, GRAIN, D), low),
            pltpu.VMEM((late, 2, 2, GRAIN, D), low),
            dma((chunks,)),
            dma((2, chunks)),
            dma,
        ]
        extra = dict(collective_id=3, has_side_effects=True)
        more = sources
    return pl.pallas_call(
        attend_back_kernel,
        grid=(passages,),
        out_shape=(
            jax.ShapeDtypeStruct((passages, span, D), low),
            table_shape,
            jax.ShapeDtypeStruct((VEC_LEN // D, D), f32),
        )
        + red_shape,
        in_specs=[
            pl.BlockSpec(memory_space=pltpu.SMEM),
            rows,
            pl.BlockSpec((3 * D, D), lambda p: (0, 0)),
            rows,
            rows,
            rows,
            pl.BlockSpec((1, HEADS, 1, span), lambda p: (p, 0, 0, 0)),
            rows,
            rows,
            pl.BlockSpec((VEC_LEN // D, D), lambda p: (0, 0)),
        ]
        + [any_spec] * len(more),
        out_specs=(
            rows,
            table_spec,
            pl.BlockSpec((VEC_LEN // D, D), lambda p: (0, 0)),
        )
        + (any_spec,) * len(red_shape),
        scratch_shapes=[pltpu.VMEM((D, span), low), pltpu.VMEM((128, span), f32)]
        + [whole] * 4
        + [pltpu.VMEM((2, span, span // 2), kind) for kind in (f32, f32, low, low)]
        + beside,
        compiler_params=pltpu.CompilerParams(vmem_limit_bytes=60 * 1024 * 1024, **extra),
        cost_estimate=pl.CostEstimate(
            flops=passages * span * (12 * D * D + 10 * D * span),
            bytes_accessed=passages * span * D * 24,
            transcendentals=passages * HEADS * span * span,
        ),
        name="attend_back",
    )(lengths, tokens, table, queries, keys, values, lse, d_ctx, d_mixed, vec_grad, *more)


ERFC_SLOPE = 0.42
ERFC_TERMS = (
    0.23681282137224371,
    0.23975548803522717,
    0.19369618325685073,
    0.27205881038432234,
    -0.136659548208163,
    0.44720921707821076,
    -0.32398587364624676,
    0.07111276080879629,
)


def gelu_pair(x):
    slope = 1.0 + (ERFC_SLOPE * math.sqrt(0.5)) * jnp.abs(x)
    t = pltpu.reciprocal(slope, approx=True)
    t = t * (2.0 - slope * t)
    bell = jnp.exp2(x * x * (-0.5 / math.log(2.0)))
    series = 0.5 * ERFC_TERMS[-1]
    for term in ERFC_TERMS[-2::-1]:
        series = series * t + 0.5 * term
    low_side = series * t * bell
    cdf = jnp.where(x < 0.0, low_side, 1.0 - low_side)
    return x * cdf, cdf + x * bell * (1.0 / math.sqrt(2.0 * math.pi))


def ffn_kernel(
    lengths_ref,
    vec_ref,
    normed_ref,
    inv_ref,
    cot_ref,
    ctx_ref,
    table_ref,
    output_ref,
    d_mixed_ref,
    d_ctx_ref,
    vec_grad_ref,
    d_out_ref,
    d_inner_ref,
    d_outer_ref,
    *refs,
):
    beside = len(refs) > 20
    if beside:
        red_ref, refs = refs[0], refs[1:]
    (
        w_out,
        w_inner,
        w_outer,
        normed,
        inv_std,
        cot,
        left_pre,
        right_pre,
        slope,
        active,
        hidden,
        output,
        d_branch,
        d_mixed,
        staged,
        staged_outer,
        load_sem,
        store_sem,
        done_sem,
        wide_sem,
        *extra,
    ) = refs
    f32, low = jnp.float32, jnp.bfloat16
    count = normed.shape[0]
    chunk = left_pre.shape[1]
    chunks = FF // chunk
    tile, strip = 256, 32
    tiles = count // tile
    sources = (
        (normed_ref, normed),
        (table_ref.at[pl.ds(4 * D + FF, FF)], w_outer),
        (cot_ref, cot),
        (inv_ref, inv_std),
        (table_ref.at[pl.ds(3 * D, D)], w_out),
        (ctx_ref, hidden),
    )
    loads = [
        pltpu.make_async_copy(src, dst, load_sem.at[slot])
        for slot, (src, dst) in enumerate(sources)
    ]
    loads[0].start()

    def columns(part):
        return pl.ds(pl.multiple_of(part * chunk, chunk), chunk)

    def load_wide(part):
        rows = pl.ds(4 * D + part * chunk, chunk)
        return pltpu.make_async_copy(
            table_ref.at[rows], w_inner.at[columns(part)], wide_sem.at[part]
        )

    for part in range(chunks):
        load_wide(part).start()
    for load in loads[1:5]:
        load.start()

    if beside:
        acc, core_land, one_land, two_land, *sems, red_sem, swap_sem = extra
        summed = PlaneSum((d_outer_ref,), OUTER_COUNTS, acc, core_land, one_land, None, None, sems)
        dp, blk = summed.place[:2]
        diagonal = (3 - blk, dp)
        greet((*summed.place[6:], diagonal))

    def vec(row):
        return vec_ref[row : row + 1]

    vec_grad_ref[...] = jnp.zeros_like(vec_grad_ref)
    loads[0].wait()

    @pl.loop(0, count // strip)
    def _(at):
        rows = pl.ds(pl.multiple_of(at * strip, strip), strip)
        hidden[rows, :] = (normed[rows, :] * vec(8) + vec(9)).astype(low)

    def widen(part, pre):
        load_wide(part).wait()
        pre[...] = contract_cols(hidden[...], w_inner[columns(part), :])

    per_row = D // chunk

    def bend(part, pre):
        bias = vec_ref[pl.ds(3 + part // per_row, 1), :]
        side = lax.rem(part, per_row)
        piece = bias[:, 0:chunk]
        for other in range(1, per_row):
            piece = jnp.where(side == other, bias[:, other * chunk : (other + 1) * chunk], piece)
        for at in range(0, count, strip):
            value, pull = gelu_pair(pre[at : at + strip] + piece)
            active[at : at + strip, columns(part)] = value.astype(low)
            slope[at : at + strip, columns(part)] = pull

    widen(0, left_pre)

    @pl.loop(0, chunks // 2 - 1)
    def _(turn):
        widen(2 * turn + 1, right_pre)
        bend(2 * turn, left_pre)
        widen(2 * turn + 2, left_pre)
        bend(2 * turn + 1, right_pre)

    widen(chunks - 1, right_pre)
    bend(chunks - 2, left_pre)
    bend(chunks - 1, right_pre)

    for load in loads[1:4]:
        load.wait()
    passages = lengths_ref.shape[0] // lax.axis_size("blk")
    per_passage = count // passages

    def put_tile(at, value):
        rows = slice(at % 2 * tile, (at % 2 + 1) * tile)
        left_pre[rows] = value[:, 0:chunk]
        right_pre[rows] = value[:, chunk:]

    def get_strip(at, inner_at):
        first = at % 2 * tile + inner_at
        rows = slice(first, first + strip)
        return jnp.concatenate([left_pre[rows], right_pre[rows]], axis=1)

    def narrow(at):
        return jnp.dot(active[at * tile : (at + 1) * tile], w_outer[...], preferred_element_type=f32)

    def sums(totals, values):
        return [
            total + jnp.sum(value, axis=0, keepdims=True) for total, value in zip(totals, values)
        ]

    nothing = [jnp.zeros((1, D), f32)] * 3
    totals = nothing
    for at in range(tiles):
        put_tile(at, narrow(at))
        passage = at * tile // per_passage
        length = lengths_ref[lax.axis_index("blk") * passages + passage]
        for inner_at in range(0, tile, strip):
            first = at * tile + inner_at
            rows = slice(first, first + strip)
            mixed = normed[rows] * vec(8) + vec(9) + (
                get_strip(at, inner_at) + vec(7)
            )
            normed_two, inv_two = norm_rows(mixed)
            local = first - passage * per_passage
            output[passage, local : local + strip] = (normed_two * vec(10) + vec(11)).astype(low)
            position = local + lax.broadcasted_iota(
                jnp.int32, (strip, 1), 0
            )
            grad_out = jnp.where(position < length, cot[rows].astype(f32), 0.0)
            d_mixed_two = norm_back(grad_out * vec(10), normed_two, inv_two)
            d_mixed[rows] = d_mixed_two
            low_branch = d_mixed_two.astype(low)
            d_branch[rows] = low_branch
            totals = sums(totals, (grad_out * normed_two, grad_out, low_branch.astype(f32)))
    for row, total in zip((10, 11, 7), totals):
        vec_grad_ref[row : row + 1] = total
    if beside:
        blk = lax.axis_index("blk")
        pl.semaphore_wait(pltpu.get_barrier_semaphore(), 4)
        span = output_ref.shape[1]
        there = output_ref.at[pl.ds(blk * passages, passages)]
        given = [
            remote_copy(output.at[:, pl.ds(peer[0] * span, span)], there, swap_sem, slot, peer)
            for slot, peer in enumerate((*summed.place[7:], diagonal))
        ]
        own_piece = output.at[:, pl.ds(blk * span, span)]
        given.append(pltpu.make_async_copy(own_piece, there, done_sem.at[0]))
    else:
        given = [pltpu.make_async_copy(output, output_ref, done_sem.at[0])]
    for copy in given:
        copy.start()

    order = plane_order(chunks)

    def store(turn, side):
        part, slot = order(turn), lax.rem(turn, 2)
        if side == 0:
            return pltpu.make_async_copy(
                staged_outer.at[slot], d_outer_ref.at[part], store_sem.at[slot, 0]
            )
        rows = pl.ds(part * chunk, chunk)
        return pltpu.make_async_copy(staged.at[slot], d_inner_ref.at[rows], store_sem.at[slot, 1])

    tasks = {}
    if beside:

        tasks = {
            2: lambda: summed.begin([0]),
            4: lambda: (summed.paired([0]), summed.begin([1])),
            6: lambda: (summed.paired([1]), summed.begin([2])),
        }

    @pl.loop(0, chunks)
    def _(turn):
        part, slot = order(turn), lax.rem(turn, 2)
        cols = columns(part)
        left_pre[...] = contract_cols(d_branch[...], w_outer[cols, :])
        outer_rows = contract_rows(active[:, cols], d_branch[...]).astype(low)
        staged_outer[slot] = outer_rows.reshape(staged_outer.shape[1:])
        total = jnp.zeros((1, chunk), f32)
        for at in range(0, count, strip):
            d_pre = (left_pre[at : at + strip] * slope[at : at + strip, cols]).astype(low)
            active[at : at + strip, cols] = d_pre
            total = total + jnp.sum(d_pre.astype(f32), axis=0, keepdims=True)
        bias_row = pl.ds(3 + part // per_row, 1)
        side_at = lax.rem(part, per_row)
        for other in range(per_row):
            lanes = slice(other * chunk, (other + 1) * chunk)
            vec_grad_ref[bias_row, lanes] += jnp.where(side_at == other, total, 0.0)
        staged[slot] = contract_rows(active[:, cols], hidden[...]).astype(low)
        for side in range(2):
            store(turn, side).start()

        @pl.when(turn >= 1)
        def _():
            for side in range(2):
                store(turn - 1, side).wait()

        for at in sorted(tasks):
            run_when(turn == at, tasks[at])

    for side in range(2):
        store(chunks - 1, side).wait()
    if beside:
        summed.begin([3])
        summed.paired([2])
    loads[5].start()
    loads[4].wait()
    ctx, d_attn, d_ctx = hidden, d_branch, cot
    totals = nothing
    for at in range(tiles):
        span = slice(at * tile, (at + 1) * tile)
        put_tile(at, jnp.dot(active[span], w_inner[...], preferred_element_type=f32))
        for inner_at in range(0, tile, strip):
            first = at * tile + inner_at
            rows = slice(first, first + strip)
            d_hidden = d_mixed[rows] + get_strip(at, inner_at)
            normed_one = normed[rows]
            d_mixed_one = norm_back(d_hidden * vec(8), normed_one, inv_std[rows, 0:1])
            d_mixed[rows] = d_mixed_one
            low_attn = d_mixed_one.astype(low)
            d_attn[rows] = low_attn
            totals = sums(totals, (d_hidden * normed_one, d_hidden, low_attn.astype(f32)))
        d_ctx[span] = contract_cols(d_attn[span], w_out[...]).astype(low)
        if beside and at == 0:
            summed.paired([3])
        if beside and at == 2:
            summed.half_settled([0, 1], red_ref, red_sem)
    for row, total in zip((8, 9, 2), totals):
        vec_grad_ref[row : row + 1] = total
    results = [
        pltpu.make_async_copy(d_ctx, d_ctx_ref, done_sem.at[1]),
        pltpu.make_async_copy(d_mixed, d_mixed_ref, done_sem.at[2]),
    ]
    for copy in results:
        copy.start()
    half = staged.shape[1]
    loads[5].wait()
    for side in range(2):
        rows = slice(side * half, (side + 1) * half)
        staged[side] = contract_rows(ctx[:, rows], d_attn[...]).astype(low)
        copy = pltpu.make_async_copy(staged.at[side], d_out_ref.at[rows], done_sem.at[3 + side])
        copy.start()
        results.append(copy)
    if beside:
        summed.half_settled([2, 3], red_ref, red_sem)
        results += [summed.kept(slot, red_ref, red_sem) for slot in range(4)]
    for copy in given + results:
        copy.wait()


def ffn(lengths, normed, inv_std, cotangent, context, vec_rows, table, passages, beside):
    f32, low = jnp.float32, jnp.bfloat16
    count = normed.shape[0]
    shares = (4 * passages, count // passages // 4) if beside else (passages, count // passages)
    chunk = 8 * GRAIN
    any_spec = pl.BlockSpec(memory_space=pl.ANY)
    vmem = pl.BlockSpec(memory_space=pltpu.VMEM)
    dma = pltpu.SemaphoreType.DMA
    whole = lambda width, kind=low: pltpu.VMEM((count, width), kind)
    granules = FF // chunk
    more_shape, more, extra = (), [], {}
    if beside:
        more_shape = (jax.ShapeDtypeStruct((granules, 2, GRAIN, D), low),)
        more = PlaneSum.scratch(OUTER_COUNTS, with_part=False)
        more[3] = pltpu.VMEM((1, GRAIN, D), low)
        more += [dma((4,)), dma((2, 3))]
        extra = dict(collective_id=4, has_side_effects=True)
    return pl.pallas_call(
        ffn_kernel,
        out_shape=(
            jax.ShapeDtypeStruct((*shares, D), low),
            jax.ShapeDtypeStruct((count, D), f32),
            jax.ShapeDtypeStruct((count, D), low),
            jax.ShapeDtypeStruct((VEC_LEN // D, D), f32),
            jax.ShapeDtypeStruct((D, D), low),
            jax.ShapeDtypeStruct((FF, D), low),
            jax.ShapeDtypeStruct((granules, 2, 2, 2, GRAIN, D), low),
        )
        + more_shape,
        in_specs=[pl.BlockSpec(memory_space=pltpu.SMEM), vmem] + [any_spec] * 5,
        out_specs=(any_spec, any_spec, any_spec, vmem)
        + (any_spec,) * (3 + len(more_shape)),
        scratch_shapes=[
            pltpu.VMEM((D, D), low),
            pltpu.VMEM((FF, D), low),
            pltpu.VMEM((FF, D), low),
            whole(D, f32),
            whole(128, f32),
            whole(D),
            whole(chunk, f32),
            whole(chunk, f32),
            whole(FF, f32),
            whole(FF),
            whole(D),
            pltpu.VMEM((passages, count // passages, D), low),
            whole(D),
            whole(D, f32),
            pltpu.VMEM((2, chunk, D), low),
            pltpu.VMEM((2, 2, 2, 2, GRAIN, D), low),
            dma((6,)),
            dma((2, 2)),
            dma((5,)),
            dma((granules,)),
        ]
        + more,
        compiler_params=pltpu.CompilerParams(vmem_limit_bytes=63 * 1024 * 1024, **extra),
        cost_estimate=pl.CostEstimate(
            flops=count * (12 * D * FF + 4 * D * D),
            bytes_accessed=2 * (14 * D * D + 14 * D * count),
            transcendentals=count * FF,
        ),
        name="ffn",
    )(lengths, vec_rows, normed, inv_std, cotangent, context, table)


def paired(own_rows, dp_count, blk_count):
    return blk_count == 4 and dp_count % 2 == 0 and own_rows % 384 == 0


def swap_in(rows):
    return lax.all_to_all(rows, "blk", split_axis=0, concat_axis=1, tiled=True)


def swap_out(rows):
    return lax.all_to_all(rows, "blk", split_axis=1, concat_axis=0, tiled=True)


def pick_blocks(blocks, order):
    return jnp.concatenate(
        [lax.dynamic_index_in_dim(blocks, order[i], 0) for i in range(blocks.shape[0])], axis=0
    )


def body(
    tokens,
    cotangent,
    lengths,
    owners,
    master,
    moment_one,
    moment_two,
    vectors,
    vector_one,
    vector_two,
):
    dp_count = lax.axis_size("dp")
    blk_count = lax.axis_size("blk")
    blk = lax.axis_index("blk")
    own_rows = master.shape[0]
    grain = math.gcd(own_rows, D)
    part = grain // blk_count
    own_grains = own_rows // grain
    fast = paired(own_rows, dp_count, blk_count)
    if fast:
        full = own_rows * 2 // 9
        tokens, cotangent, table, *attended, vec_rows = enter(
            dp_count // 2, full, owners, tokens, cotangent, master, lengths, vectors
        )
    else:
        own_part = lax.dynamic_index_in_dim(
            master.reshape(own_grains, blk_count, part, D), blk, 1, keepdims=False
        ).astype(jnp.bfloat16)
        part_blocks = lax.all_gather(own_part, "dp", axis=0)
        part_table = pick_blocks(part_blocks, jnp.argsort(owners)).reshape(dp_count * own_grains, part, D)
        tokens = swap_in(tokens)
        cotangent = swap_in(cotangent)

        rows = lax.all_gather(part_table, "blk", axis=1)
        table = rows.reshape(-1, D)
        vec_rows = vectors.reshape(-1, D)
        attended = attend(lengths, tokens, table, vec_rows)
    queries, keys, values, log_total, context, normed_one, inv_one = attended
    passages, span_len, _ = tokens.shape
    tok_rows = passages * span_len
    flat = lambda rows: rows.reshape(tok_rows, -1)
    output, d_mixed_one, d_context, grad_vector, d_w_out, d_w_inner, d_w_outer, *outer_red = ffn(
        lengths,
        flat(normed_one),
        flat(inv_one),
        flat(cotangent),
        flat(context),
        vec_rows,
        table,
        passages,
        fast,
    )
    split = lambda g: g.reshape(-1, 2, 2, 2, GRAIN, D)
    d_tokens, d_w_qkv, grad_vector, *back = attend_back(
        lengths,
        tokens,
        table,
        queries,
        keys,
        values,
        log_total,
        d_context.reshape(passages, span_len, D),
        d_mixed_one.reshape(passages, span_len, D),
        grad_vector,
        [split(d_w_out), split(d_w_inner), *outer_red] if fast else (),
    )

    def own_parts(rows):
        split = rows.astype(jnp.bfloat16).reshape(-1, blk_count, part, D)
        return lax.psum_scatter(split, "blk", scatter_dimension=1)

    if fast:
        own_block, vector_sum, norms, grad_tokens = tail(
            dp_count // 2, owners, d_w_qkv, back[0], grad_vector, d_tokens
        )
        grad_norm = norms[0, 0]
        vector_sum = vector_sum.reshape(-1)
    else:
        output, grad_tokens = swap_out(output), swap_out(d_tokens)
        part_grads = jnp.concatenate(
            [own_parts(d_w_qkv), own_parts(d_w_out), own_parts(d_w_inner), own_parts(d_w_outer.reshape(FF, D))],
            axis=0,
        )
        ordered = pick_blocks(part_grads.reshape(dp_count, own_grains, part, D), owners)
        own_grad = lax.psum_scatter(ordered, "dp", scatter_dimension=0)
        own_f32 = own_grad.astype(jnp.float32)
        own_block = lax.all_gather(own_grad, "blk", axis=1).reshape(own_rows, D)
        vector_sum = lax.psum(grad_vector, ("dp", "blk"))
        squares = lax.psum(jnp.sum(own_f32 * own_f32), ("dp", "blk"))
        vector_sum = vector_sum.reshape(-1)
        grad_norm = jnp.sqrt(squares + jnp.sum(vector_sum * vector_sum))
    factor = jnp.minimum(1.0, clip_norm / (grad_norm + 1e-06))
    own_grad = own_block.astype(jnp.float32) * factor
    new_vectors, new_vone, new_vtwo = adamw(
        vectors, vector_one, vector_two, vector_sum * factor, 0.0, vector_rate
    )
    new_master, new_one, new_two = adamw(
        master, moment_one, moment_two, own_grad, weight_decay, learn_rate
    )
    return (
        output,
        grad_tokens,
        grad_norm,
        new_master,
        new_one,
        new_two,
        new_vectors,
        new_vone,
        new_vtwo,
    )


def solution(mesh):
    in_specs = (
        P("dp", "blk", None),
        P("dp", "blk", None),
        P("dp"),
        P(),
        P("dp", None),
        P("dp", None),
        P("dp", None),
        P(),
        P(),
        P(),
    )
    out_specs = (
        P("dp", "blk", None),
        P("dp", "blk", None),
        P(),
        P("dp", None),
        P("dp", None),
        P("dp", None),
        P(),
        P(),
        P(),
    )
    return jax.shard_map(body, mesh=mesh, in_specs=in_specs, out_specs=out_specs, check_vma=False)
```

```python
import functools
import math

import jax
import jax.numpy as jnp
from jax import lax
from jax.experimental import pallas as pl
from jax.experimental.pallas import tpu as pltpu
from jax.sharding import PartitionSpec as P

D = 768
HEADS = 12
HEAD_DIM = 64
FF = 3072
STEP = 10
VEC_LEN = 8 * D + FF


beta_one = 0.5
beta_two = 0.5
learn_rate = 0.05
vector_rate = 0.3
weight_decay = 0.01
adam_eps = 1e-08
clip_norm = 1.0


def norm_back(d_normed, normed, inv_std):
    first_mean = jnp.mean(d_normed, axis=-1, keepdims=True)
    second_mean = jnp.mean(d_normed * normed, axis=-1, keepdims=True)
    return inv_std * (d_normed - first_mean - normed * second_mean)


def contract_rows(left, right):
    return lax.dot_general(
        left, right, (((0,), (0,)), ((), ())), preferred_element_type=jnp.float32
    )


def contract_cols(left, right):
    return lax.dot_general(
        left, right, (((1,), (1,)), ((), ())), preferred_element_type=jnp.float32
    )


def adamw(weight, first, second, grad, decay, rate):
    new_first = beta_one * first + (1.0 - beta_one) * grad
    new_second = beta_two * second + (1.0 - beta_two) * grad * grad
    direction = (
        new_first
        / (1.0 - beta_one**STEP)
        / (jnp.sqrt(new_second / (1.0 - beta_two**STEP)) + adam_eps)
    )
    return (weight - rate * (direction + decay * weight), new_first, new_second)


MESH = pl.DeviceIdType.MESH
GRAIN = 48
OUTER_COUNTS = (8,)
BACK_COUNTS = (2, 8)
QKV_COUNTS = (6,)


def add_low(left, right):
    return (left.astype(jnp.float32) + right.astype(jnp.float32)).astype(jnp.bfloat16)


def enter_kernel(
    nz,
    full,
    owners_ref,
    tokens_ref,
    cot_ref,
    master_ref,
    lengths_ref,
    lanes_ref,
    tokens_out,
    cot_out,
    table_out,
    q_out,
    k_out,
    v_out,
    lse_out,
    ctx_out,
    normed_out,
    inv_out,
    vec_ref,
    wide,
    own_wide,
    tokens_land,
    cot_land,
    whole_out,
    quarter_out,
    ordered,
    load_sem,
    swap_sem,
    keep_sem,
    z_sem,
    one_sem,
    two_sem,
    sib_sem,
    sib_own_sem,
    out_sem,
    q_all,
    k_all,
    v_all,
    v_turned,
    lse_all,
    ctx_all,
    normed_all,
    inv_all,
    ctx_turned,
    scores,
    weights,
    work_sem,
):
    dp, blk, z, c, y, x, sibling, x_peer, y_peer = place_of()
    diagonal = (3 - blk, dp)
    passages, span = tokens_out.shape[0], tokens_ref.shape[1]
    quarter = quarter_out.shape[4]
    low_whole, low_quarter = whole_out.at[dp], quarter_out.at[dp]

    own_rows = pl.ds(pl.multiple_of(full + blk * 2 * quarter, 16), 2 * quarter)
    loads = [
        pltpu.make_async_copy(master_ref.at[own_rows], own_wide, load_sem.at[0]),
        pltpu.make_async_copy(master_ref, wide, load_sem.at[1]),
    ]
    for load in loads:
        load.start()
    own_copies = []
    for slot, (rows_in, rows_out) in enumerate(((tokens_ref, tokens_land), (cot_ref, cot_land))):
        own_copies.append(
            pltpu.make_async_copy(
                rows_in.at[pl.ds(blk * passages, passages)],
                rows_out.at[:, pl.ds(blk * span, span)],
                keep_sem.at[slot],
            )
        )
        own_copies[-1].start()

    for row in range(VEC_LEN // D):
        for col in range(D // 128):
            at = row * (D // 128) + col
            vec_ref[row : row + 1, col * 128 : (col + 1) * 128] = lanes_ref[at : at + 1]

    barrier = pltpu.get_barrier_semaphore()
    for partner in (sibling, x_peer, y_peer, diagonal):
        pl.semaphore_signal(barrier, inc=1, device_id=partner, device_id_type=MESH)
    below, above = z > 0, z < nz - 1

    @pl.when(below)
    def _():
        pl.semaphore_signal(barrier, inc=1, device_id=(blk, dp - 2), device_id_type=MESH)

    @pl.when(above)
    def _():
        pl.semaphore_signal(barrier, inc=1, device_id=(blk, dp + 2), device_id_type=MESH)

    pl.semaphore_wait(barrier, 4 + jnp.where(below, 1, 0) + jnp.where(above, 1, 0))

    def remote(src, dst, sems, slot, device):
        return pltpu.make_async_remote_copy(
            src_ref=src,
            dst_ref=dst,
            send_sem=sems.at[(0, *slot)],
            recv_sem=sems.at[(1, *slot)],
            device_id=device,
            device_id_type=MESH,
        )

    def swap(which, rows_in, rows_out, peer, slot):
        return remote(
            rows_in.at[pl.ds(peer[0] * passages, passages)],
            rows_out.at[:, pl.ds(blk * span, span)],
            swap_sem,
            (which, slot),
            peer,
        )

    swaps = [
        swap(which, rows_in, rows_out, peer, slot)
        for which, (rows_in, rows_out) in enumerate(((tokens_ref, tokens_land), (cot_ref, cot_land)))
        for slot, peer in enumerate((x_peer, y_peer, diagonal))
    ]
    loads[0].wait()
    for half in range(2):
        quarter_out[dp, y, x, half] = own_wide[half * quarter : (half + 1) * quarter].astype(
            jnp.bfloat16
        )

    def pass_on(src_quarter, src_whole, at, upward, which):
        device = (blk, dp + 2 if upward else dp - 2)
        way = 0 if upward else 1
        if which == 0:
            return remote(src_quarter, quarter_out.at[at, y, x], z_sem, (way, 0, at // 2), device)
        return remote(src_whole, whole_out.at[at], z_sem, (way, 1, at // 2), device)

    @pl.when(above)
    def _():
        pass_on(low_quarter.at[y, x], None, dp, True, 0).start()

    @pl.when(below)
    def _():
        pass_on(low_quarter.at[y, x], None, dp, False, 0).start()

    for copy in swaps[:3]:
        copy.start()
    loads[1].wait()
    whole_out[dp] = wide[0:full].astype(jnp.bfloat16)
    for part in range(8):

        @pl.when(blk != part // 2)
        def _(part=part):
            start = full + part * quarter
            quarter_out[dp, part // 4, part // 2 % 2, part % 2] = wide[
                start : start + quarter
            ].astype(jnp.bfloat16)

    def own_whole(turn):
        @pl.when(jnp.logical_and(above, z + 1 == turn))
        def _():
            pass_on(None, low_whole, dp, True, 1).start()

        @pl.when(jnp.logical_and(below, nz - z == turn))
        def _():
            pass_on(None, low_whole, dp, False, 1).start()

    sib_own = [
        remote(low_quarter, quarter_out.at[dp], sib_own_sem, (0,), sibling),
        remote(low_whole, whole_out.at[dp], sib_own_sem, (1,), sibling),
    ]
    for copy in sib_own:
        copy.start()
    def sources(act):
        def at_distance(distance):
            @pl.when(z >= distance)
            def _():
                act(dp - 2 * distance, True, z < nz - 1)

            @pl.when(z + distance < nz)
            def _():
                act(dp + 2 * distance, False, z > 0)

        return at_distance

    def forward(ref_view, at, slot):
        return remote(ref_view, ref_view, sib_sem, (slot, at // 2), sibling)

    def one_x(at):
        view = quarter_out.at[at, y, x, 0]
        return remote(view, view, one_sem, (0, at // 2), x_peer)

    def one_y(at):
        view = quarter_out.at[at, y, x, 1]
        return remote(view, view, one_sem, (1, at // 2), y_peer)

    def two_y(at):
        view = quarter_out.at[at, y, :, 0]
        return remote(view, view, two_sem, (0, at // 2), y_peer)

    def two_x(at):
        view = quarter_out.at[at, :, x, 1]
        return remote(view, view, two_sem, (1, at // 2), x_peer)

    def sib_views(at):
        return [
            quarter_out.at[at, y, x],
            quarter_out.at[at, y, 1 - x, 0],
            quarter_out.at[at, 1 - y, x, 1],
            quarter_out.at[at, 1 - y, :, 0],
            quarter_out.at[at, :, 1 - x, 1],
            whole_out.at[at],
        ]

    def quarter_came(at, upward, onward):
        view = quarter_out.at[at, y, x]
        pass_on(view, None, at, upward, 0).wait_recv()

        @pl.when(onward)
        def _():
            pass_on(view, None, at, upward, 0).start()

        one_x(at).start()
        one_y(at).start()
        forward(sib_views(at)[0], at, 0).start()

    def whole_came(at, upward, onward):
        view = whole_out.at[at]
        pass_on(None, view, at, upward, 1).wait_recv()

        @pl.when(onward)
        def _():
            pass_on(None, view, at, upward, 1).start()

        forward(sib_views(at)[5], at, 5).start()

    def one_came(at, upward, onward):
        one_x(at).wait_recv()
        two_y(at).start()
        forward(sib_views(at)[1], at, 1).start()
        one_y(at).wait_recv()
        two_x(at).start()
        forward(sib_views(at)[2], at, 2).start()

    def two_came(at, upward, onward):
        two_y(at).wait_recv()
        forward(sib_views(at)[3], at, 3).start()
        two_x(at).wait_recv()
        forward(sib_views(at)[4], at, 4).start()

    def finished(at, upward, onward):
        view = quarter_out.at[at, y, x]

        @pl.when(onward)
        def _():
            pass_on(view, None, at, upward, 0).wait_send()
            pass_on(None, whole_out.at[at], at, upward, 1).wait_send()

        one_x(at).wait_send()
        one_y(at).wait_send()
        two_x(at).wait_send()
        two_y(at).wait_send()
        for slot, ref_view in enumerate(sib_views(at)):
            copy = forward(ref_view, at, slot)
            copy.wait_send()
            copy.wait_recv()

    for distance in range(1, nz):
        sources(quarter_came)(distance)
        if distance == nz - 1:
            sources(one_came)(1)
        own_whole(distance)
    plan = [(whole_came, 1)] + [(one_came, d) for d in range(2, nz)]
    for distance in range(2, nz):
        plan += [(whole_came, distance), (two_came, distance - 1)]
    plan += [(two_came, nz - 1)]
    for act, distance in plan:
        sources(act)(distance)
    for distance in range(1, nz):
        sources(finished)(distance)

    @pl.when(above)
    def _():
        pass_on(low_quarter.at[y, x], None, dp, True, 0).wait_send()
        pass_on(None, low_whole, dp, True, 1).wait_send()

    @pl.when(below)
    def _():
        pass_on(low_quarter.at[y, x], None, dp, False, 0).wait_send()
        pass_on(None, low_whole, dp, False, 1).wait_send()

    for copy in swaps[3:]:
        copy.start()
    for copy in own_copies[:1] + swaps[:3] + sib_own:
        copy.wait()
    stores = [pltpu.make_async_copy(tokens_land, tokens_out, out_sem.at[2 * nz])]
    stores[0].start()

    def put(block):
        place = 0
        for index in range(2 * nz):
            place = jnp.where(owners_ref[index] == block, index, place)
        rows = wide.shape[0]
        base = block * rows
        ordered[base : base + full] = whole_out[place]
        for part in range(8):
            start = base + full + part * quarter
            ordered[start : start + quarter] = quarter_out[
                place, part // 4, part // 2 % 2, part % 2
            ]
        table = pl.ds(base, rows)
        return pltpu.make_async_copy(ordered.at[table], table_out.at[table], out_sem.at[block])

    early = -(-4 * D // wide.shape[0])
    for block in range(early):
        stores.append(put(block))
        stores[-1].start()

    results = []

    def give(src, dst):
        copy = pltpu.make_async_copy(src, dst, work_sem.at[len(results)])
        results.append(copy)
        return copy

    for p in range(passages):
        project(
            tokens_land[p], ordered, vec_ref, q_all.at[p], k_all.at[p], v_all.at[p], v_turned.at[p]
        )
    for src, dst in ((q_all, q_out), (k_all, k_out), (v_all, v_out)):
        give(src, dst).start()
    pairs = HEADS // 2
    lengths = [lengths_ref[blk * passages + p] for p in range(passages)]

    def finish(p):
        first_norm(
            tokens_land[p], ctx_all[p], ordered, vec_ref, normed_all.at[p], inv_all.at[p]
        )
        for src, dst in (
            (ctx_all, ctx_out),
            (normed_all, normed_out),
            (inv_all, inv_out),
            (lse_all, lse_out),
        ):
            give(src.at[p], dst.at[p]).start()

    for p in range(passages):

        @pl.loop(0, pairs)
        def _(pair, p=p):
            for slot in range(pairs):
                block = early + p * pairs + slot
                if block < 2 * nz:

                    @pl.when(pair == slot)
                    def _(block=block):
                        put(block).start()

            attend_pair(
                pair,
                lengths[p],
                q_all.at[p],
                k_all.at[p],
                v_turned.at[p],
                lse_all.at[p],
                ctx_all.at[p],
                ctx_turned,
                scores,
                weights,
            )

        if p == passages - 1:
            for copy in own_copies[1:] + swaps[3:]:
                copy.wait()
            give(cot_land, cot_out).start()
        finish(p)
    for block in range(early, 2 * nz):
        table = pl.ds(block * wide.shape[0], wide.shape[0])
        stores.append(
            pltpu.make_async_copy(ordered.at[table], table_out.at[table], out_sem.at[block])
        )
    for copy in stores + results:
        copy.wait()


def enter(nz, full, owners, tokens, cotangent, master, lengths, vectors):
    f32, low = jnp.float32, jnp.bfloat16
    rows = master.shape[0]
    quarter = (rows - full) // 8
    shares, span, _ = tokens.shape
    passages, span = shares // 4, 4 * span
    swapped = (passages, span, D)
    any_spec = pl.BlockSpec(memory_space=pl.ANY)
    smem = pl.BlockSpec(memory_space=pltpu.SMEM)
    dma = pltpu.SemaphoreType.DMA
    shape = lambda kind: jax.ShapeDtypeStruct(swapped, kind)
    lse = (passages, HEADS, 1, span)
    return pl.pallas_call(
        functools.partial(enter_kernel, nz, full),
        out_shape=(
            shape(low),
            shape(low),
            jax.ShapeDtypeStruct((2 * nz * rows, D), low),
            shape(low),
            shape(low),
            shape(low),
            jax.ShapeDtypeStruct(lse, f32),
            shape(low),
            shape(f32),
            jax.ShapeDtypeStruct((passages, span, 128), f32),
            jax.ShapeDtypeStruct((VEC_LEN // D, D), f32),
        ),
        in_specs=[smem] + [any_spec] * 3 + [smem, pl.BlockSpec(memory_space=pltpu.VMEM)],
        out_specs=[any_spec] * 10 + [pl.BlockSpec(memory_space=pltpu.VMEM)],
        scratch_shapes=[
            pltpu.VMEM((rows, D), f32),
            pltpu.VMEM((2 * quarter, D), f32),
            pltpu.VMEM(swapped, low),
            pltpu.VMEM(swapped, low),
            pltpu.VMEM((2 * nz, full, D), low),
            pltpu.VMEM((2 * nz, 2, 2, 2, quarter, D), low),
            pltpu.VMEM((2 * nz * rows, D), low),
            dma((2,)),
            dma((2, 2, 3)),
            dma((2,)),
            dma((2, 2, 2, nz)),
            dma((2, 2, nz)),
            dma((2, 2, nz)),
            dma((2, 6, nz)),
            dma((2, 2)),
            dma((2 * nz + 1,)),
            pltpu.VMEM(swapped, low),
            pltpu.VMEM(swapped, low),
            pltpu.VMEM(swapped, low),
            pltpu.VMEM((passages, D, span), low),
            pltpu.VMEM(lse, f32),
            pltpu.VMEM(swapped, low),
            pltpu.VMEM(swapped, f32),
            pltpu.VMEM((passages, span, 128), f32),
            pltpu.VMEM((128, span), f32),
            pltpu.VMEM((2, span, span // 2), f32),
            pltpu.VMEM((2, span, span // 2), low),
            dma((4 + 4 * passages,)),
        ],
        compiler_params=pltpu.CompilerParams(
            collective_id=2, has_side_effects=True, vmem_limit_bytes=60 * 1024 * 1024
        ),
        cost_estimate=pl.CostEstimate(
            flops=passages * span * (8 * D * D + 4 * D * span),
            bytes_accessed=6 * 10**7,
            transcendentals=passages * HEADS * span * span,
        ),
        name="enter",
    )(owners, tokens, cotangent, master, lengths, vectors.reshape(-1, 128))


def tail_kernel(
    nz,
    owners_ref,
    qkv_ref,
    back_ref,
    vec_ref,
    d_tokens_ref,
    own_ref,
    vec_sum_ref,
    norm_ref,
    d_tokens_out,
    acc,
    land_one,
    land_two,
    one_sem,
    two_sem,
    late_sem,
    part,
    mine,
    up_land,
    down_land,
    up_send,
    down_send,
    own_part,
    assembled,
    vec_send,
    vec_land,
    sq_send,
    sq_land,
    part_sem,
    up_sem,
    down_sem,
    gather_sem,
    vec_sem,
    sq_sem,
    out_sem,
    *swap_refs,
):
    dp, blk, z, c, y, x, sibling, x_peer, y_peer = place_of()

    def z_peer(hop):
        return (blk, 2 * lax.rem(z + hop, nz) + c)

    def send(src, dst, sems, slot, device):
        copy = remote_copy(src, dst, sems, slot, device)
        copy.start()
        return copy

    swaps = [
        PositionSwap(d_tokens_ref, d_tokens_out, *swap_refs),
    ]
    partners = [sibling, x_peer, y_peer, swaps[0].diagonal] + [z_peer(h) for h in range(1, nz)]
    barrier = greet(partners)
    late = qkv_ref.shape[0]
    load = pltpu.make_async_copy(back_ref, part.at[pl.ds(late, back_ref.shape[0])], part_sem)
    load.start()
    late_load = pltpu.make_async_copy(qkv_ref, acc, late_sem)
    late_load.start()
    sems = (None, None, one_sem, two_sem)
    summed = PlaneSum((), QKV_COUNTS, acc, None, land_one, land_two, part, sems)
    slots = range(len(summed.chunks))
    for row in range(VEC_LEN // D):
        for col in range(D // 128):
            at = row * (D // 128) + col
            vec_send[0, at : at + 1] = vec_ref[row : row + 1, col * 128 : (col + 1) * 128]
    late_load.wait()
    pl.semaphore_wait(barrier, len(partners))
    for slot in slots:
        summed.one(slot).start()

    def vec_copy(turn):
        peer = (sibling, x_peer, y_peer)[turn]
        return remote_copy(vec_send.at[turn], vec_land.at[turn], vec_sem, turn, peer)

    def vec_next(turn):
        vec_copy(turn).wait()
        vec_send[turn + 1] = vec_send[turn] + vec_land[turn]
        if turn < 2:
            vec_copy(turn + 1).start()

    vec_copy(0).start()
    vec_next(0)
    vec_next(1)
    vec_next(2)
    vec_z = [
        send(vec_send.at[3], vec_land.at[3 + z], vec_sem, 2 + hop, z_peer(hop))
        for hop in range(1, nz)
    ]
    summed.crossed(slots)
    load.wait()
    summed.settled(slots)
    for swap in swaps:
        swap.begin()

    grains = part.shape[0] // (2 * nz)
    for block in range(2 * nz):
        place = owners_ref[block] * grains
        for g in range(grains):
            mine[block, g] = part[place + g]

    def gather(turn, piece):
        views = (
            (own_part.at[1 - c, piece], assembled.at[piece, c, y, x], sibling),
            (assembled.at[piece, 0, y, x], assembled.at[piece, 0, y, x], x_peer),
            (assembled.at[piece, 1, y, x], assembled.at[piece, 1, y, x], y_peer),
            (assembled.at[piece, 0, y], assembled.at[piece, 0, y], y_peer),
            (assembled.at[piece, 1, :, x], assembled.at[piece, 1, :, x], x_peer),
        )
        src, dst, peer = views[turn]
        return remote_copy(src, dst, gather_sem, turn * grains + piece, peer)

    def chain(zv):
        unit, wait = 3.0, 2.5
        steps, copies = [], []

        def message(upward, d, piece):
            land, sends, sems = (
                (up_land, up_send, up_sem) if upward else (down_land, down_send, down_sem)
            )
            target = (blk, dp + 2 if upward else dp - 2)
            return remote_copy(
                sends.at[d, piece], land.at[d, piece], sems, d * grains + piece, target
            )

        def passing(upward, d, piece):
            def run():
                land, sends = (up_land, up_send) if upward else (down_land, down_send)
                fed = zv > 0 if upward else zv < nz - 1
                copy = message(upward, d, piece)
                if fed:
                    copy.wait_recv()
                for j in range(2):
                    value = mine[2 * d + j, piece]
                    if fed:
                        value = add_low(value, land[d, piece, j])
                    sends[d, piece, j] = value
                copy.start()
                copies.append(copy)

            return run

        def arrived(piece):
            if zv > 0:
                message(True, zv, piece).wait_recv()
            if zv < nz - 1:
                message(False, zv, piece).wait_recv()
            squares = jnp.zeros((8, D), jnp.float32)
            for j in range(2):
                value = mine[2 * zv + j, piece].astype(jnp.float32)
                if zv > 0:
                    value = value + up_land[zv, piece, j].astype(jnp.float32)
                if zv < nz - 1:
                    value = value + down_land[zv, piece, j].astype(jnp.float32)
                rounded = value.astype(jnp.bfloat16)
                own_part[j, piece] = rounded
                again = rounded.astype(jnp.float32)
                squares = squares + jnp.sum((again * again).reshape(-1, 8, D), axis=0)
            total = squares[:, 0:128]
            for col in range(1, D // 128):
                total = total + squares[:, col * 128 : (col + 1) * 128]
            sq_send[0] = total if piece == 0 else sq_send[0] + total
            assembled[piece, c, y, x] = own_part[c, piece]
            gather(0, piece).start()

        def over_pair(piece):
            gather(0, piece).wait()
            gather(1, piece).start()
            gather(2, piece).start()

        def over_plane(piece):
            gather(1, piece).wait()
            gather(3, piece).start()
            gather(2, piece).wait()
            gather(4, piece).start()

        for piece in range(grains):
            first = piece * (nz - 1)
            for d in range(zv + 1, nz):
                at = (zv + first + nz - 1 - d) * unit + zv * wait
                steps.append((at, passing(True, d, piece)))
            for d in range(zv):
                at = (nz - 1 - zv + first + d) * unit + (nz - 1 - zv) * wait
                steps.append((at, passing(False, d, piece)))
            end = (first + nz - 1) * unit + (nz - 1) * wait
            steps.append((end, functools.partial(arrived, piece)))
            if piece < grains - 1:
                steps.append((end + 5.0, functools.partial(over_pair, piece)))
                steps.append((end + 9.5, functools.partial(over_plane, piece)))
        for _, step in sorted(steps, key=lambda entry: entry[0]):
            step()
        for copy in copies:
            copy.wait_send()
        sq = remote_copy(sq_send.at[0], sq_land.at[0], sq_sem, 0, sibling)
        sq.start()
        over_pair(grains - 1)
        sq.wait()

    for zv in range(nz):
        run_when(z == zv, functools.partial(chain, zv))

    for swap in swaps:
        swap.passed()
    sq_send[1] = sq_send[0] + sq_land[0]
    sq = send(sq_send.at[1], sq_land.at[1], sq_sem, 1, x_peer)
    sq.wait()
    sq_send[2] = sq_send[1] + sq_land[1]
    sq = send(sq_send.at[2], sq_land.at[2], sq_sem, 2, y_peer)
    last = grains - 1
    gather(1, last).wait()
    gather(3, last).start()
    gather(2, last).wait()
    gather(4, last).start()
    sq.wait()
    sq_send[3] = sq_send[2] + sq_land[2]
    sq_z = [
        send(sq_send.at[3], sq_land.at[3 + z], sq_sem, 2 + hop, z_peer(hop)) for hop in range(1, nz)
    ]
    for copy in vec_z + sq_z:
        copy.wait()
    vec_land[3 + z] = vec_send[3]
    sq_land[3 + z] = sq_send[3]
    vec_total, sq_total = vec_land[3], sq_land[3]
    for other in range(1, nz):
        vec_total = vec_total + vec_land[3 + other]
        sq_total = sq_total + sq_land[3 + other]
    vec_sum_ref[...] = vec_total
    grad_norm = jnp.sqrt(
        jnp.sum(sq_total, keepdims=True) + jnp.sum(vec_total * vec_total, keepdims=True)
    )
    norm_ref[...] = grad_norm
    done = []
    for piece in range(grains):
        gather(3, piece).wait()
        gather(4, piece).wait()
        for place in range(8):
            at = (piece * 8 + place) * GRAIN
            done.append(
                pltpu.make_async_copy(
                    assembled.at[piece, place // 4, place // 2 % 2, place % 2],
                    own_ref.at[pl.ds(at, GRAIN)],
                    out_sem.at[piece, place],
                )
            )
            done[-1].start()
    for swap in swaps:
        swap.end()
    for copy in done:
        copy.wait()


def tail(nz, owners, g_qkv, back, grad_vector, d_tokens):
    low, f32 = jnp.bfloat16, jnp.float32
    passages, span, _ = d_tokens.shape
    swapped = jax.ShapeDtypeStruct((4 * passages, span // 4, D), low)
    late = g_qkv.shape[0]
    granules = late + back.shape[0]
    grains = granules // (2 * nz)
    any_spec = pl.BlockSpec(memory_space=pl.ANY)
    vmem = pl.BlockSpec(memory_space=pltpu.VMEM)
    dma = pltpu.SemaphoreType.DMA
    block = lambda *lead: pltpu.VMEM((*lead, GRAIN, D), low)
    lanes = (VEC_LEN // 128, 128)
    return pl.pallas_call(
        functools.partial(tail_kernel, nz),
        out_shape=(
            jax.ShapeDtypeStruct((grains * 8 * GRAIN, D), low),
            jax.ShapeDtypeStruct(lanes, f32),
            jax.ShapeDtypeStruct((1, 1), f32),
            swapped,
        ),
        in_specs=[pl.BlockSpec(memory_space=pltpu.SMEM)]
        + [any_spec] * 2
        + [vmem, any_spec],
        out_specs=(any_spec, vmem, vmem, any_spec),
        scratch_shapes=[
            block(late, 2, 2),
            block(late, 2),
            block(late),
            dma((2, len(plane_chunks(QKV_COUNTS)))),
            dma((2, len(plane_chunks(QKV_COUNTS)))),
            dma(()),
            block(granules),
            block(2 * nz, grains),
            block(nz, grains, 2),
            block(nz, grains, 2),
            block(nz, grains, 2),
            block(nz, grains, 2),
            block(2, grains),
            block(grains, 2, 2, 2),
            pltpu.VMEM((4, *lanes), f32),
            pltpu.VMEM((3 + nz, *lanes), f32),
            pltpu.VMEM((4, 8, 128), f32),
            pltpu.VMEM((3 + nz, 8, 128), f32),
            dma(()),
            dma((2, nz * grains)),
            dma((2, nz * grains)),
            dma((2, 5 * grains)),
            dma((2, 2 + nz)),
            dma((2, 2 + nz)),
            dma((grains, 8)),
        ]
        + PositionSwap.scratch(passages, span),
        compiler_params=pltpu.CompilerParams(
            collective_id=1, has_side_effects=True, vmem_limit_bytes=60 * 1024 * 1024
        ),
        cost_estimate=pl.CostEstimate(flops=10**7, bytes_accessed=3 * 10**7, transcendentals=0),
        name="grad_tail",
    )(owners, g_qkv, back, grad_vector, d_tokens)


def keep_lanes(rows, half):
    lane = lax.broadcasted_iota(jnp.int32, rows.shape, 1)
    keep = lane < HEAD_DIM if half == 0 else lane >= HEAD_DIM
    return jnp.where(keep, rows, jnp.zeros_like(rows))


def norm_rows(mixed):
    row_mean = jnp.mean(mixed, axis=-1, keepdims=True)
    centred = mixed - row_mean
    inv_std = lax.rsqrt(jnp.mean(centred * centred, axis=-1, keepdims=True) + 1e-12)
    return centred * inv_std, inv_std


def project(x, w_ref, vec_ref, q_out, k_out, v_out, v_turned):
    f32, low = jnp.float32, jnp.bfloat16

    def product(lo):
        return jnp.dot(x, w_ref[lo : lo + D], preferred_element_type=f32)

    q_out[...] = ((product(0) + vec_ref[0:1]).astype(low).astype(f32) * 0.125).astype(low)
    k_out[...] = product(D).astype(low)
    values = product(2 * D) + vec_ref[1:2]
    v_out[...] = values.astype(low)
    v_turned[...] = values.T.astype(low)


def attend_pair(pair, length, q_ref, k_ref, v_turned, lse_ref, ctx_ref, ctx_turned, scores, weights):
    f32, low = jnp.float32, jnp.bfloat16
    span = q_ref.shape[0]
    width, strip = span // 2, 64
    lanes = pl.ds(pl.multiple_of(pair * 128, 128), 128)
    keys = k_ref[:, lanes]
    head_keys = [keep_lanes(keys, half) for half in range(2)]
    units = [(half, part) for half in range(2) for part in range(2)]

    def score(unit):
        half, part = units[unit]
        scores[unit % 2] = contract_cols(head_keys[half], q_ref[part * width : (part + 1) * width, lanes])

    def masked(unit, at):
        row = at + lax.broadcasted_iota(jnp.int32, (strip, width), 0)
        return jnp.where(row < length, scores[unit % 2, at : at + strip], -1000000000.0)

    def fold(value, op):
        return op(value.reshape(strip // 8, 8, width), axis=0)

    score(0)
    for unit, (half, part) in enumerate(units):
        if unit + 1 < len(units):
            score(unit + 1)
        cols = pl.ds(part * width, width)
        tops = fold(masked(unit, 0), jnp.max)
        for at in range(strip, span, strip):
            tops = jnp.maximum(tops, fold(masked(unit, at), jnp.max))
        peak = jnp.max(tops, axis=0, keepdims=True)
        sums = jnp.zeros((8, width), f32)
        for at in range(0, span, strip):
            weight = jnp.exp(masked(unit, at) - peak)
            sums = sums + fold(weight, jnp.sum)
            weights[unit % 2, at : at + strip] = weight.astype(low)
        total = jnp.sum(sums, axis=0, keepdims=True)
        lse_ref[2 * pair + half, :, cols] = peak + jnp.log(total)
        turned = v_turned[pl.ds(pl.multiple_of(pair * 128 + half * 64, 64), 64), :]
        out = jnp.dot(turned, weights[unit % 2], preferred_element_type=f32)
        ctx_turned[half * 64 : half * 64 + 64, cols] = out / total
    ctx_ref[:, lanes] = ctx_turned[...].T.astype(low)


def first_norm(x, ctx, w_ref, vec_ref, normed_ref, inv_ref):
    attn_out = jnp.dot(ctx, w_ref[3 * D : 4 * D], preferred_element_type=jnp.float32)
    normed, inv_std = norm_rows(x.astype(jnp.float32) + (attn_out + vec_ref[2:3]))
    normed_ref[...] = normed
    inv_ref[...] = jnp.broadcast_to(inv_std, inv_ref.shape)


def attend_kernel(
    lengths_ref,
    x_ref,
    w_ref,
    vec_ref,
    q_ref,
    k_ref,
    v_ref,
    lse_ref,
    ctx_ref,
    normed_ref,
    inv_ref,
    v_turned,
    ctx_turned,
    scores,
    weights,
):
    length = lengths_ref[lax.axis_index("blk") * pl.num_programs(0) + pl.program_id(0)]
    x = x_ref[0]
    project(x, w_ref, vec_ref, q_ref.at[0], k_ref.at[0], v_ref.at[0], v_turned)

    @pl.loop(0, HEADS // 2)
    def _(pair):
        attend_pair(
            pair,
            length,
            q_ref.at[0],
            k_ref.at[0],
            v_turned,
            lse_ref.at[0],
            ctx_ref.at[0],
            ctx_turned,
            scores,
            weights,
        )

    first_norm(x, ctx_ref[0], w_ref, vec_ref, normed_ref.at[0], inv_ref.at[0])


def attend(lengths, tokens, table, vec_rows):
    f32, low = jnp.float32, jnp.bfloat16
    passages, span, _ = tokens.shape
    rows = pl.BlockSpec((1, span, D), lambda p: (p, 0, 0))
    shape = lambda kind: jax.ShapeDtypeStruct((passages, span, D), kind)
    return pl.pallas_call(
        attend_kernel,
        grid=(passages,),
        out_shape=(
            shape(low),
            shape(low),
            shape(low),
            jax.ShapeDtypeStruct((passages, HEADS, 1, span), f32),
            shape(low),
            shape(f32),
            jax.ShapeDtypeStruct((passages, span, 128), f32),
        ),
        in_specs=[
            pl.BlockSpec(memory_space=pltpu.SMEM),
            rows,
            pl.BlockSpec((4 * D, D), lambda p: (0, 0)),
            pl.BlockSpec((VEC_LEN // D, D), lambda p: (0, 0)),
        ],
        out_specs=(
            rows,
            rows,
            rows,
            pl.BlockSpec((1, HEADS, 1, span), lambda p: (p, 0, 0, 0)),
            rows,
            rows,
            pl.BlockSpec((1, span, 128), lambda p: (p, 0, 0)),
        ),
        scratch_shapes=[
            pltpu.VMEM((D, span), low),
            pltpu.VMEM((128, span), f32),
            pltpu.VMEM((2, span, span // 2), f32),
            pltpu.VMEM((2, span, span // 2), low),
        ],
        compiler_params=pltpu.CompilerParams(vmem_limit_bytes=56 * 1024 * 1024),
        cost_estimate=pl.CostEstimate(
            flops=passages * span * (8 * D * D + 4 * D * span),
            bytes_accessed=passages * span * D * 20,
            transcendentals=passages * HEADS * span * span,
        ),
        name="attend",
    )(lengths, tokens, table, vec_rows)


def plane_chunks(counts):
    chunks, base = [], 0
    for source, count in enumerate(counts):
        half = count // 2
        step = half if half % 2 else 2
        for first in range(0, half, step):
            chunks.append((source, first, step, base + first, True))
            chunks.append((source, half + first, step, base + half + first, False))
        base += count
    return chunks


def plane_order(granules):
    half = granules // 2

    def order(turn):
        pair = turn // 2
        return lax.rem(pair, 2) * half + (pair // 2) * 2 + lax.rem(turn, 2)

    return order


def place_of():
    dp, blk = lax.axis_index("dp"), lax.axis_index("blk")
    z, c, y, x = dp // 2, dp % 2, blk // 2, blk % 2
    sibling = (blk, 2 * z + 1 - c)
    x_peer = (2 * y + 1 - x, dp)
    y_peer = (2 * (1 - y) + x, dp)
    return dp, blk, z, c, y, x, sibling, x_peer, y_peer


def remote_copy(src, dst, sems, slot, device):
    return pltpu.make_async_remote_copy(
        src_ref=src,
        dst_ref=dst,
        send_sem=sems.at[0, slot],
        recv_sem=sems.at[1, slot],
        device_id=device,
        device_id_type=MESH,
    )


class PlaneSum:
    def __init__(self, sources, counts, acc, core_land, one_land, two_land, part, sems, base=0):
        self.sources, self.acc, self.core_land = sources, acc, core_land
        self.one_land, self.two_land, self.part, self.base = one_land, two_land, part, base
        self.load_sem, self.core_sem, self.one_sem, self.two_sem = sems
        self.chunks = plane_chunks(counts)
        self.place = place_of()

    def load(self, slot):
        source, first, count, at, _ = self.chunks[slot]
        return pltpu.make_async_copy(
            self.sources[source].at[pl.ds(first, count), self.place[3]],
            self.acc.at[pl.ds(at, count)],
            self.load_sem.at[slot],
        )

    def core(self, slot):
        source, first, count, at, _ = self.chunks[slot]
        return remote_copy(
            self.sources[source].at[pl.ds(first, count), 1 - self.place[3]],
            self.core_land.at[pl.ds(at, count)],
            self.core_sem,
            slot,
            self.place[6],
        )

    def one(self, slot):
        _, _, count, at, x_first = self.chunks[slot]
        _, _, _, _, y, x, _, x_peer, y_peer = self.place
        rows = pl.ds(at, count)
        view = self.acc.at[rows, :, 1 - x] if x_first else self.acc.at[rows, 1 - y]
        return remote_copy(
            view, self.one_land.at[rows], self.one_sem, slot, x_peer if x_first else y_peer
        )

    def two(self, slot):
        _, _, count, at, x_first = self.chunks[slot]
        _, _, _, _, y, x, _, x_peer, y_peer = self.place
        rows = pl.ds(at, count)
        view = self.acc.at[rows, 1 - y, x] if x_first else self.acc.at[rows, y, 1 - x]
        return remote_copy(
            view, self.two_land.at[rows], self.two_sem, slot, y_peer if x_first else x_peer
        )

    def begin(self, slots):
        for slot in slots:
            self.load(slot).start()
            self.core(slot).start()

    def paired(self, slots, go_on=True):
        for slot in slots:
            self.load(slot).wait()
            self.core(slot).wait()
            _, _, count, at, _ = self.chunks[slot]

            @pl.loop(at, at + count)
            def _(g):
                self.acc[g] = add_low(self.acc[g], self.core_land[g])

            if go_on:
                self.one(slot).start()

    def crossed(self, slots):
        _, _, _, _, y, x, _, _, _ = self.place
        for slot in slots:
            self.one(slot).wait()
            _, _, count, at, x_first = self.chunks[slot]

            @pl.loop(at, at + count)
            def _(g):
                for side in range(2):
                    if x_first:
                        self.acc[g, side, x] = add_low(self.acc[g, side, x], self.one_land[g, side])
                    else:
                        self.acc[g, y, side] = add_low(self.acc[g, y, side], self.one_land[g, side])

            self.two(slot).start()

    def half_settled(self, slots, red_ref, red_sem):
        _, _, _, _, y, x, _, _, _ = self.place
        for slot in slots:
            self.one(slot).wait()
            _, _, count, at, x_first = self.chunks[slot]

            @pl.loop(at, at + count)
            def _(g):
                for side in range(2):
                    if x_first:
                        self.acc[g, side, x] = add_low(self.acc[g, side, x], self.one_land[g, side])
                    else:
                        self.acc[g, y, side] = add_low(self.acc[g, y, side], self.one_land[g, side])

            self.kept(slot, red_ref, red_sem).start()

    def kept(self, slot, red_ref, red_sem):
        _, _, count, at, x_first = self.chunks[slot]
        _, _, _, _, y, x, _, _, _ = self.place
        rows = pl.ds(at, count)
        view = self.acc.at[rows, :, x] if x_first else self.acc.at[rows, y]
        return pltpu.make_async_copy(view, red_ref.at[rows], red_sem.at[slot])

    def settled(self, slots):
        _, _, _, _, y, x, _, _, _ = self.place
        for slot in slots:
            self.two(slot).wait()
            _, _, count, at, _ = self.chunks[slot]

            @pl.loop(at, at + count)
            def _(g):
                self.part[self.base + g] = add_low(self.acc[g, y, x], self.two_land[g])

    @staticmethod
    def scratch(counts, with_part=True):
        low, dma = jnp.bfloat16, pltpu.SemaphoreType.DMA
        total, slots = sum(counts), len(plane_chunks(counts))
        shapes = [
            pltpu.VMEM((total, 2, 2, GRAIN, D), low),
            pltpu.VMEM((total, 2, 2, GRAIN, D), low),
            pltpu.VMEM((total, 2, GRAIN, D), low),
            pltpu.VMEM((total, GRAIN, D), low),
            dma((slots,)),
            dma((2, slots)),
            dma((2, slots)),
            dma((2, slots)),
        ]
        return shapes + ([pltpu.VMEM((total, GRAIN, D), low)] if with_part else [])


class SecondStep:
    def __init__(self, red_ref, counts, keep, land, part, load_sem, two_sem, base):
        _, _, _, _, y, x, _, x_peer, y_peer = place_of()
        self.keep, self.land, self.part, self.base = keep, land, part, base
        self.chunks = plane_chunks(counts)
        self.loads, self.sends = [], []
        for slot, (_, _, count, at, x_first) in enumerate(self.chunks):
            rows = pl.ds(at, count)
            near, far, peer = (y, 1 - y, y_peer) if x_first else (x, 1 - x, x_peer)
            self.loads.append(
                pltpu.make_async_copy(red_ref.at[rows, near], keep.at[rows], load_sem.at[slot])
            )
            self.sends.append(
                remote_copy(red_ref.at[rows, far], land.at[rows], two_sem, slot, peer)
            )

    def begin(self):
        for copy in self.loads + self.sends:
            copy.start()

    def end(self):
        for slot, (_, _, count, at, _) in enumerate(self.chunks):
            self.loads[slot].wait()
            self.sends[slot].wait()

            @pl.loop(at, at + count)
            def _(g):
                self.part[self.base + g] = add_low(self.keep[g], self.land[g])

    @staticmethod
    def scratch(counts):
        low, dma = jnp.bfloat16, pltpu.SemaphoreType.DMA
        total, slots = sum(counts), len(plane_chunks(counts))
        block = pltpu.VMEM((total, GRAIN, D), low)
        return [block, block, dma((slots,)), dma((2, slots))]


def run_when(condition, task):
    @pl.when(condition)
    def _():
        task()


def greet(partners):
    barrier = pltpu.get_barrier_semaphore()
    for partner in partners:
        pl.semaphore_signal(barrier, inc=1, device_id=partner, device_id_type=MESH)
    return barrier


class PositionSwap:
    def __init__(self, rows_in, rows_out, keep, keep_sem, swap_sem):
        dp, blk, _, _, _, _, _, x_peer, y_peer = place_of()
        passages, span = rows_in.shape[0], rows_out.shape[1]
        self.diagonal = (3 - blk, dp)
        at = pl.ds(blk * passages, passages)
        self.first = pltpu.make_async_copy(
            rows_in.at[:, pl.ds(blk * span, span)], keep, keep_sem.at[0]
        )
        self.second = pltpu.make_async_copy(keep, rows_out.at[at], keep_sem.at[1])
        self.pushes = [
            remote_copy(
                rows_in.at[:, pl.ds(peer[0] * span, span)], rows_out.at[at], swap_sem, slot, peer
            )
            for slot, peer in enumerate((x_peer, y_peer, self.diagonal))
        ]

    def begin(self):
        for copy in [self.first] + self.pushes:
            copy.start()

    def passed(self):
        self.first.wait()
        self.second.start()

    def end(self):
        for copy in [self.second] + self.pushes:
            copy.wait()

    @staticmethod
    def scratch(passages, span):
        dma = pltpu.SemaphoreType.DMA
        return [pltpu.VMEM((passages, span // 4, D), jnp.bfloat16), dma((2,)), dma((2, 3))]


def attend_back_kernel(
    lengths_ref,
    x_ref,
    w_ref,
    q_ref,
    k_ref,
    v_ref,
    lse_ref,
    d_ctx_ref,
    d_mixed_ref,
    vec_in_ref,
    *refs,
):
    f32, low = jnp.float32, jnp.bfloat16
    beside = len(refs) > 13
    tasks = {}
    if beside:
        *sources, outer_red, refs = *refs[:3], refs[3:]
        red_ref, refs = refs[3], refs[:3] + refs[4:]
        extra, refs = refs[13:], refs[:13]
        acc, core_land, one_land, two_land, *sems, keep, land, keep_sem, keep_two, share, red_sem = extra[:14]
        late, late_acc, late_land, late_load, late_core, late_sem = extra[14:]
    grad_ref, table_ref, vec_ref, k_turned, dq_turned, dq_all, dk_all, dv_all, x_all = refs[:9]
    scores, d_probs, probs_low, d_scores = refs[9:]
    passage = pl.program_id(0)
    if beside:
        summed = PlaneSum(sources, BACK_COUNTS, acc, core_land, one_land, two_land, share, sems)
        second = SecondStep(
            outer_red, OUTER_COUNTS, keep, land, share, keep_sem, keep_two, sum(BACK_COUNTS)
        )
        slots = range(len(summed.chunks))
        late_sems = (late_load, late_core, None, None)
        late_sum = PlaneSum((late,), QKV_COUNTS, late_acc, late_land, None, None, None, late_sems)
        late_slots = range(len(late_sum.chunks))

        @pl.when(passage == 0)
        def _():
            greet(summed.place[6:])

        def begin():
            pl.semaphore_wait(pltpu.get_barrier_semaphore(), 3)
            summed.begin(slots)
            second.begin()

        tasks = {
            0: begin,
            3: lambda: summed.paired(slots),
            5: second.end,
            9: lambda: summed.crossed(slots),
        }

        def end():
            summed.settled(slots)
            stored = [pltpu.make_async_copy(share, red_ref, red_sem)]
            stored[0].start()
            late_sum.paired(late_slots, go_on=False)
            stored.append(pltpu.make_async_copy(late_acc, table_ref, late_sem))
            stored[1].start()
            for copy in stored:
                copy.wait()

    span = x_ref.shape[1]
    half_span, strip = span // 2, 64
    length = lengths_ref[lax.axis_index("blk") * pl.num_programs(0) + passage]
    rows = pl.ds(pl.multiple_of(passage * span, span), span)
    x_all[rows, :] = x_ref[0]
    k_turned[...] = k_ref[0].astype(f32).T.astype(low)
    @pl.loop(0, HEADS // 2)
    def _(pair):
        slot = passage * (HEADS // 2) + pair
        for at in sorted(tasks):
            run_when(slot == at, tasks[at])
        lanes = pl.ds(pl.multiple_of(pair * 128, 128), 128)
        keys, values = k_ref[0, :, lanes], v_ref[0, :, lanes]
        dk, dv = jnp.zeros((span, 128), f32), jnp.zeros((span, 128), f32)
        units = [(half, part) for half in range(2) for part in range(2)]

        def products(unit):
            half, part = units[unit]
            cols = pl.ds(part * half_span, half_span)
            scores[unit % 2] = contract_cols(keep_lanes(keys, half), q_ref[0, cols, lanes])
            d_probs[unit % 2] = contract_cols(keep_lanes(values, half), d_ctx_ref[0, cols, lanes])

        def fold(value):
            return jnp.sum(value.reshape(strip // 8, 8, half_span), axis=0)

        products(0)
        for unit, (half, part) in enumerate(units):
            if unit + 1 < len(units):
                products(unit + 1)
            cols = pl.ds(part * half_span, half_span)
            side = unit % 2
            log_total = lse_ref[0, 2 * pair + half, :, cols]
            sums = jnp.zeros((8, half_span), f32)
            for at in range(0, span, strip):
                here = slice(at, at + strip)
                row = at + lax.broadcasted_iota(jnp.int32, (strip, half_span), 0)
                masked = jnp.where(row < length, scores[side, here], -1000000000.0)
                probs = jnp.exp(masked - log_total)
                weighted = probs * d_probs[side, here]
                probs_low[side, here] = probs.astype(low)
                scores[side, here] = probs
                d_probs[side, here] = weighted
                sums = sums + fold(weighted)
            inner = jnp.sum(sums, axis=0, keepdims=True)
            for at in range(0, span, strip):
                here = slice(at, at + strip)
                d_scores[side, here] = (d_probs[side, here] - scores[side, here] * inner).astype(low)
            d_out = keep_lanes(d_ctx_ref[0, cols, lanes], half)
            dv = dv + jnp.dot(probs_low[side], d_out, preferred_element_type=f32)
            queries = keep_lanes(q_ref[0, cols, lanes], half)
            dk = dk + jnp.dot(d_scores[side], queries, preferred_element_type=f32)
            turned = k_turned[pl.ds(pl.multiple_of(pair * 128 + half * 64, 64), 64), :]
            dq_turned[half * 64 : half * 64 + 64, cols] = (
                jnp.dot(turned, d_scores[side], preferred_element_type=f32) * 0.125
            )
        dq_all[rows, lanes] = dq_turned[...].T.astype(low)
        dk_all[rows, lanes] = dk.astype(low)
        dv_all[rows, lanes] = dv.astype(low)

    @pl.when(passage == pl.num_programs(0) - 1)
    def _():
        for at, part in enumerate((dq_all, dk_all, dv_all)):
            d_weight = contract_rows(x_all[...], part[...]).astype(low)
            if beside:
                late[2 * at : 2 * at + 2] = d_weight.reshape(2, 2, 2, 2, GRAIN, D)
                if at >= 1:
                    late_sum.begin([at - 1])
            else:
                table_ref[at * D : (at + 1) * D] = d_weight

    grad = d_mixed_ref[0]
    for lo, part in ((0, dq_all), (D, dk_all), (2 * D, dv_all)):
        grad = grad + contract_cols(part[rows, :], w_ref[lo : lo + D])
    grad_ref[0] = grad.astype(low)

    @pl.when(passage == pl.num_programs(0) - 1)
    def _():
        vec_ref[...] = vec_in_ref[...]
        vec_ref[0:1] = jnp.sum(dq_all[...].astype(f32), axis=0, keepdims=True)
        vec_ref[1:2] = jnp.sum(dv_all[...].astype(f32), axis=0, keepdims=True)
        if beside:
            end()


def attend_back(
    lengths, tokens, table, queries, keys, values, lse, d_ctx, d_mixed, vec_grad, sources=()
):
    f32, low = jnp.float32, jnp.bfloat16
    passages, span, _ = tokens.shape
    rows = pl.BlockSpec((1, span, D), lambda p: (p, 0, 0))
    whole = pltpu.VMEM((passages * span, D), low)
    any_spec = pl.BlockSpec(memory_space=pl.ANY)
    red_shape, beside, extra, more = (), [], {}, ()
    table_shape = jax.ShapeDtypeStruct((3 * D, D), low)
    table_spec = pl.BlockSpec((3 * D, D), lambda p: (0, 0))
    if sources:
        total = sum(BACK_COUNTS) + sum(OUTER_COUNTS)
        red_shape = (jax.ShapeDtypeStruct((total, GRAIN, D), low),)
        beside = PlaneSum.scratch(BACK_COUNTS, with_part=False) + SecondStep.scratch(OUTER_COUNTS)
        dma = pltpu.SemaphoreType.DMA
        beside += [pltpu.VMEM((total, GRAIN, D), low), dma]
        late, chunks = sum(QKV_COUNTS), len(plane_chunks(QKV_COUNTS))
        table_shape = jax.ShapeDtypeStruct((late, 2, 2, GRAIN, D), low)
        table_spec = any_spec
        beside += [
            pltpu.VMEM((late, 2, 2, 2, GRAIN, D), low),
            pltpu.VMEM((late, 2, 2, GRAIN, D), low),
            pltpu.VMEM((late, 2, 2, GRAIN, D), low),
            dma((chunks,)),
            dma((2, chunks)),
            dma,
        ]
        extra = dict(collective_id=3, has_side_effects=True)
        more = sources
    return pl.pallas_call(
        attend_back_kernel,
        grid=(passages,),
        out_shape=(
            jax.ShapeDtypeStruct((passages, span, D), low),
            table_shape,
            jax.ShapeDtypeStruct((VEC_LEN // D, D), f32),
        )
        + red_shape,
        in_specs=[
            pl.BlockSpec(memory_space=pltpu.SMEM),
            rows,
            pl.BlockSpec((3 * D, D), lambda p: (0, 0)),
            rows,
            rows,
            rows,
            pl.BlockSpec((1, HEADS, 1, span), lambda p: (p, 0, 0, 0)),
            rows,
            rows,
            pl.BlockSpec((VEC_LEN // D, D), lambda p: (0, 0)),
        ]
        + [any_spec] * len(more),
        out_specs=(
            rows,
            table_spec,
            pl.BlockSpec((VEC_LEN // D, D), lambda p: (0, 0)),
        )
        + (any_spec,) * len(red_shape),
        scratch_shapes=[pltpu.VMEM((D, span), low), pltpu.VMEM((128, span), f32)]
        + [whole] * 4
        + [pltpu.VMEM((2, span, span // 2), kind) for kind in (f32, f32, low, low)]
        + beside,
        compiler_params=pltpu.CompilerParams(vmem_limit_bytes=60 * 1024 * 1024, **extra),
        cost_estimate=pl.CostEstimate(
            flops=passages * span * (12 * D * D + 10 * D * span),
            bytes_accessed=passages * span * D * 24,
            transcendentals=passages * HEADS * span * span,
        ),
        name="attend_back",
    )(lengths, tokens, table, queries, keys, values, lse, d_ctx, d_mixed, vec_grad, *more)


ERFC_SLOPE = 0.42
ERFC_TERMS = (
    0.23681282137224371,
    0.23975548803522717,
    0.19369618325685073,
    0.27205881038432234,
    -0.136659548208163,
    0.44720921707821076,
    -0.32398587364624676,
    0.07111276080879629,
)


def gelu_pair(x):
    slope = 1.0 + (ERFC_SLOPE * math.sqrt(0.5)) * jnp.abs(x)
    t = pltpu.reciprocal(slope, approx=True)
    t = t * (2.0 - slope * t)
    bell = jnp.exp2(x * x * (-0.5 / math.log(2.0)))
    series = 0.5 * ERFC_TERMS[-1]
    for term in ERFC_TERMS[-2::-1]:
        series = series * t + 0.5 * term
    low_side = series * t * bell
    cdf = jnp.where(x < 0.0, low_side, 1.0 - low_side)
    return x * cdf, cdf + x * bell * (1.0 / math.sqrt(2.0 * math.pi))


def ffn_kernel(
    lengths_ref,
    vec_ref,
    normed_ref,
    inv_ref,
    cot_ref,
    ctx_ref,
    table_ref,
    output_ref,
    d_mixed_ref,
    d_ctx_ref,
    vec_grad_ref,
    d_out_ref,
    d_inner_ref,
    d_outer_ref,
    *refs,
):
    beside = len(refs) > 20
    if beside:
        red_ref, refs = refs[0], refs[1:]
    (
        w_out,
        w_inner,
        w_outer,
        normed,
        inv_std,
        cot,
        left_pre,
        right_pre,
        slope,
        active,
        hidden,
        output,
        d_branch,
        d_mixed,
        staged,
        staged_outer,
        load_sem,
        store_sem,
        done_sem,
        wide_sem,
        *extra,
    ) = refs
    f32, low = jnp.float32, jnp.bfloat16
    count = normed.shape[0]
    chunk = left_pre.shape[1]
    chunks = FF // chunk
    tile, strip = 512, 32
    tiles = count // tile
    sources = (
        (normed_ref, normed),
        (table_ref.at[pl.ds(4 * D + FF, FF)], w_outer),
        (cot_ref, cot),
        (inv_ref, inv_std),
        (table_ref.at[pl.ds(3 * D, D)], w_out),
        (ctx_ref, hidden),
    )
    loads = [
        pltpu.make_async_copy(src, dst, load_sem.at[slot])
        for slot, (src, dst) in enumerate(sources)
    ]
    loads[0].start()

    def columns(part):
        return pl.ds(pl.multiple_of(part * chunk, chunk), chunk)

    def load_wide(part):
        rows = pl.ds(4 * D + part * chunk, chunk)
        return pltpu.make_async_copy(
            table_ref.at[rows], w_inner.at[columns(part)], wide_sem.at[part]
        )

    for part in range(chunks):
        load_wide(part).start()
    for load in loads[1:5]:
        load.start()

    if beside:
        acc, core_land, one_land, two_land, *sems, red_sem, swap_sem = extra
        summed = PlaneSum((d_outer_ref,), OUTER_COUNTS, acc, core_land, one_land, None, None, sems)
        dp, blk = summed.place[:2]
        diagonal = (3 - blk, dp)
        greet((*summed.place[6:], diagonal))

    def vec(row):
        return vec_ref[row : row + 1]

    vec_grad_ref[...] = jnp.zeros_like(vec_grad_ref)
    loads[0].wait()

    @pl.loop(0, count // strip)
    def _(at):
        rows = pl.ds(pl.multiple_of(at * strip, strip), strip)
        hidden[rows, :] = (normed[rows, :] * vec(8) + vec(9)).astype(low)

    def widen(part, pre):
        load_wide(part).wait()
        pre[...] = contract_cols(hidden[...], w_inner[columns(part), :])

    per_row = D // chunk

    def bend(part, pre):
        bias = vec_ref[pl.ds(3 + part // per_row, 1), :]
        side = lax.rem(part, per_row)
        piece = bias[:, 0:chunk]
        for other in range(1, per_row):
            piece = jnp.where(side == other, bias[:, other * chunk : (other + 1) * chunk], piece)
        for at in range(0, count, strip):
            value, pull = gelu_pair(pre[at : at + strip] + piece)
            active[at : at + strip, columns(part)] = value.astype(low)
            slope[at : at + strip, columns(part)] = pull

    widen(0, left_pre)

    @pl.loop(0, chunks // 2 - 1)
    def _(turn):
        widen(2 * turn + 1, right_pre)
        bend(2 * turn, left_pre)
        widen(2 * turn + 2, left_pre)
        bend(2 * turn + 1, right_pre)

    widen(chunks - 1, right_pre)
    bend(chunks - 2, left_pre)
    bend(chunks - 1, right_pre)

    for load in loads[1:4]:
        load.wait()
    passages = lengths_ref.shape[0] // lax.axis_size("blk")
    per_passage = count // passages

    def put_tile(at, value):
        rows = slice(at % 2 * tile, (at % 2 + 1) * tile)
        left_pre[rows] = value[:, 0:chunk]
        right_pre[rows] = value[:, chunk:]

    def get_strip(at, inner_at):
        first = at % 2 * tile + inner_at
        rows = slice(first, first + strip)
        return jnp.concatenate([left_pre[rows], right_pre[rows]], axis=1)

    def narrow(at):
        return jnp.dot(active[at * tile : (at + 1) * tile], w_outer[...], preferred_element_type=f32)

    def sums(totals, values):
        return [
            total + jnp.sum(value, axis=0, keepdims=True) for total, value in zip(totals, values)
        ]

    nothing = [jnp.zeros((1, D), f32)] * 3
    totals = nothing
    for at in range(tiles):
        put_tile(at, narrow(at))
        passage = at * tile // per_passage
        length = lengths_ref[lax.axis_index("blk") * passages + passage]
        for inner_at in range(0, tile, strip):
            first = at * tile + inner_at
            rows = slice(first, first + strip)
            mixed = normed[rows] * vec(8) + vec(9) + (
                get_strip(at, inner_at) + vec(7)
            )
            normed_two, inv_two = norm_rows(mixed)
            local = first - passage * per_passage
            output[passage, local : local + strip] = (normed_two * vec(10) + vec(11)).astype(low)
            position = local + lax.broadcasted_iota(
                jnp.int32, (strip, 1), 0
            )
            grad_out = jnp.where(position < length, cot[rows].astype(f32), 0.0)
            d_mixed_two = norm_back(grad_out * vec(10), normed_two, inv_two)
            d_mixed[rows] = d_mixed_two
            low_branch = d_mixed_two.astype(low)
            d_branch[rows] = low_branch
            totals = sums(totals, (grad_out * normed_two, grad_out, low_branch.astype(f32)))
    for row, total in zip((10, 11, 7), totals):
        vec_grad_ref[row : row + 1] = total
    if beside:
        blk = lax.axis_index("blk")
        pl.semaphore_wait(pltpu.get_barrier_semaphore(), 4)
        span = output_ref.shape[1]
        there = output_ref.at[pl.ds(blk * passages, passages)]
        given = [
            remote_copy(output.at[:, pl.ds(peer[0] * span, span)], there, swap_sem, slot, peer)
            for slot, peer in enumerate((*summed.place[7:], diagonal))
        ]
        own_piece = output.at[:, pl.ds(blk * span, span)]
        given.append(pltpu.make_async_copy(own_piece, there, done_sem.at[0]))
    else:
        given = [pltpu.make_async_copy(output, output_ref, done_sem.at[0])]
    for copy in given:
        copy.start()

    order = plane_order(chunks)

    def store(turn, side):
        part, slot = order(turn), lax.rem(turn, 2)
        if side == 0:
            return pltpu.make_async_copy(
                staged_outer.at[slot], d_outer_ref.at[part], store_sem.at[slot, 0]
            )
        rows = pl.ds(part * chunk, chunk)
        return pltpu.make_async_copy(staged.at[slot], d_inner_ref.at[rows], store_sem.at[slot, 1])

    tasks = {}
    if beside:

        tasks = {
            2: lambda: summed.begin([0]),
            4: lambda: (summed.paired([0]), summed.begin([1])),
            6: lambda: (summed.paired([1]), summed.begin([2])),
        }

    @pl.loop(0, chunks)
    def _(turn):
        part, slot = order(turn), lax.rem(turn, 2)
        cols = columns(part)
        left_pre[...] = contract_cols(d_branch[...], w_outer[cols, :])
        outer_rows = contract_rows(active[:, cols], d_branch[...]).astype(low)
        staged_outer[slot] = outer_rows.reshape(staged_outer.shape[1:])
        total = jnp.zeros((1, chunk), f32)
        for at in range(0, count, strip):
            d_pre = (left_pre[at : at + strip] * slope[at : at + strip, cols]).astype(low)
            active[at : at + strip, cols] = d_pre
            total = total + jnp.sum(d_pre.astype(f32), axis=0, keepdims=True)
        bias_row = pl.ds(3 + part // per_row, 1)
        side_at = lax.rem(part, per_row)
        for other in range(per_row):
            lanes = slice(other * chunk, (other + 1) * chunk)
            vec_grad_ref[bias_row, lanes] += jnp.where(side_at == other, total, 0.0)
        staged[slot] = contract_rows(active[:, cols], hidden[...]).astype(low)
        for side in range(2):
            store(turn, side).start()

        @pl.when(turn >= 1)
        def _():
            for side in range(2):
                store(turn - 1, side).wait()

        for at in sorted(tasks):
            run_when(turn == at, tasks[at])

    for side in range(2):
        store(chunks - 1, side).wait()
    if beside:
        summed.begin([3])
        summed.paired([2])
    loads[5].start()
    loads[4].wait()
    ctx, d_attn, d_ctx = hidden, d_branch, cot
    totals = nothing
    for at in range(tiles):
        span = slice(at * tile, (at + 1) * tile)
        put_tile(at, jnp.dot(active[span], w_inner[...], preferred_element_type=f32))
        for inner_at in range(0, tile, strip):
            first = at * tile + inner_at
            rows = slice(first, first + strip)
            d_hidden = d_mixed[rows] + get_strip(at, inner_at)
            normed_one = normed[rows]
            d_mixed_one = norm_back(d_hidden * vec(8), normed_one, inv_std[rows, 0:1])
            d_mixed[rows] = d_mixed_one
            low_attn = d_mixed_one.astype(low)
            d_attn[rows] = low_attn
            totals = sums(totals, (d_hidden * normed_one, d_hidden, low_attn.astype(f32)))
        d_ctx[span] = contract_cols(d_attn[span], w_out[...]).astype(low)
        if beside and at == 0:
            summed.paired([3])
        if beside and at == tiles - 1:
            summed.half_settled([0, 1], red_ref, red_sem)
    for row, total in zip((8, 9, 2), totals):
        vec_grad_ref[row : row + 1] = total
    results = [
        pltpu.make_async_copy(d_ctx, d_ctx_ref, done_sem.at[1]),
        pltpu.make_async_copy(d_mixed, d_mixed_ref, done_sem.at[2]),
    ]
    for copy in results:
        copy.start()
    half = staged.shape[1]
    loads[5].wait()
    for side in range(2):
        rows = slice(side * half, (side + 1) * half)
        staged[side] = contract_rows(ctx[:, rows], d_attn[...]).astype(low)
        copy = pltpu.make_async_copy(staged.at[side], d_out_ref.at[rows], done_sem.at[3 + side])
        copy.start()
        results.append(copy)
    if beside:
        summed.half_settled([2, 3], red_ref, red_sem)
        results += [summed.kept(slot, red_ref, red_sem) for slot in range(4)]
    for copy in given + results:
        copy.wait()


def ffn(lengths, normed, inv_std, cotangent, context, vec_rows, table, passages, beside):
    f32, low = jnp.float32, jnp.bfloat16
    count = normed.shape[0]
    shares = (4 * passages, count // passages // 4) if beside else (passages, count // passages)
    chunk = 8 * GRAIN
    any_spec = pl.BlockSpec(memory_space=pl.ANY)
    vmem = pl.BlockSpec(memory_space=pltpu.VMEM)
    dma = pltpu.SemaphoreType.DMA
    whole = lambda width, kind=low: pltpu.VMEM((count, width), kind)
    granules = FF // chunk
    more_shape, more, extra = (), [], {}
    if beside:
        more_shape = (jax.ShapeDtypeStruct((granules, 2, GRAIN, D), low),)
        more = PlaneSum.scratch(OUTER_COUNTS, with_part=False)
        more[3] = pltpu.VMEM((1, GRAIN, D), low)
        more += [dma((4,)), dma((2, 3))]
        extra = dict(collective_id=4, has_side_effects=True)
    return pl.pallas_call(
        ffn_kernel,
        out_shape=(
            jax.ShapeDtypeStruct((*shares, D), low),
            jax.ShapeDtypeStruct((count, D), f32),
            jax.ShapeDtypeStruct((count, D), low),
            jax.ShapeDtypeStruct((VEC_LEN // D, D), f32),
            jax.ShapeDtypeStruct((D, D), low),
            jax.ShapeDtypeStruct((FF, D), low),
            jax.ShapeDtypeStruct((granules, 2, 2, 2, GRAIN, D), low),
        )
        + more_shape,
        in_specs=[pl.BlockSpec(memory_space=pltpu.SMEM), vmem] + [any_spec] * 5,
        out_specs=(any_spec, any_spec, any_spec, vmem)
        + (any_spec,) * (3 + len(more_shape)),
        scratch_shapes=[
            pltpu.VMEM((D, D), low),
            pltpu.VMEM((FF, D), low),
            pltpu.VMEM((FF, D), low),
            whole(D, f32),
            whole(128, f32),
            whole(D),
            whole(chunk, f32),
            whole(chunk, f32),
            whole(FF, f32),
            whole(FF),
            whole(D),
            pltpu.VMEM((passages, count // passages, D), low),
            whole(D),
            whole(D, f32),
            pltpu.VMEM((2, chunk, D), low),
            pltpu.VMEM((2, 2, 2, 2, GRAIN, D), low),
            dma((6,)),
            dma((2, 2)),
            dma((5,)),
            dma((granules,)),
        ]
        + more,
        compiler_params=pltpu.CompilerParams(vmem_limit_bytes=63 * 1024 * 1024, **extra),
        cost_estimate=pl.CostEstimate(
            flops=count * (12 * D * FF + 4 * D * D),
            bytes_accessed=2 * (14 * D * D + 14 * D * count),
            transcendentals=count * FF,
        ),
        name="ffn",
    )(lengths, vec_rows, normed, inv_std, cotangent, context, table)


def paired(own_rows, dp_count, blk_count):
    return blk_count == 4 and dp_count % 2 == 0 and own_rows % 384 == 0


def swap_in(rows):
    return lax.all_to_all(rows, "blk", split_axis=0, concat_axis=1, tiled=True)


def swap_out(rows):
    return lax.all_to_all(rows, "blk", split_axis=1, concat_axis=0, tiled=True)


def pick_blocks(blocks, order):
    return jnp.concatenate(
        [lax.dynamic_index_in_dim(blocks, order[i], 0) for i in range(blocks.shape[0])], axis=0
    )


def body(
    tokens,
    cotangent,
    lengths,
    owners,
    master,
    moment_one,
    moment_two,
    vectors,
    vector_one,
    vector_two,
):
    dp_count = lax.axis_size("dp")
    blk_count = lax.axis_size("blk")
    blk = lax.axis_index("blk")
    own_rows = master.shape[0]
    grain = math.gcd(own_rows, D)
    part = grain // blk_count
    own_grains = own_rows // grain
    fast = paired(own_rows, dp_count, blk_count)
    if fast:
        full = own_rows * 2 // 9
        tokens, cotangent, table, *attended, vec_rows = enter(
            dp_count // 2, full, owners, tokens, cotangent, master, lengths, vectors
        )
    else:
        own_part = lax.dynamic_index_in_dim(
            master.reshape(own_grains, blk_count, part, D), blk, 1, keepdims=False
        ).astype(jnp.bfloat16)
        part_blocks = lax.all_gather(own_part, "dp", axis=0)
        part_table = pick_blocks(part_blocks, jnp.argsort(owners)).reshape(dp_count * own_grains, part, D)
        tokens = swap_in(tokens)
        cotangent = swap_in(cotangent)

        rows = lax.all_gather(part_table, "blk", axis=1)
        table = rows.reshape(-1, D)
        vec_rows = vectors.reshape(-1, D)
        attended = attend(lengths, tokens, table, vec_rows)
    queries, keys, values, log_total, context, normed_one, inv_one = attended
    passages, span_len, _ = tokens.shape
    tok_rows = passages * span_len
    flat = lambda rows: rows.reshape(tok_rows, -1)
    output, d_mixed_one, d_context, grad_vector, d_w_out, d_w_inner, d_w_outer, *outer_red = ffn(
        lengths,
        flat(normed_one),
        flat(inv_one),
        flat(cotangent),
        flat(context),
        vec_rows,
        table,
        passages,
        fast,
    )
    split = lambda g: g.reshape(-1, 2, 2, 2, GRAIN, D)
    d_tokens, d_w_qkv, grad_vector, *back = attend_back(
        lengths,
        tokens,
        table,
        queries,
        keys,
        values,
        log_total,
        d_context.reshape(passages, span_len, D),
        d_mixed_one.reshape(passages, span_len, D),
        grad_vector,
        [split(d_w_out), split(d_w_inner), *outer_red] if fast else (),
    )

    def own_parts(rows):
        split = rows.astype(jnp.bfloat16).reshape(-1, blk_count, part, D)
        return lax.psum_scatter(split, "blk", scatter_dimension=1)

    if fast:
        own_block, vector_sum, norms, grad_tokens = tail(
            dp_count // 2, owners, d_w_qkv, back[0], grad_vector, d_tokens
        )
        grad_norm = norms[0, 0]
        vector_sum = vector_sum.reshape(-1)
    else:
        output, grad_tokens = swap_out(output), swap_out(d_tokens)
        part_grads = jnp.concatenate(
            [own_parts(d_w_qkv), own_parts(d_w_out), own_parts(d_w_inner), own_parts(d_w_outer.reshape(FF, D))],
            axis=0,
        )
        ordered = pick_blocks(part_grads.reshape(dp_count, own_grains, part, D), owners)
        own_grad = lax.psum_scatter(ordered, "dp", scatter_dimension=0)
        own_f32 = own_grad.astype(jnp.float32)
        own_block = lax.all_gather(own_grad, "blk", axis=1).reshape(own_rows, D)
        vector_sum = lax.psum(grad_vector, ("dp", "blk"))
        squares = lax.psum(jnp.sum(own_f32 * own_f32), ("dp", "blk"))
        vector_sum = vector_sum.reshape(-1)
        grad_norm = jnp.sqrt(squares + jnp.sum(vector_sum * vector_sum))
    factor = jnp.minimum(1.0, clip_norm / (grad_norm + 1e-06))
    own_grad = own_block.astype(jnp.float32) * factor
    new_vectors, new_vone, new_vtwo = adamw(
        vectors, vector_one, vector_two, vector_sum * factor, 0.0, vector_rate
    )
    new_master, new_one, new_two = adamw(
        master, moment_one, moment_two, own_grad, weight_decay, learn_rate
    )
    return (
        output,
        grad_tokens,
        grad_norm,
        new_master,
        new_one,
        new_two,
        new_vectors,
        new_vone,
        new_vtwo,
    )


def solution(mesh):
    in_specs = (
        P("dp", "blk", None),
        P("dp", "blk", None),
        P("dp"),
        P(),
        P("dp", None),
        P("dp", None),
        P("dp", None),
        P(),
        P(),
        P(),
    )
    out_specs = (
        P("dp", "blk", None),
        P("dp", "blk", None),
        P(),
        P("dp", None),
        P("dp", None),
        P("dp", None),
        P(),
        P(),
        P(),
    )
    return jax.shard_map(body, mesh=mesh, in_specs=in_specs, out_specs=out_specs, check_vma=False)
```
